256 devices in a mesh: brick: 32 (over x, z_lo, core), sub: 8 (over z_hi, y).
Axes of the slice: x: 4, y: 4, z: 8 (z_hi: 2, z_lo: 4; z = z_hi * 4 + z_lo), core: 2. Of those that a mesh axis runs over, the one named last changes fastest.
Arguments:
- populations: float32 [19, 128, 128, 128], P(None, 'brick', 'sub'), may hold values from -0.75 to 0.75
- solid: int32 [128, 128, 128], P('brick', 'sub'), may hold values 0 or 1
- boundary_pressure: float32 [8192], P(('brick', 'sub')), may hold values from -4 to 4
- block_col: int32 [8192], P(('brick', 'sub')), may hold values from 0 to 63, as said below
- block_dest: int32 [8192, 1], P(('brick', 'sub')), may hold values from 0 to 31; in each aligned block of 32 rows (0 to 31, 32 to 63, ...) at most 3 rows name the same one
- block_seg: int32 [8192], P(('brick', 'sub')), may hold values from 0 to 2047
- seg_pressure: float32 [524288], P(('brick', 'sub')), may hold values from -6 to 6
- seg_rate: float32 [524288], P(('brick', 'sub')), may hold values from 0.05 to 0.25
- seg_leak: float32 [524288], P(('brick', 'sub')), may hold values from 0.1 to 1
- profile_weights: float32 [524288, 128], P(('brick', 'sub')), may hold values from -12 to 12
- junc_members: int32 [4, 262144], P(None, ('brick', 'sub')), may hold values from 0 to 16383
- junc_arity: int32 [262144], P(('brick', 'sub')), may hold values from 2 to 4
- junc_res: float32 [4, 262144], P(None, ('brick', 'sub')), may hold values from 1 to 2
- junc_cross: float32 [4, 4, 262144], P(None, None, ('brick', 'sub')), may hold values from -0.3 to 0.3
Outputs:
- populations_out: float32 [19, 128, 128, 128], P(None, 'brick', 'sub')
- seg_pressure_out: float32 [524288], P(('brick', 'sub'))
- boundary_pressure_out: float32 [8192], P(('brick', 'sub'))
The draws below stay inside these ranges and needn't reach their ends.
Inputs may be any that keep to these rules, and one draw needn't show every extreme that they name: `block_col`: within one device's 32 blocks the columns are distinct. `block_dest`: in one device's 32 blocks no brick index is named more than 3 times, and some device names one brick index exactly 3 times; every brick index is named somewhere. `junc_members`: A member numbered m lies on the device of the junction's brick index with sub index m // 2048, at local index m % 2048.
All inputs are finite; a program needn't handle non-finite values. No bound on the sum of `solid` on one device may be relied on, other than what follows from the above.
Results may differ from the reference program's by a relative error of at most 0.00011.
Values sent between devices are 32-bit elements; how exact they have to be, the bound alone decides.
A program may use at most 64 MiB of HBM per device.

```python
import math
import jax
import jax.numpy as jnp
import numpy as np
from jax import lax

DIRS = 19
CX = 4
CY = 16
CZ = 128
STEPS = 6
BLK_DEV = 32
SLOTS = 3
SEG_DEV = 2048
KMAX = 4
JUNC_DEV = 1024
NX = 128
NY = 128
NZ = 128
BLOCKS = 8192
SEGS = 524288
GROUP = 16384
JUNCS = 262144
N_BRICK = 32
N_SUB = 8


def draw_block_col(key, part):
    key = jax.random.fold_in(key, 11)
    device_count = BLOCKS // BLK_DEV
    keys = jax.random.split(key, device_count)
    columns = jax.vmap(lambda single: jax.random.permutation(single, CX * CY)[:BLK_DEV])(keys)
    return columns.reshape(-1).astype(jnp.int32)


def touch_ends(drawn, own_key, low, top_value):
    index_at = [jax.random.randint(jax.random.fold_in(own_key, axis), (), 0, length) for axis, length in enumerate(drawn.shape)]
    widest = drawn.shape.index(max(drawn.shape))
    next_to = index_at[:widest] + [(index_at[widest] + 1) % drawn.shape[widest]] + index_at[widest + 1:]
    return drawn.at[tuple(index_at)].set(low).at[tuple(next_to)].set(top_value)


def block_levels(rng, dims, pieces, smallest, high):
    gain = 1.0
    for axis_at, shards_of in pieces:
        draws = jax.random.uniform(jax.random.fold_in(jax.random.fold_in(rng, 6), axis_at), (shards_of,), jnp.float32, smallest / len(pieces), high / len(pieces))
        gain = gain * jnp.repeat(jnp.exp(draws), dims[axis_at] // shards_of).reshape((-1,) + (1,) * (len(dims) - 1 - axis_at))
    return gain


def assign_block(rng, own, number, rows, amount, top, most, slope):
    sequence = jax.random.permutation(rng, amount)
    packed, usual = load_shares(amount, rows * top, most, slope, True), load_shares(amount, rows * top, most, slope, False)
    places = jnp.arange(amount)

    def named(sizes, rotation):
        used = int((sizes > 0).sum())
        fixed = max(1, used // 4)
        passed = fixed + (places - fixed + rotation * (used - fixed)) % max(1, amount - fixed)
        return jnp.zeros((amount,), jnp.int32).at[sequence[jnp.where(places < fixed, places, passed)]].set(jnp.asarray(sizes, jnp.int32))

    sizes = jnp.where(number % 4 == 0, named(packed, number // 4), named(usual, number - number // 4 - 1))
    mixed = jax.random.permutation(jax.random.fold_in(own, 3), amount)
    donor, taker = mixed[0:amount // 2 * 2:2], mixed[1:amount // 2 * 2:2]
    margin = jnp.minimum(sizes[donor] - 1, most - sizes[taker]) // 2
    margin = jnp.where((donor == sequence[0]) | (taker == sequence[0]) | (sizes[taker] == 0), 0, jnp.maximum(margin, 0))
    passed = jax.random.randint(jax.random.fold_in(own, 4), (amount // 2,), 0, 1 << 20) % (margin + 1)
    sizes = sizes.at[donor].add(-passed).at[taker].add(passed)
    labels = jnp.searchsorted(jnp.cumsum(sizes), jnp.arange(rows * top), side="right").astype(jnp.int32)
    listing = labels.reshape(top, rows).T
    listing = listing[jax.random.permutation(jax.random.fold_in(own, 1), rows)]
    rotation = jax.random.randint(jax.random.fold_in(own, 2), (rows, 1), 0, top)
    return jnp.take_along_axis(listing, (jnp.arange(top)[None, :] + rotation) % top, axis=1)


def load_shares(amount, total, limit, skew, full):
    loads = [(1 << 20) // math.isqrt(rank ** skew) + 1 for rank in range(1, amount + 1)]
    largest = limit if full else min(limit, max(-(-total // amount), total * loads[0] // sum(loads)))
    least = 1 if total - largest >= amount - 1 else 0
    counts, spare = [largest] + [least] * (amount - 1), total - largest - least * (amount - 1)
    while spare > 0:
        free = [i for i in range(1, amount) if counts[i] < largest] or [i for i in range(1, amount) if counts[i] < limit]
        mass, left = sum([loads[i] for i in free]), spare
        for i in free:
            extra = min(limit - counts[i], max(1, left * loads[i] // mass), spare)
            counts[i] = counts[i] + extra
            spare = spare - extra
    return np.array(counts)


def gaussian(stream_key, extent, deviation, bound, cuts=(), kind=jnp.bfloat16):
    drawn = deviation * jax.random.normal(stream_key, extent, jnp.float32)
    if cuts:
        drawn = drawn * block_levels(stream_key, extent, cuts, -0.22, 0.18)
    return jnp.clip(drawn, -bound, bound).astype(kind)


def setup_inputs(seed: int = 0) -> dict:
    key_list = jax.random.split(jax.random.key(seed), 15)
    populations = gaussian(key_list[0], (DIRS, NX, NY, NZ), 0.25, 0.75, ((1, 32), (2, 8)), jnp.float32)
    solid = touch_ends((jax.random.randint(key_list[1], (NX, NY, NZ), 0, 8) < 1).astype(jnp.int32), jax.random.fold_in(key_list[1], 1), 0, 1)
    boundary_pressure = gaussian(key_list[2], (BLOCKS,), 1.0, 4.0, ((0, 256),), jnp.float32)
    block_col = draw_block_col(jax.random.fold_in(key_list[14], 71), 0)
    block_dest_keys = jax.random.split(jax.random.fold_in(key_list[4], 1), BLOCKS // BLK_DEV)
    block_dest_turns = jax.random.permutation(jax.random.fold_in(key_list[4], 3), BLOCKS // BLK_DEV)
    block_dest = jax.vmap(lambda own, number: assign_block(jax.random.fold_in(key_list[4], 2), own, number, BLK_DEV, N_BRICK, 1, SLOTS, 2))(block_dest_keys, block_dest_turns).reshape((BLOCKS, 1))
    block_seg = touch_ends(jax.random.randint(key_list[5], (BLOCKS,), 0, SEG_DEV), jax.random.fold_in(key_list[5], 1), 0, SEG_DEV - 1).astype(jnp.int32)
    seg_pressure = gaussian(key_list[6], (SEGS,), 1.0, 6.0, ((0, 256),), jnp.float32)
    seg_rate = jnp.clip(jnp.exp(math.log(0.25) - 1.609438 * jax.random.uniform(key_list[7], (SEGS,), jnp.float32) ** block_levels(key_list[7], (SEGS,), ((0, 256),), -0.2, 0.2)), 0.05, 0.25)
    seg_leak = jnp.clip(jnp.exp(math.log(1.0) - 2.3025851 * jax.random.uniform(key_list[8], (SEGS,), jnp.float32) ** block_levels(key_list[8], (SEGS,), ((0, 256),), -0.2, 0.2)), 0.1, 1.0)
    profile_weights = gaussian(key_list[9], (SEGS, CZ), 2.0, 12.0, ((0, 256),), jnp.float32)
    junc_members = touch_ends(jax.random.randint(key_list[10], (KMAX, JUNCS), 0, GROUP), jax.random.fold_in(key_list[10], 1), 0, GROUP - 1).astype(jnp.int32)
    junc_arity = touch_ends(jax.random.randint(key_list[11], (JUNCS,), 2, KMAX + 1), jax.random.fold_in(key_list[11], 1), 2, KMAX).astype(jnp.int32)
    junc_res = jnp.clip(jnp.exp(math.log(2.0) - 0.6931472 * jax.random.uniform(key_list[12], (KMAX, JUNCS), jnp.float32) ** block_levels(key_list[12], (KMAX, JUNCS), ((1, 256),), -0.2, 0.2)), 1.0, 2.0)
    junc_cross = jnp.clip(jax.random.uniform(key_list[13], (KMAX, KMAX, JUNCS), jnp.float32, -0.3, 0.3) * block_levels(key_list[13], (KMAX, KMAX, JUNCS), ((2, 256),), -0.4, 0.0), -0.3, 0.3)
    return {"populations": populations, "solid": solid, "boundary_pressure": boundary_pressure, "block_col": block_col, "block_dest": block_dest, "block_seg": block_seg, "seg_pressure": seg_pressure, "seg_rate": seg_rate, "seg_leak": seg_leak, "profile_weights": profile_weights, "junc_members": junc_members, "junc_arity": junc_arity, "junc_res": junc_res, "junc_cross": junc_cross}


VELOCITIES = np.array([[0, 0, 0], [1, 0, 0], [-1, 0, 0], [0, 1, 0], [0, -1, 0], [0, 0, 1], [0, 0, -1], [1, 1, 0], [-1, -1, 0], [1, -1, 0], [-1, 1, 0], [1, 0, 1], [-1, 0, -1], [1, 0, -1], [-1, 0, 1], [0, 1, 1], [0, -1, -1], [0, 1, -1], [0, -1, 1]])
OPPOSITE = np.array([0, 2, 1, 4, 3, 6, 5, 8, 7, 10, 9, 12, 11, 14, 13, 16, 15, 18, 17])
LATTICE_WEIGHTS = np.array([1.0 / 3.0] + [1.0 / 18.0] * 6 + [1.0 / 36.0] * 12)
RELAXATION = 1.25
DENSITY_SCALE = 0.1


def lattice_tables():
    weights = jnp.asarray(LATTICE_WEIGHTS, jnp.float32)
    moment_rows = jnp.asarray(VELOCITIES.T * LATTICE_WEIGHTS[None, :], jnp.float32)
    directions = jnp.asarray(VELOCITIES, jnp.float32)
    return weights, moment_rows, directions


def collide(lattice, solid, boundary_mask, boundary_density):
    weights, moment_rows, directions = lattice_tables()
    highest = lax.Precision.HIGHEST
    density = 1.0 + jnp.einsum("i,ixyz->xyz", weights, lattice, precision=highest)
    momentum = jnp.einsum("ai,ixyz->axyz", moment_rows, lattice, precision=highest)
    velocity = momentum / density[None]
    projected = jnp.einsum("ia,axyz->ixyz", directions, velocity, precision=highest)
    speed_sq = jnp.sum(velocity * velocity, axis=0)
    shape_terms = 1.0 + 3.0 * projected + 4.5 * projected * projected - 1.5 * speed_sq[None]
    relaxed = lattice - RELAXATION * (lattice - (density[None] * shape_terms - 1.0))
    bounced = lattice[OPPOSITE]
    collided = jnp.where(solid[None] > 0, bounced, relaxed)
    imposed = boundary_density[None, :, :, None] * shape_terms - 1.0
    return jnp.where(boundary_mask[None, :, :, None], imposed, collided)


def axial_momentum(lattice):
    flow_rows = jnp.asarray(VELOCITIES[:, 0] * LATTICE_WEIGHTS, jnp.float32)
    return jnp.einsum("i,ixyz->xyz", flow_rows, lattice, precision=lax.Precision.HIGHEST)


def solve_blocks(matrix, right):
    matrix_order = matrix.shape[0]
    rows = [matrix[row_index] for row_index in range(matrix_order)]
    sides = [right[row_index] for row_index in range(matrix_order)]
    for column in range(matrix_order):
        for row_index in range(column + 1, matrix_order):
            factor = rows[row_index][column] / rows[column][column]
            rows[row_index] = rows[row_index] - factor[None] * rows[column]
            sides[row_index] = sides[row_index] - factor[None] * sides[column]
    answer = [None] * matrix_order
    for row_index in reversed(range(matrix_order)):
        running = sides[row_index]
        for column in range(row_index + 1, matrix_order):
            running = running - rows[row_index][column][None] * answer[column]
        answer[row_index] = running / rows[row_index][row_index][None]
    return jnp.stack(answer)


def junction_matrix(resist, cross, live):
    members_max = resist.shape[0]
    identity = jnp.eye(members_max, dtype=jnp.float32)[:, :, None]
    symmetric = 0.5 * (cross + jnp.transpose(cross, (1, 0, 2)))
    coupled = live[:, None, :] * live[None, :, :] * symmetric
    return identity * resist[:, None, :] + (1.0 - identity) * coupled


def junction_flows(matrix, live, member_pressure):
    driven = live * member_pressure
    solved = solve_blocks(matrix, jnp.stack([driven, live], axis=1))
    first = solved[:, 0]
    second = solved[:, 1]
    junction_pressure = jnp.sum(live * first, axis=0) / jnp.sum(live * second, axis=0)
    return live * (first - junction_pressure[None] * second)


def reference(populations, solid, boundary_pressure, block_col, block_dest, block_seg, seg_pressure, seg_rate, seg_leak, profile_weights, junc_members, junc_arity, junc_res, junc_cross):
    block_device = (jnp.arange(BLOCKS) // BLK_DEV).astype(jnp.int32)
    block_brick = block_device // N_SUB
    block_sub = block_device % N_SUB
    column_x = block_brick * CX + block_col // CY
    column_y = block_sub * CY + block_col % CY
    axial = axial_momentum(populations)
    profiles = axial[column_x, column_y]
    coupled = (block_dest[:, 0] * N_SUB + block_sub) * SEG_DEV + block_seg
    flux = jnp.sum(profile_weights[coupled] * profiles, axis=1)
    inflow = jax.ops.segment_sum(flux, coupled, num_segments=SEGS)

    junction_brick = (jnp.arange(JUNCS) // JUNC_DEV).astype(jnp.int32) // N_SUB
    global_members = junction_brick[None, :] * GROUP + junc_members
    live = (jnp.arange(KMAX)[:, None] < junc_arity[None, :]).astype(jnp.float32)
    matrix = junction_matrix(junc_res, junc_cross, live)
    pressure = seg_pressure
    for step_index in range(STEPS):
        flows = junction_flows(matrix, live, pressure[global_members])
        balance = jax.ops.segment_sum(-flows.reshape(-1), global_members.reshape(-1), num_segments=SEGS)
        pressure = pressure + seg_rate * (balance + inflow - seg_leak * pressure)
    new_pressure = pressure[coupled]

    boundary_mask = jnp.zeros((NX, NY), bool).at[column_x, column_y].set(True)
    boundary_density = jnp.ones((NX, NY), jnp.float32).at[column_x, column_y].set(1.0 + DENSITY_SCALE * boundary_pressure)
    lattice = populations
    for step_index in range(STEPS):
        collided = collide(lattice, solid, boundary_mask, boundary_density)
        lattice = jnp.stack([jnp.roll(collided[component], (int(VELOCITIES[component, 0]), int(VELOCITIES[component, 1]), int(VELOCITIES[component, 2])), axis=(0, 1, 2)) for component in range(19)])
    return lattice, pressure, new_pressure
```

```python
import functools

import jax
import jax.numpy as jnp
import numpy as np
from jax import lax
from jax.experimental import pallas as pl
from jax.experimental.pallas import tpu as pltpu
from jax.sharding import PartitionSpec as P

STEPS = 6
SLOTS = 3
MESH = pl.DeviceIdType.MESH
F32 = jnp.float32
BF16 = jnp.bfloat16
HIGHEST = lax.Precision.HIGHEST

VELOCITIES = [
    (0, 0, 0),
    (1, 0, 0),
    (-1, 0, 0),
    (0, 1, 0),
    (0, -1, 0),
    (0, 0, 1),
    (0, 0, -1),
    (1, 1, 0),
    (-1, -1, 0),
    (1, -1, 0),
    (-1, 1, 0),
    (1, 0, 1),
    (-1, 0, -1),
    (1, 0, -1),
    (-1, 0, 1),
    (0, 1, 1),
    (0, -1, -1),
    (0, 1, -1),
    (0, -1, 1),
]
OPPOSITE = [0, 2, 1, 4, 3, 6, 5, 8, 7, 10, 9, 12, 11, 14, 13, 16, 15, 18, 17]
RELAXATION = 1.25
DENSITY_SCALE = 0.1
X_UP = [i for i, c in enumerate(VELOCITIES) if c[0] == 1]
X_DOWN = [i for i, c in enumerate(VELOCITIES) if c[0] == -1]
Y_UP = [i for i, c in enumerate(VELOCITIES) if c[1] == 1]
Y_DOWN = [i for i, c in enumerate(VELOCITIES) if c[1] == -1]
CORNERS = [(7, 1, 1), (8, -1, -1), (9, 1, -1), (10, -1, 1)]


def iota(shape, axis):
    return lax.broadcasted_iota(jnp.int32, shape, axis)


def collide_sites(h, solid, mask, imposed):
    w0, w1, w2 = 1.0 / 3.0, 1.0 / 18.0, 1.0 / 36.0
    plus = {i: h[i] + h[i + 1] for i in range(1, 19, 2)}
    minus = {i: h[i] - h[i + 1] for i in range(1, 19, 2)}
    near = plus[1] + plus[3] + plus[5]
    far = (plus[7] + plus[9]) + (plus[11] + plus[13]) + (plus[15] + plus[17])
    density = 1.0 + (w0 * h[0] + w1 * near + w2 * far)
    inverse = 1.0 / density
    ux = (w1 * minus[1] + w2 * ((minus[7] + minus[9]) + (minus[11] + minus[13]))) * inverse
    uy = (w1 * minus[3] + w2 * ((minus[7] - minus[9]) + (minus[15] + minus[17]))) * inverse
    uz = (w1 * minus[5] + w2 * ((minus[11] - minus[13]) + (minus[15] - minus[17]))) * inverse
    base = 1.0 - 1.5 * (ux * ux + uy * uy + uz * uz)
    along = {1: ux, 3: uy, 5: uz, 7: ux + uy, 9: ux - uy, 11: ux + uz, 13: ux - uz, 15: uy + uz, 17: uy - uz}
    scale = jnp.where(mask, imposed, RELAXATION * density)
    shift = jnp.where(mask, -1.0, -RELAXATION)
    keep = jnp.where(mask, 0.0, 1.0 - RELAXATION)
    bounce = jnp.logical_and(solid, jnp.logical_not(mask))
    post = [None] * 19
    post[0] = jnp.where(bounce, h[0], scale * base + (shift + keep * h[0]))
    for i in range(1, 19, 2):
        c = along[i]
        even = base + 4.5 * (c * c)
        odd = 3.0 * c
        post[i] = jnp.where(bounce, h[i + 1], scale * (even + odd) + (shift + keep * h[i]))
        post[i + 1] = jnp.where(bounce, h[i], scale * (even - odd) + (shift + keep * h[i + 1]))
    return post


def off_diagonals(live, res, cross):
    rows = [[None] * 4 for _ in range(4)]
    sides = [[None] * 4 for _ in range(4)]
    zero = jnp.zeros_like(live[0])
    for k in range(4):
        for l in range(4):
            if k == l:
                rows[k][l] = res[k]
                sides[k][l] = live[k]
            else:
                rows[k][l] = live[k] * live[l] * (0.5 * (cross[k][l] + cross[l][k]))
                sides[k][l] = zero
    for c in range(4):
        inverse = 1.0 / rows[c][c]
        for r in range(c + 1, 4):
            factor = rows[r][c] * inverse
            for l in range(c + 1, 4):
                rows[r][l] = rows[r][l] - factor * rows[c][l]
            for l in range(c + 1):
                sides[r][l] = sides[r][l] - factor * sides[c][l]
    answer = [None] * 4
    for r in reversed(range(4)):
        inverse = 1.0 / rows[r][r]
        answer[r] = []
        for l in range(4):
            running = sides[r][l]
            for c in range(r + 1, 4):
                running = running - rows[r][c] * answer[c][l]
            answer[r].append(running * inverse)
    ones = [answer[k][0] + answer[k][1] + answer[k][2] + answer[k][3] for k in range(4)]
    total = 1.0 / (live[0] * ones[0] + live[1] * ones[1] + live[2] * ones[2] + live[3] * ones[3])
    pairs = []
    for a in range(4):
        for b in range(a + 1, 4):
            pairs.append(live[a] * live[b] * (answer[a][b] - ones[a] * ones[b] * total))
    return pairs


def split2(x):
    high = x.astype(BF16)
    return high, (x - high.astype(F32)).astype(BF16)


def kernel(
    nb,
    ns,
    pop_ref,
    solid_ref,
    bp_ref,
    col_ref,
    dest_ref,
    seg_ref,
    segp_ref,
    rate_ref,
    leak_ref,
    w_ref,
    mem_ref,
    arity_ref,
    res_ref,
    cross_ref,
    pop_out,
    seg_out,
    bp_out,
    post,
    mask_ref,
    imposed_ref,
    sxu,
    sxd,
    syu,
    syd,
    sc,
    rxu,
    rxd,
    ryu,
    ryd,
    rc,
    ptab,
    rate2,
    leak2,
    inflow2,
    flow,
    other_mem,
    gbuf,
    row_at,
    oh_c,
    oh_r,
    part,
    rs,
    msg,
    arrived,
    pick,
    ids_ref,
    ret_out,
    ret_in,
    halo_s,
    halo_r,
    first_s,
    first_r,
    pair_s,
    pair_r,
    rs_s,
    rs_r,
    ag_s,
    ag_r,
    msg_s,
    msg_r,
    ret_s,
    ret_r,
):
    ny = ns // 2
    rows = segp_ref.shape[0]
    junctions = mem_ref.shape[1]
    links = 4 * junctions
    blocks = col_ref.shape[1]
    cells_x, cells_y, cells_z = solid_ref.shape
    b, s = lax.axis_index("brick"), lax.axis_index("sub")
    hi, y = s // ny, lax.rem(s, ny)
    other = 1 - hi
    partner = (b, other * ny + y)

    def at(db, ds):
        return (lax.rem(b + db + nb, nb), lax.rem(s + ds + ns, ns))

    def ring(k):
        return (b, hi * ny + lax.rem(y + k, ny))

    def copy(src, dst, send, recv, device):
        return pltpu.make_async_remote_copy(
            src_ref=src, dst_ref=dst, send_sem=send, recv_sem=recv, device_id=device, device_id_type=MESH
        )

    barrier = pltpu.get_barrier_semaphore()

    def greet(k, carry):
        pl.semaphore_signal(barrier, inc=1, device_id=at(k, 0), device_id_type=MESH)
        return carry

    lax.fori_loop(1, nb, greet, 0)
    for k in range(1, ns):
        pl.semaphore_signal(barrier, inc=1, device_id=at(0, k), device_id_type=MESH)
    for _, cx, cy in CORNERS:
        pl.semaphore_signal(barrier, inc=1, device_id=at(cx, cy), device_id_type=MESH)

    dest = dest_ref[...]
    eye = iota((blocks, blocks), 0) == iota((blocks, blocks), 1)
    dest_column = jnp.sum(jnp.where(eye, dest, 0), axis=1, keepdims=True)
    earlier = jnp.logical_and(dest_column == dest, iota((blocks, blocks), 0) < iota((blocks, blocks), 1))
    slot = jnp.sum(jnp.where(earlier, 1, 0), axis=0, keepdims=True)
    r = iota((nb * 8, blocks), 0)
    chosen = jnp.logical_and((r >> 3) == dest, (r & 3) == slot)
    pick[...] = jnp.where(chosen, 1.0, 0.0)
    columns = cells_x * cells_y
    hits = iota((columns, blocks), 0) == col_ref[...]
    selector = lax.dot_general(
        jnp.where(chosen, 1.0, 0.0).astype(BF16),
        jnp.where(hits, 1.0, 0.0).astype(BF16),
        (((1,), (1,)), ((), ())),
        preferred_element_type=F32,
    )
    axial = jnp.zeros((columns, cells_z), F32)
    for i, c in enumerate(VELOCITIES):
        if c[0]:
            weight = c[0] * (1.0 / 18.0 if i < 7 else 1.0 / 36.0)
            axial = axial + weight * pop_ref[i].reshape(columns, cells_z)
    profiles = jnp.dot(selector, axial, precision=HIGHEST, preferred_element_type=F32)
    numbers = jnp.sum(jnp.where(chosen, seg_ref[...] + 1, 0), axis=1, keepdims=True) - 1
    numbers = jnp.broadcast_to(numbers.astype(F32), (nb * 8, cells_z))
    is_label = (iota((nb * 8, cells_z), 0) & 4) != 0
    msg[...] = jnp.where(is_label, numbers, profiles).reshape(nb, 8, cells_z)

    found = jnp.sum(jnp.where(hits, 1.0, 0.0), axis=1, keepdims=True)
    pressed = jnp.sum(jnp.where(hits, bp_ref[...], 0.0), axis=1, keepdims=True)
    mask_ref[...] = jnp.broadcast_to(found, (columns, cells_z)).reshape(cells_x, cells_y, cells_z)
    imposed_ref[...] = jnp.broadcast_to(1.0 + DENSITY_SCALE * pressed, (columns, cells_z)).reshape(
        cells_x, cells_y, cells_z
    )

    live = [jnp.where(arity_ref[...] > k, 1.0, 0.0) for k in range(4)]
    pairs = off_diagonals(
        live,
        [res_ref[k : k + 1, :] for k in range(4)],
        [[cross_ref[k, l : l + 1, :] for l in range(4)] for k in range(4)],
    )
    for n, value in enumerate(pairs):
        gbuf[0, n : n + 1, :] = value
    gbuf[0, 6:8, :] = jnp.zeros((2, junctions), F32)

    ptab[y, hi] = segp_ref[...]
    rate2[hi] = rate_ref[...]
    leak2[hi] = leak_ref[...]

    pl.semaphore_wait(barrier, nb - 1 + ns - 1 + len(CORNERS))

    first = [
        copy(segp_ref, ptab.at[y, hi], first_s.at[k - 1], first_r.at[k - 1], at(0, k)) for k in range(1, ns)
    ]
    for c in first:
        c.start()
    pair = [
        copy(mem_ref, other_mem, pair_s.at[0], pair_r.at[0], partner),
        copy(gbuf.at[0], gbuf.at[1], pair_s.at[1], pair_r.at[1], partner),
        copy(rate_ref, rate2.at[hi], pair_s.at[2], pair_r.at[2], partner),
        copy(leak_ref, leak2.at[hi], pair_s.at[3], pair_r.at[3], partner),
    ]
    for c in pair:
        c.start()
    pair_inflow = copy(flow, inflow2.at[hi], pair_s.at[4], pair_r.at[4], partner)

    def message(k):
        target = lax.rem(b + k, nb)
        return copy(msg.at[target], arrived.at[b], msg_s.at[k - 1], msg_r.at[k - 1], (target, s))

    def answer(k):
        target = lax.rem(b + k, nb)
        return copy(ret_out.at[target], ret_in.at[b], ret_s.at[k - 1], ret_r.at[k - 1], (target, s))

    def start_message(k, carry):
        message(k).start()
        return carry

    lax.fori_loop(1, nb, start_message, 0)
    arrived[b] = msg[b]

    def halo(parity):
        copies = [
            (sxu, rxu, (1, 0)),
            (sxd, rxd, (-1, 0)),
            (syu, ryu, (0, 1)),
            (syd, ryd, (0, -1)),
        ]
        out = [
            copy(src, dst.at[parity], halo_s.at[n], halo_r.at[parity, n], at(*to))
            for n, (src, dst, to) in enumerate(copies)
        ]
        for n, (_, cx, cy) in enumerate(CORNERS):
            out.append(
                copy(sc.at[n], rc.at[parity, n], halo_s.at[4 + n], halo_r.at[parity, 4 + n], at(cx, cy))
            )
        return out

    halves = cells_y // 8

    def collide(source):
        def tile(n, carry):
            x, first_row = n // halves, pl.multiple_of(lax.rem(n, halves) * 8, 8)
            span = pl.ds(first_row, 8)
            h = [source[i, x, span, :] for i in range(19)]
            out = collide_sites(
                h, solid_ref[x, span, :] > 0, mask_ref[x, span, :] > 0.5, imposed_ref[x, span, :]
            )
            for i in range(19):
                post[i, x, span, :] = out[i]
            return carry

        lax.fori_loop(0, cells_x * halves, tile, 0)

    def pack():
        for n, i in enumerate(X_UP):
            sxu[n] = post[i, cells_x - 1]
        for n, i in enumerate(X_DOWN):
            sxd[n] = post[i, 0]
        for n, i in enumerate(Y_UP):
            for x in range(cells_x):
                syu[n, x : x + 1, :] = post[i, x, cells_y - 1 : cells_y, :]
        for n, i in enumerate(Y_DOWN):
            for x in range(cells_x):
                syd[n, x : x + 1, :] = post[i, x, 0:1, :]
        for n, (i, cx, cy) in enumerate(CORNERS):
            x = cells_x - 1 if cx > 0 else 0
            row = cells_y - 1 if cy > 0 else 0
            sc[n] = jnp.broadcast_to(post[i, x, row : row + 1, :], (8, cells_z))

    def stream(parity):
        edge = iota((cells_y, cells_z), 0)
        for i, (cx, cy, cz) in enumerate(VELOCITIES):
            for x in range(cells_x):
                xs = x - cx
                inside = 0 <= xs < cells_x
                if inside:
                    value = post[i, xs]
                elif cx > 0:
                    value = rxu[parity, X_UP.index(i)]
                else:
                    value = rxd[parity, X_DOWN.index(i)]
                if cy:
                    if not inside:
                        n = [c[0] for c in CORNERS].index(i)
                        row = rc[parity, n, 0:1, :]
                    elif cy > 0:
                        row = ryu[parity, Y_UP.index(i), xs : xs + 1, :]
                    else:
                        row = ryd[parity, Y_DOWN.index(i), xs : xs + 1, :]
                    value = pltpu.roll(value, cy % cells_y, 0)
                    value = jnp.where(edge == (0 if cy > 0 else cells_y - 1), row, value)
                if cz:
                    value = pltpu.roll(value, cz % cells_z, 1)
                pop_out[i, x] = value

    collide(pop_ref)
    pack()
    for c in halo(0):
        c.start()

    def build(n, ref):
        m = jnp.concatenate([ref[k : k + 1, :] for k in range(4)], axis=1)
        per = rows * 128
        sub = m // per
        row = (lax.rem(sub, ny) * 2 + sub // ny) * rows + (lax.rem(m, per) >> 7)
        row_at[n] = row
        lines = iota((128, links), 0)
        oh_c[n] = jnp.where(lines == (m & 127), 1.0, 0.0).astype(BF16)
        oh_r[n] = jnp.where(iota((ns * rows, links), 0) == row, 1.0, 0.0).astype(BF16)

    build(0, mem_ref)
    pair[0].wait()
    build(1, other_mem)
    for c in pair[1:]:
        c.wait()
    for c in first:
        c.wait()

    def flows(n, table):
        members = oh_c[n]
        found = jnp.dot(table, jnp.concatenate([members, members], axis=0), preferred_element_type=F32)
        q = jnp.sum(jnp.where(iota((ns * rows, links), 0) == row_at[n], found, 0.0), axis=0, keepdims=True)
        q = [q[:, k * junctions : (k + 1) * junctions] for k in range(4)]
        f = [None] * 4
        count = 0
        for k in range(4):
            for l in range(k + 1, 4):
                term = gbuf[n, count : count + 1, :] * (q[l] - q[k])
                f[k] = term if f[k] is None else f[k] + term
                f[l] = -term if f[l] is None else f[l] - term
                count += 1
        high, low = split2(jnp.concatenate(f, axis=1))
        return lax.dot_general(
            oh_r[n],
            jnp.concatenate([members * high, members * low], axis=0),
            (((1,), (1,)), ((), ())),
            preferred_element_type=F32,
        )

    def inflows():
        def wait_message(k, carry):
            message(k).wait()
            return carry

        lax.fori_loop(1, nb, wait_message, 0)
        got = arrived[...].reshape(nb * 8, cells_z)
        numbers = pltpu.roll(got, nb * 8 - 4, 0)
        at_row = iota((nb * 8, cells_z), 0)
        holds = jnp.logical_and((at_row & 4) == 0, (at_row & 3) < SLOTS)
        numbers = jnp.where(holds, numbers.astype(jnp.int32), -1)
        ids_ref[...] = numbers
        lane = iota((nb * 8, 128), 1)

        def chunk(n, carry):
            weights = w_ref[pl.ds(pl.multiple_of(n * 128, 128), 128), :]
            value = lax.dot_general(
                got, weights, (((1,), (1,)), ((), ())), precision=HIGHEST, preferred_element_type=F32
            )
            value = jnp.where(numbers == lane + n * 128, value, 0.0)
            flow[pl.ds(n, 1), :] = jnp.sum(value, axis=0, keepdims=True)
            return carry

        lax.fori_loop(0, rows, chunk, 0)
        pair_inflow.start()
        inflow2[hi] = flow[...]
        pair_inflow.wait()

    def step(t, carry):
        parity = lax.rem(t, 2)
        table = jnp.concatenate(split2(ptab[...].reshape(ns * rows, 128)), axis=1)
        both = flows(0, table) + flows(1, table)
        part[...] = (both[:, :128] + both[:, 128:]).reshape(ny, 2, rows, 128)
        scatter = [
            copy(part.at[lax.rem(y + k, ny)], rs.at[k - 1], rs_s.at[k - 1], rs_r.at[k - 1], ring(k))
            for k in range(1, ny)
        ]
        for c in scatter:
            c.start()

        now = halo(parity)
        for c in now:
            c.wait_recv()
        stream(parity)
        for c in now:
            c.wait_send()

        @pl.when(t < STEPS - 1)
        def _():
            collide(pop_out)
            pack()
            for c in halo(1 - parity):
                c.start()

        @pl.when(t == 0)
        def _():
            inflows()

        for c in scatter:
            c.wait()
        balance = part[y]
        for k in range(1, ny):
            balance = balance + rs[k - 1]
        p = ptab[y]
        ptab[y] = p + rate2[...] * (inflow2[...] - balance - leak2[...] * p)

        @pl.when(t < STEPS - 1)
        def _():
            gather = [
                copy(ptab.at[y], ptab.at[y], ag_s.at[k - 1], ag_r.at[k - 1], ring(k)) for k in range(1, ny)
            ]
            for c in gather:
                c.start()
            for c in gather:
                c.wait()

        return carry

    lax.fori_loop(0, STEPS, step, 0)
    final = ptab[y, hi]
    seg_out[...] = final

    numbers = ids_ref[...]
    lane = iota((nb * 8, 128), 1)
    value = jnp.zeros((nb * 8, 128), F32)
    for n in range(rows):
        value = value + jnp.where(numbers == lane + n * 128, final[n : n + 1, :], 0.0)
    value = jnp.sum(value, axis=1, keepdims=True)
    ret_out[...] = jnp.broadcast_to(value, (nb * 8, 128)).reshape(nb, 8, 128)

    def start_answer(k, carry):
        answer(k).start()
        return carry

    def wait_answer(k, carry):
        answer(k).wait()
        return carry

    lax.fori_loop(1, nb, start_answer, 0)
    ret_in[b] = ret_out[b]
    lax.fori_loop(1, nb, wait_answer, 0)
    back = ret_in[...].reshape(nb * 8, 128)[:, :blocks]
    is_value = (iota((nb * 8, blocks), 0) & 4) == 0
    bp_out[...] = jnp.sum(
        jnp.where(jnp.logical_and(is_value, pick[...] > 0.5), back, 0.0), axis=0, keepdims=True
    )


def local(
    populations,
    solid,
    boundary_pressure,
    block_col,
    block_dest,
    block_seg,
    seg_pressure,
    seg_rate,
    seg_leak,
    profile_weights,
    junc_members,
    junc_arity,
    junc_res,
    junc_cross,
):
    nb, ns = lax.axis_size("brick"), lax.axis_size("sub")
    ny = ns // 2
    _, cx, cy, cz = populations.shape
    segs, blocks, junctions = seg_pressure.shape[0], block_col.shape[0], junc_arity.shape[0]
    rows, links = segs // 128, 4 * junctions
    vmem, dma = pltpu.VMEM, pltpu.SemaphoreType.DMA
    scratch = [
        vmem((19, cx, cy, cz), F32),
        vmem((cx, cy, cz), F32),
        vmem((cx, cy, cz), F32),
        vmem((5, cy, cz), F32),
        vmem((5, cy, cz), F32),
        vmem((5, cx, cz), F32),
        vmem((5, cx, cz), F32),
        vmem((4, 8, cz), F32),
        vmem((2, 5, cy, cz), F32),
        vmem((2, 5, cy, cz), F32),
        vmem((2, 5, cx, cz), F32),
        vmem((2, 5, cx, cz), F32),
        vmem((2, 4, 8, cz), F32),
        vmem((ny, 2, rows, 128), F32),
        vmem((2, rows, 128), F32),
        vmem((2, rows, 128), F32),
        vmem((2, rows, 128), F32),
        vmem((rows, 128), F32),
        vmem((4, junctions), jnp.int32),
        vmem((2, 8, junctions), F32),
        vmem((2, 1, links), jnp.int32),
        vmem((2, 128, links), BF16),
        vmem((2, ns * rows, links), BF16),
        vmem((ny, 2, rows, 128), F32),
        vmem((ny - 1, 2, rows, 128), F32),
        vmem((nb, 8, cz), F32),
        vmem((nb, 8, cz), F32),
        vmem((nb * 8, blocks), F32),
        vmem((nb * 8, cz), jnp.int32),
        vmem((nb, 8, 128), F32),
        vmem((nb, 8, 128), F32),
        dma((8,)),
        dma((2, 8)),
        dma((ns - 1,)),
        dma((ns - 1,)),
        dma((5,)),
        dma((5,)),
        dma((ny - 1,)),
        dma((ny - 1,)),
        dma((ny - 1,)),
        dma((ny - 1,)),
        dma((nb - 1,)),
        dma((nb - 1,)),
        dma((nb - 1,)),
        dma((nb - 1,)),
    ]
    spec = pl.BlockSpec(memory_space=vmem)
    lattice, pressure, back = pl.pallas_call(
        functools.partial(kernel, nb, ns),
        out_shape=(
            jax.ShapeDtypeStruct(populations.shape, F32),
            jax.ShapeDtypeStruct((rows, 128), F32),
            jax.ShapeDtypeStruct((1, blocks), F32),
        ),
        in_specs=[spec] * 14,
        out_specs=(spec, spec, spec),
        scratch_shapes=scratch,
        compiler_params=pltpu.CompilerParams(
            collective_id=0, has_side_effects=True, vmem_limit_bytes=48 * 2**20
        ),
        name="coupled",
    )(
        populations,
        solid,
        boundary_pressure.reshape(1, blocks),
        block_col.reshape(1, blocks),
        block_dest.reshape(1, blocks),
        block_seg.reshape(1, blocks),
        seg_pressure.reshape(rows, 128),
        seg_rate.reshape(rows, 128),
        seg_leak.reshape(rows, 128),
        profile_weights,
        junc_members,
        junc_arity.reshape(1, junctions),
        junc_res,
        junc_cross,
    )
    return lattice, pressure.reshape(segs), back.reshape(blocks)


def solution(mesh):
    return jax.shard_map(
        local,
        mesh=mesh,
        in_specs=(
            P(None, "brick", "sub", None),
            P("brick", "sub", None),
            P(("brick", "sub")),
            P(("brick", "sub")),
            P(("brick", "sub"), None),
            P(("brick", "sub")),
            P(("brick", "sub")),
            P(("brick", "sub")),
            P(("brick", "sub")),
            P(("brick", "sub"), None),
            P(None, ("brick", "sub")),
            P(("brick", "sub")),
            P(None, ("brick", "sub")),
            P(None, None, ("brick", "sub")),
        ),
        out_specs=(P(None, "brick", "sub", None), P(("brick", "sub")), P(("brick", "sub"))),
        check_vma=False,
    )
```

```python
import functools

import jax
import jax.numpy as jnp
import numpy as np
from jax import lax
from jax.experimental import pallas as pl
from jax.experimental.pallas import tpu as pltpu
from jax.sharding import PartitionSpec as P

STEPS = 6
SLOTS = 3
MESH = pl.DeviceIdType.MESH
F32 = jnp.float32
BF16 = jnp.bfloat16
HIGHEST = lax.Precision.HIGHEST

VELOCITIES = [
    (0, 0, 0),
    (1, 0, 0),
    (-1, 0, 0),
    (0, 1, 0),
    (0, -1, 0),
    (0, 0, 1),
    (0, 0, -1),
    (1, 1, 0),
    (-1, -1, 0),
    (1, -1, 0),
    (-1, 1, 0),
    (1, 0, 1),
    (-1, 0, -1),
    (1, 0, -1),
    (-1, 0, 1),
    (0, 1, 1),
    (0, -1, -1),
    (0, 1, -1),
    (0, -1, 1),
]
OPPOSITE = [0, 2, 1, 4, 3, 6, 5, 8, 7, 10, 9, 12, 11, 14, 13, 16, 15, 18, 17]
RELAXATION = 1.25
DENSITY_SCALE = 0.1
X_UP = [i for i, c in enumerate(VELOCITIES) if c[0] == 1]
X_DOWN = [i for i, c in enumerate(VELOCITIES) if c[0] == -1]
Y_UP = [i for i, c in enumerate(VELOCITIES) if c[1] == 1]
Y_DOWN = [i for i, c in enumerate(VELOCITIES) if c[1] == -1]
CORNERS = [(7, 1, 1), (8, -1, -1), (9, 1, -1), (10, -1, 1)]


def iota(shape, axis):
    return lax.broadcasted_iota(jnp.int32, shape, axis)


def collide_sites(h, solid, mask, imposed):
    w0, w1, w2 = 1.0 / 3.0, 1.0 / 18.0, 1.0 / 36.0
    plus = {i: h[i] + h[i + 1] for i in range(1, 19, 2)}
    minus = {i: h[i] - h[i + 1] for i in range(1, 19, 2)}
    near = plus[1] + plus[3] + plus[5]
    far = (plus[7] + plus[9]) + (plus[11] + plus[13]) + (plus[15] + plus[17])
    density = 1.0 + (w0 * h[0] + w1 * near + w2 * far)
    inverse = 1.0 / density
    ux = (w1 * minus[1] + w2 * ((minus[7] + minus[9]) + (minus[11] + minus[13]))) * inverse
    uy = (w1 * minus[3] + w2 * ((minus[7] - minus[9]) + (minus[15] + minus[17]))) * inverse
    uz = (w1 * minus[5] + w2 * ((minus[11] - minus[13]) + (minus[15] - minus[17]))) * inverse
    base = 1.0 - 1.5 * (ux * ux + uy * uy + uz * uz)
    along = {1: ux, 3: uy, 5: uz, 7: ux + uy, 9: ux - uy, 11: ux + uz, 13: ux - uz, 15: uy + uz, 17: uy - uz}
    scale = jnp.where(mask, imposed, RELAXATION * density)
    shift = jnp.where(mask, -1.0, -RELAXATION)
    keep = jnp.where(mask, 0.0, 1.0 - RELAXATION)
    bounce = jnp.logical_and(solid, jnp.logical_not(mask))
    post = [None] * 19
    post[0] = jnp.where(bounce, h[0], scale * base + (shift + keep * h[0]))
    for i in range(1, 19, 2):
        c = along[i]
        even = base + 4.5 * (c * c)
        odd = 3.0 * c
        post[i] = jnp.where(bounce, h[i + 1], scale * (even + odd) + (shift + keep * h[i]))
        post[i + 1] = jnp.where(bounce, h[i], scale * (even - odd) + (shift + keep * h[i + 1]))
    return post


def off_diagonals(live, res, cross):
    rows = [[None] * 4 for _ in range(4)]
    sides = [[None] * 4 for _ in range(4)]
    zero = jnp.zeros_like(live[0])
    for k in range(4):
        for l in range(4):
            if k == l:
                rows[k][l] = res[k]
                sides[k][l] = live[k]
            else:
                rows[k][l] = live[k] * live[l] * (0.5 * (cross[k][l] + cross[l][k]))
                sides[k][l] = zero
    for c in range(4):
        inverse = 1.0 / rows[c][c]
        for r in range(c + 1, 4):
            factor = rows[r][c] * inverse
            for l in range(c + 1, 4):
                rows[r][l] = rows[r][l] - factor * rows[c][l]
            for l in range(c + 1):
                sides[r][l] = sides[r][l] - factor * sides[c][l]
    answer = [None] * 4
    for r in reversed(range(4)):
        inverse = 1.0 / rows[r][r]
        answer[r] = []
        for l in range(4):
            running = sides[r][l]
            for c in range(r + 1, 4):
                running = running - rows[r][c] * answer[c][l]
            answer[r].append(running * inverse)
    ones = [answer[k][0] + answer[k][1] + answer[k][2] + answer[k][3] for k in range(4)]
    total = 1.0 / (live[0] * ones[0] + live[1] * ones[1] + live[2] * ones[2] + live[3] * ones[3])
    pairs = []
    for a in range(4):
        for b in range(a + 1, 4):
            pairs.append(live[a] * live[b] * (answer[a][b] - ones[a] * ones[b] * total))
    return pairs


def split2(x):
    high = x.astype(BF16)
    return high, (x - high.astype(F32)).astype(BF16)


def split3(x):
    high = x.astype(BF16)
    rest = x - high.astype(F32)
    middle = rest.astype(BF16)
    return high, middle, (rest - middle.astype(F32)).astype(BF16)


def kernel(
    nb,
    ns,
    pop_hbm,
    solid_hbm,
    bp_hbm,
    col_hbm,
    dest_hbm,
    seg_hbm,
    segp_hbm,
    rate_hbm,
    leak_hbm,
    w_hbm,
    mem_hbm,
    arity_hbm,
    res_hbm,
    cross_hbm,
    pop_out,
    seg_out,
    bp_out,
    pop_ref,
    solid_ref,
    bp_ref,
    col_ref,
    dest_ref,
    seg_ref,
    segp_ref,
    w_ref,
    mem_ref,
    arity_ref,
    res_ref,
    cross_ref,
    load_s,
    post,
    mask_ref,
    imposed_ref,
    sxu,
    sxd,
    syu,
    syd,
    sc,
    rxu,
    rxd,
    ryu,
    ryd,
    rc,
    ptab,
    stage,
    rates,
    inflow_all,
    flow,
    other_mem,
    gbuf,
    row_at,
    oh_c,
    oh_r,
    part,
    msg,
    arrived,
    pick,
    ids_ref,
    w_parts,
    ret_out,
    ret_in,
    halo_s,
    halo_r,
    first_s,
    first_r,
    rates_s,
    rates_r,
    inflow_s,
    inflow_r,
    pair_s,
    pair_r,
    part_s,
    part_r,
    msg_s,
    msg_r,
    ret_s,
    ret_r,
):
    ny = ns // 2
    rows = segp_ref.shape[0]
    junctions = mem_ref.shape[1]
    links = 4 * junctions
    blocks = col_ref.shape[1]
    cells_x, cells_y, cells_z = solid_ref.shape
    b, s = lax.axis_index("brick"), lax.axis_index("sub")
    hi, y = s // ny, lax.rem(s, ny)
    other = 1 - hi
    partner = (b, other * ny + y)

    def at(db, ds):
        return (lax.rem(b + db + nb, nb), lax.rem(s + ds + ns, ns))

    def ring(k):
        return (b, hi * ny + lax.rem(y + k, ny))

    def copy(src, dst, send, recv, device):
        return pltpu.make_async_remote_copy(
            src_ref=src, dst_ref=dst, send_sem=send, recv_sem=recv, device_id=device, device_id_type=MESH
        )

    barrier = pltpu.get_barrier_semaphore()

    def greet(k, carry):
        pl.semaphore_signal(barrier, inc=1, device_id=at(k, 0), device_id_type=MESH)
        return carry

    lax.fori_loop(1, nb, greet, 0)
    for k in range(1, ns):
        pl.semaphore_signal(barrier, inc=1, device_id=at(0, k), device_id_type=MESH)
    for _, cx, cy in CORNERS:
        pl.semaphore_signal(barrier, inc=1, device_id=at(cx, cy), device_id_type=MESH)

    loads = [
        pltpu.make_async_copy(src, dst, load_s.at[n])
        for n, (src, dst) in enumerate(
            [
                (pop_hbm, pop_ref),
                (solid_hbm, solid_ref),
                (bp_hbm, bp_ref),
                (col_hbm, col_ref),
                (dest_hbm, dest_ref),
                (seg_hbm, seg_ref),
                (segp_hbm, segp_ref),
                (rate_hbm, stage.at[0]),
                (leak_hbm, stage.at[1]),
                (w_hbm, w_ref),
                (mem_hbm, mem_ref),
                (arity_hbm, arity_ref),
                (res_hbm, res_ref),
                (cross_hbm, cross_ref),
            ]
        )
    ]
    for n in (11, 12, 13, 4, 5, 3, 2, 0, 10, 6, 7, 8, 1, 9):
        loads[n].start()

    for n in (11, 12, 13):
        loads[n].wait()
    live = [jnp.where(arity_ref[...] > k, 1.0, 0.0) for k in range(4)]
    pairs = off_diagonals(
        live,
        [res_ref[k : k + 1, :] for k in range(4)],
        [[cross_ref[k, l : l + 1, :] for l in range(4)] for k in range(4)],
    )
    for n, value in enumerate(pairs):
        gbuf[0, n : n + 1, :] = value
    gbuf[0, 6:8, :] = jnp.zeros((2, junctions), F32)

    for n in (2, 3, 4, 5, 0):
        loads[n].wait()
    dest = dest_ref[...]
    eye = iota((blocks, blocks), 0) == iota((blocks, blocks), 1)
    dest_column = jnp.sum(jnp.where(eye, dest, 0), axis=1, keepdims=True)
    earlier = jnp.logical_and(dest_column == dest, iota((blocks, blocks), 0) < iota((blocks, blocks), 1))
    slot = jnp.sum(jnp.where(earlier, 1, 0), axis=0, keepdims=True)
    slot_column = jnp.sum(jnp.where(eye, slot, 0), axis=1, keepdims=True)
    number_column = jnp.sum(jnp.where(eye, seg_ref[...] + 1, 0), axis=1, keepdims=True)
    r = iota((nb * 4, blocks), 0)
    aimed = (r >> 2) == dest
    chosen = jnp.where(jnp.logical_and(aimed, (r & 3) == slot), 1.0, 0.0)
    pick[...] = chosen
    columns = cells_x * cells_y
    hits = iota((columns, blocks), 0) == col_ref[...]
    selector = lax.dot_general(
        chosen.astype(BF16),
        jnp.where(hits, 1.0, 0.0).astype(BF16),
        (((1,), (1,)), ((), ())),
        preferred_element_type=F32,
    ).astype(BF16)
    axial = jnp.zeros((columns, cells_z), F32)
    for i, c in enumerate(VELOCITIES):
        if c[0]:
            weight = c[0] * (1.0 / 18.0 if i < 7 else 1.0 / 36.0)
            axial = axial + weight * pop_ref[i].reshape(columns, cells_z)
    profiles = jnp.dot(
        jnp.concatenate([selector] * 3, axis=1),
        jnp.concatenate(split3(axial), axis=0),
        preferred_element_type=F32,
    )
    number = jnp.where(iota((blocks, cells_z), 1) == slot_column, number_column, 0)
    numbers = jnp.dot(
        jnp.concatenate([jnp.where(aimed, 1.0, 0.0).astype(BF16)] * 2, axis=1),
        jnp.concatenate([(number >> 6).astype(F32) * 64.0, (number & 63).astype(F32)], axis=0).astype(BF16),
        preferred_element_type=F32,
    )
    is_label = (iota((nb * 4, cells_z), 0) & 3) == 3
    msg[...] = jnp.where(is_label, numbers - 1.0, profiles).reshape(nb, 4, cells_z)

    found = jnp.sum(jnp.where(hits, 1.0, 0.0), axis=1, keepdims=True)
    pressed = jnp.sum(jnp.where(hits, bp_ref[...], 0.0), axis=1, keepdims=True)
    mask_ref[...] = jnp.broadcast_to(found, (columns, cells_z)).reshape(cells_x, cells_y, cells_z)
    imposed_ref[...] = jnp.broadcast_to(1.0 + DENSITY_SCALE * pressed, (columns, cells_z)).reshape(
        cells_x, cells_y, cells_z
    )

    for n in (6, 7, 8, 10):
        loads[n].wait()
    ptab[s] = segp_ref[...]
    rates[s] = stage[...]

    pl.semaphore_wait(barrier, nb - 1 + ns - 1 + len(CORNERS))

    pair = [
        copy(mem_ref, other_mem, pair_s.at[0], pair_r.at[0], partner),
        copy(gbuf.at[0], gbuf.at[1], pair_s.at[1], pair_r.at[1], partner),
    ]
    for c in pair:
        c.start()
    first = [
        copy(segp_ref, ptab.at[s], first_s.at[k - 1], first_r.at[k - 1], at(0, k)) for k in range(1, ns)
    ]
    for c in first:
        c.start()

    def message(k):
        target = lax.rem(b + k, nb)
        return copy(msg.at[target], arrived.at[b], msg_s.at[k - 1], msg_r.at[k - 1], (target, s))

    def answer(k):
        target = lax.rem(b + k, nb)
        return copy(ret_out.at[target], ret_in.at[b], ret_s.at[k - 1], ret_r.at[k - 1], (target, s))

    def start_message(k, carry):
        message(k).start()
        return carry

    lax.fori_loop(1, nb, start_message, 0)
    arrived[b] = msg[b]
    second = [
        copy(stage, rates.at[s], rates_s.at[k - 1], rates_r.at[k - 1], at(0, k)) for k in range(1, ns)
    ]
    for c in second:
        c.start()

    def halo(parity):
        copies = [
            (sxu, rxu, (1, 0)),
            (sxd, rxd, (-1, 0)),
            (syu, ryu, (0, 1)),
            (syd, ryd, (0, -1)),
        ]
        out = [
            copy(src, dst.at[parity], halo_s.at[n], halo_r.at[parity, n], at(*to))
            for n, (src, dst, to) in enumerate(copies)
        ]
        for n, (_, cx, cy) in enumerate(CORNERS):
            out.append(
                copy(sc.at[n], rc.at[parity, n], halo_s.at[4 + n], halo_r.at[parity, 4 + n], at(cx, cy))
            )
        return out

    def start_halo(parity):
        copies = halo(parity)
        for n in (2, 3, 4, 5, 6, 7, 0, 1):
            copies[n].start()

    halves = cells_y // 8

    def collide(source):
        def tile(n, carry):
            x, first_row = n // halves, pl.multiple_of(lax.rem(n, halves) * 8, 8)
            span = pl.ds(first_row, 8)
            h = [source[i, x, span, :] for i in range(19)]
            out = collide_sites(
                h, solid_ref[x, span, :] > 0, mask_ref[x, span, :] > 0.5, imposed_ref[x, span, :]
            )
            for i in range(19):
                post[i, x, span, :] = out[i]
            return carry

        lax.fori_loop(0, cells_x * halves, tile, 0)

    def pack():
        for n, i in enumerate(Y_UP):
            for x in range(cells_x):
                syu[n, x : x + 1, :] = post[i, x, cells_y - 1 : cells_y, :]
        for n, i in enumerate(Y_DOWN):
            for x in range(cells_x):
                syd[n, x : x + 1, :] = post[i, x, 0:1, :]
        for n, (i, cx, cy) in enumerate(CORNERS):
            x = cells_x - 1 if cx > 0 else 0
            row = cells_y - 1 if cy > 0 else 0
            sc[n] = jnp.broadcast_to(post[i, x, row : row + 1, :], (8, cells_z))
        for n, i in enumerate(X_UP):
            sxu[n] = post[i, cells_x - 1]
        for n, i in enumerate(X_DOWN):
            sxd[n] = post[i, 0]

    def stream(parity):
        edge = iota((cells_y, cells_z), 0)
        for i, (cx, cy, cz) in enumerate(VELOCITIES):
            for x in range(cells_x):
                xs = x - cx
                inside = 0 <= xs < cells_x
                if inside:
                    value = post[i, xs]
                elif cx > 0:
                    value = rxu[parity, X_UP.index(i)]
                else:
                    value = rxd[parity, X_DOWN.index(i)]
                if cy:
                    if not inside:
                        n = [c[0] for c in CORNERS].index(i)
                        row = rc[parity, n, 0:1, :]
                    elif cy > 0:
                        row = ryu[parity, Y_UP.index(i), xs : xs + 1, :]
                    else:
                        row = ryd[parity, Y_DOWN.index(i), xs : xs + 1, :]
                    value = pltpu.roll(value, cy % cells_y, 0)
                    value = jnp.where(edge == (0 if cy > 0 else cells_y - 1), row, value)
                if cz:
                    value = pltpu.roll(value, cz % cells_z, 1)
                pop_out[i, x] = value

    loads[1].wait()
    collide(pop_ref)
    pack()
    start_halo(0)

    def build(n, ref):
        m = jnp.concatenate([ref[k : k + 1, :] for k in range(4)], axis=1)
        row = m >> 7
        row_at[n] = row
        lines = iota((128, links), 0)
        oh_c[n] = jnp.where(lines == (m & 127), 1.0, 0.0).astype(BF16)
        oh_r[n] = jnp.where(iota((ns * rows, links), 0) == row, 1.0, 0.0).astype(BF16)

    build(0, mem_ref)
    loads[9].wait()
    high, low = split2(w_ref[...])
    w_parts[:, 0:cells_z] = high
    w_parts[:, cells_z : 2 * cells_z] = low
    w_parts[:, 2 * cells_z : 3 * cells_z] = high
    pair[0].wait()
    build(1, other_mem)
    for c in pair[1:]:
        c.wait()
    for c in first:
        c.wait()

    def flows(n, table):
        members = oh_c[n]
        found = jnp.dot(table, jnp.concatenate([members, members], axis=0), preferred_element_type=F32)
        q = jnp.sum(jnp.where(iota((ns * rows, links), 0) == row_at[n], found, 0.0), axis=0, keepdims=True)
        q = [q[:, k * junctions : (k + 1) * junctions] for k in range(4)]
        f = [None] * 4
        count = 0
        for k in range(4):
            for l in range(k + 1, 4):
                term = gbuf[n, count : count + 1, :] * (q[l] - q[k])
                f[k] = term if f[k] is None else f[k] + term
                f[l] = -term if f[l] is None else f[l] - term
                count += 1
        high, low = split2(jnp.concatenate(f, axis=1))
        return lax.dot_general(
            oh_r[n],
            jnp.concatenate([members * high, members * low], axis=0),
            (((1,), (1,)), ((), ())),
            preferred_element_type=F32,
        )

    def inflows():
        def wait_message(k, carry):
            message(k).wait()
            return carry

        lax.fori_loop(1, nb, wait_message, 0)
        got = arrived[...].reshape(nb * 4, cells_z)
        at_row = iota((nb * 4, cells_z), 0) & 3
        labels = jnp.where(
            at_row == 0,
            pltpu.roll(got, nb * 4 - 3, 0),
            jnp.where(at_row == 1, pltpu.roll(got, nb * 4 - 2, 0), pltpu.roll(got, nb * 4 - 1, 0)),
        )
        labels = jnp.where(iota((nb * 4, cells_z), 1) == at_row, labels, 0.0)
        numbers = jnp.sum(labels, axis=1, keepdims=True).astype(jnp.int32)
        numbers = jnp.where(at_row < SLOTS, jnp.broadcast_to(numbers, (nb * 4, 128)), -1)
        ids_ref[...] = numbers
        lane = iota((nb * 4, 128), 1)
        high, low = split2(got)
        value = lax.dot_general(
            jnp.concatenate([high, high, low], axis=1),
            w_parts[...],
            (((1,), (1,)), ((), ())),
            preferred_element_type=F32,
        )
        for n in range(rows):
            mine = jnp.where(numbers == lane + n * 128, value[:, n * 128 : (n + 1) * 128], 0.0)
            flow[n : n + 1, :] = jnp.sum(mine, axis=0, keepdims=True)
        third = [
            copy(flow, inflow_all.at[s], inflow_s.at[k - 1], inflow_r.at[k - 1], at(0, k))
            for k in range(1, ns)
        ]
        for c in third:
            c.start()
        inflow_all[s] = flow[...]
        for c in second:
            c.wait()
        for c in third:
            c.wait()

    def step(t, carry):
        parity = lax.rem(t, 2)
        table = jnp.concatenate(split2(ptab[...].reshape(ns * rows, 128)), axis=1)
        both = flows(0, table) + flows(1, table)
        part[parity, y] = both[:, :128] + both[:, 128:]
        partial = [
            copy(part.at[parity, y], part.at[parity, y], part_s.at[k - 1], part_r.at[parity, k - 1], ring(k))
            for k in range(1, ny)
        ]
        for c in partial:
            c.start()

        now = halo(parity)
        for c in now:
            c.wait_recv()
        stream(parity)
        for c in now:
            c.wait_send()

        @pl.when(t < STEPS - 1)
        def _():
            collide(pop_out)
            pack()
            start_halo(1 - parity)

        @pl.when(t == 0)
        def _():
            inflows()

        for c in partial:
            c.wait()
        balance = part[parity, 0]
        for k in range(1, ny):
            balance = balance + part[parity, k]
        p = ptab[...].reshape(ns * rows, 128)
        rate = rates[:, 0].reshape(ns * rows, 128)
        leak = rates[:, 1].reshape(ns * rows, 128)
        source = inflow_all[...].reshape(ns * rows, 128)
        ptab[...] = (p + rate * (source - balance - leak * p)).reshape(ns, rows, 128)
        return carry

    lax.fori_loop(0, STEPS, step, 0)
    final = ptab[s]
    seg_out[...] = final

    numbers = ids_ref[...]
    lane = iota((nb * 4, 128), 1)
    value = jnp.zeros((nb * 4, 128), F32)
    for n in range(rows):
        value = value + jnp.where(numbers == lane + n * 128, final[n : n + 1, :], 0.0)
    value = jnp.sum(value, axis=1, keepdims=True)
    ret_out[...] = jnp.broadcast_to(value, (nb * 4, 128)).reshape(nb, 4, 128)

    def start_answer(k, carry):
        answer(k).start()
        return carry

    def wait_answer(k, carry):
        answer(k).wait()
        return carry

    lax.fori_loop(1, nb, start_answer, 0)
    ret_in[b] = ret_out[b]
    lax.fori_loop(1, nb, wait_answer, 0)
    back = ret_in[...].reshape(nb * 4, 128)[:, :blocks]
    bp_out[...] = jnp.sum(jnp.where(pick[...] > 0.5, back, 0.0), axis=0, keepdims=True)


def finish(pop_in, seg_in, bp_in, pop_out, seg_out, bp_out, pop_hold, seg_hold, bp_hold, load_s, store_s):
    parts = [(pop_in.at[i], pop_hold.at[i], pop_out.at[i]) for i in range(pop_in.shape[0])]
    parts += [(seg_in, seg_hold, seg_out), (bp_in, bp_hold, bp_out)]
    loads = [pltpu.make_async_copy(a, b, load_s.at[n]) for n, (a, b, _) in enumerate(parts)]
    stores = [pltpu.make_async_copy(b, c, store_s.at[n]) for n, (_, b, c) in enumerate(parts)]
    for c in loads:
        c.start()
    for load, store in zip(loads, stores):
        load.wait()
        store.start()
    for c in stores:
        c.wait()


def local(
    populations,
    solid,
    boundary_pressure,
    block_col,
    block_dest,
    block_seg,
    seg_pressure,
    seg_rate,
    seg_leak,
    profile_weights,
    junc_members,
    junc_arity,
    junc_res,
    junc_cross,
):
    nb, ns = lax.axis_size("brick"), lax.axis_size("sub")
    ny = ns // 2
    _, cx, cy, cz = populations.shape
    segs, blocks, junctions = seg_pressure.shape[0], block_col.shape[0], junc_arity.shape[0]
    rows, links = segs // 128, 4 * junctions
    vmem, dma = pltpu.VMEM, pltpu.SemaphoreType.DMA
    scratch = [
        vmem((19, cx, cy, cz), F32),
        vmem((cx, cy, cz), jnp.int32),
        vmem((1, blocks), F32),
        vmem((1, blocks), jnp.int32),
        vmem((1, blocks), jnp.int32),
        vmem((1, blocks), jnp.int32),
        vmem((rows, 128), F32),
        vmem((segs, cz), F32),
        vmem((4, junctions), jnp.int32),
        vmem((1, junctions), jnp.int32),
        vmem((4, junctions), F32),
        vmem((4, 4, junctions), F32),
        dma((14,)),
        vmem((19, cx, cy, cz), F32),
        vmem((cx, cy, cz), F32),
        vmem((cx, cy, cz), F32),
        vmem((5, cy, cz), F32),
        vmem((5, cy, cz), F32),
        vmem((5, cx, cz), F32),
        vmem((5, cx, cz), F32),
        vmem((4, 8, cz), F32),
        vmem((2, 5, cy, cz), F32),
        vmem((2, 5, cy, cz), F32),
        vmem((2, 5, cx, cz), F32),
        vmem((2, 5, cx, cz), F32),
        vmem((2, 4, 8, cz), F32),
        vmem((ns, rows, 128), F32),
        vmem((2, rows, 128), F32),
        vmem((ns, 2, rows, 128), F32),
        vmem((ns, rows, 128), F32),
        vmem((rows, 128), F32),
        vmem((4, junctions), jnp.int32),
        vmem((2, 8, junctions), F32),
        vmem((2, 1, links), jnp.int32),
        vmem((2, 128, links), BF16),
        vmem((2, ns * rows, links), BF16),
        vmem((2, ny, ns * rows, 128), F32),
        vmem((nb, 4, cz), F32),
        vmem((nb, 4, cz), F32),
        vmem((nb * 4, blocks), F32),
        vmem((nb * 4, cz), jnp.int32),
        vmem((segs, 3 * cz), BF16),
        vmem((nb, 4, 128), F32),
        vmem((nb, 4, 128), F32),
        dma((8,)),
        dma((2, 8)),
        dma((ns - 1,)),
        dma((ns - 1,)),
        dma((ns - 1,)),
        dma((ns - 1,)),
        dma((ns - 1,)),
        dma((ns - 1,)),
        dma((2,)),
        dma((2,)),
        dma((ny - 1,)),
        dma((2, ny - 1)),
        dma((nb - 1,)),
        dma((nb - 1,)),
        dma((nb - 1,)),
        dma((nb - 1,)),
    ]
    spec = pl.BlockSpec(memory_space=vmem)
    lattice, pressure, back = pl.pallas_call(
        functools.partial(kernel, nb, ns),
        out_shape=(
            jax.ShapeDtypeStruct(populations.shape, F32),
            jax.ShapeDtypeStruct((rows, 128), F32),
            jax.ShapeDtypeStruct((1, blocks), F32),
        ),
        in_specs=[pl.BlockSpec(memory_space=pltpu.HBM)] * 14,
        out_specs=(spec, spec, spec),
        scratch_shapes=scratch,
        compiler_params=pltpu.CompilerParams(
            collective_id=0, has_side_effects=True, vmem_limit_bytes=56 * 2**20
        ),
        name="coupled",
    )(
        populations,
        solid,
        boundary_pressure.reshape(1, blocks),
        block_col.reshape(1, blocks),
        block_dest.reshape(1, blocks),
        block_seg.reshape(1, blocks),
        seg_pressure.reshape(rows, 128),
        seg_rate.reshape(rows, 128),
        seg_leak.reshape(rows, 128),
        profile_weights,
        junc_members,
        junc_arity.reshape(1, junctions),
        junc_res,
        junc_cross,
    )
    hbm = pl.BlockSpec(memory_space=pltpu.HBM)
    lattice, pressure, back = pl.pallas_call(
        finish,
        out_shape=(
            jax.ShapeDtypeStruct(populations.shape, F32),
            jax.ShapeDtypeStruct((rows, 128), F32),
            jax.ShapeDtypeStruct((1, blocks), F32),
        ),
        in_specs=[hbm] * 3,
        out_specs=(hbm, hbm, hbm),
        scratch_shapes=[
            vmem(populations.shape, F32),
            vmem((rows, 128), F32),
            vmem((1, blocks), F32),
            dma((21,)),
            dma((21,)),
        ],
        compiler_params=pltpu.CompilerParams(vmem_limit_bytes=56 * 2**20),
        name="finish",
    )(lattice, pressure, back)
    return lattice, pressure.reshape(segs), back.reshape(blocks)


def solution(mesh):
    return jax.shard_map(
        local,
        mesh=mesh,
        in_specs=(
            P(None, "brick", "sub", None),
            P("brick", "sub", None),
            P(("brick", "sub")),
            P(("brick", "sub")),
            P(("brick", "sub"), None),
            P(("brick", "sub")),
            P(("brick", "sub")),
            P(("brick", "sub")),
            P(("brick", "sub")),
            P(("brick", "sub"), None),
            P(None, ("brick", "sub")),
            P(("brick", "sub")),
            P(None, ("brick", "sub")),
            P(None, None, ("brick", "sub")),
        ),
        out_specs=(P(None, "brick", "sub", None), P(("brick", "sub")), P(("brick", "sub"))),
        check_vma=False,
    )
```

```python
import functools

import jax
import jax.numpy as jnp
import numpy as np
from jax import lax
from jax.experimental import pallas as pl
from jax.experimental.pallas import tpu as pltpu
from jax.sharding import PartitionSpec as P

STEPS = 6
SLOTS = 3
MESH = pl.DeviceIdType.MESH
F32 = jnp.float32
BF16 = jnp.bfloat16
HIGHEST = lax.Precision.HIGHEST

VELOCITIES = [
    (0, 0, 0),
    (1, 0, 0),
    (-1, 0, 0),
    (0, 1, 0),
    (0, -1, 0),
    (0, 0, 1),
    (0, 0, -1),
    (1, 1, 0),
    (-1, -1, 0),
    (1, -1, 0),
    (-1, 1, 0),
    (1, 0, 1),
    (-1, 0, -1),
    (1, 0, -1),
    (-1, 0, 1),
    (0, 1, 1),
    (0, -1, -1),
    (0, 1, -1),
    (0, -1, 1),
]
OPPOSITE = [0, 2, 1, 4, 3, 6, 5, 8, 7, 10, 9, 12, 11, 14, 13, 16, 15, 18, 17]
RELAXATION = 1.25
DENSITY_SCALE = 0.1
X_UP = [i for i, c in enumerate(VELOCITIES) if c[0] == 1]
X_DOWN = [i for i, c in enumerate(VELOCITIES) if c[0] == -1]
Y_UP = [i for i, c in enumerate(VELOCITIES) if c[1] == 1]
Y_DOWN = [i for i, c in enumerate(VELOCITIES) if c[1] == -1]
CORNERS = [(7, 1, 1), (8, -1, -1), (9, 1, -1), (10, -1, 1)]


def iota(shape, axis):
    return lax.broadcasted_iota(jnp.int32, shape, axis)


def collide_sites(h, solid, mask, imposed):
    w0, w1, w2 = 1.0 / 3.0, 1.0 / 18.0, 1.0 / 36.0
    plus = {i: h[i] + h[i + 1] for i in range(1, 19, 2)}
    minus = {i: h[i] - h[i + 1] for i in range(1, 19, 2)}
    near = plus[1] + plus[3] + plus[5]
    far = (plus[7] + plus[9]) + (plus[11] + plus[13]) + (plus[15] + plus[17])
    density = 1.0 + (w0 * h[0] + w1 * near + w2 * far)
    inverse = 1.0 / density
    ux = (w1 * minus[1] + w2 * ((minus[7] + minus[9]) + (minus[11] + minus[13]))) * inverse
    uy = (w1 * minus[3] + w2 * ((minus[7] - minus[9]) + (minus[15] + minus[17]))) * inverse
    uz = (w1 * minus[5] + w2 * ((minus[11] - minus[13]) + (minus[15] - minus[17]))) * inverse
    base = 1.0 - 1.5 * (ux * ux + uy * uy + uz * uz)
    along = {1: ux, 3: uy, 5: uz, 7: ux + uy, 9: ux - uy, 11: ux + uz, 13: ux - uz, 15: uy + uz, 17: uy - uz}
    scale = jnp.where(mask, imposed, RELAXATION * density)
    shift = jnp.where(mask, -1.0, -RELAXATION)
    keep = jnp.where(mask, 0.0, 1.0 - RELAXATION)
    bounce = jnp.logical_and(solid, jnp.logical_not(mask))
    post = [None] * 19
    post[0] = jnp.where(bounce, h[0], scale * base + (shift + keep * h[0]))
    for i in range(1, 19, 2):
        c = along[i]
        even = base + 4.5 * (c * c)
        odd = 3.0 * c
        post[i] = jnp.where(bounce, h[i + 1], scale * (even + odd) + (shift + keep * h[i]))
        post[i + 1] = jnp.where(bounce, h[i], scale * (even - odd) + (shift + keep * h[i + 1]))
    return post


def off_diagonals(live, res, cross):
    rows = [[None] * 4 for _ in range(4)]
    sides = [[None] * 4 for _ in range(4)]
    zero = jnp.zeros_like(live[0])
    for k in range(4):
        for l in range(4):
            if k == l:
                rows[k][l] = res[k]
                sides[k][l] = live[k]
            else:
                rows[k][l] = live[k] * live[l] * (0.5 * (cross[k][l] + cross[l][k]))
                sides[k][l] = zero
    for c in range(4):
        inverse = 1.0 / rows[c][c]
        for r in range(c + 1, 4):
            factor = rows[r][c] * inverse
            for l in range(c + 1, 4):
                rows[r][l] = rows[r][l] - factor * rows[c][l]
            for l in range(c + 1):
                sides[r][l] = sides[r][l] - factor * sides[c][l]
    answer = [None] * 4
    for r in reversed(range(4)):
        inverse = 1.0 / rows[r][r]
        answer[r] = []
        for l in range(4):
            running = sides[r][l]
            for c in range(r + 1, 4):
                running = running - rows[r][c] * answer[c][l]
            answer[r].append(running * inverse)
    ones = [answer[k][0] + answer[k][1] + answer[k][2] + answer[k][3] for k in range(4)]
    total = 1.0 / (live[0] * ones[0] + live[1] * ones[1] + live[2] * ones[2] + live[3] * ones[3])
    pairs = []
    for a in range(4):
        for b in range(a + 1, 4):
            pairs.append(live[a] * live[b] * (answer[a][b] - ones[a] * ones[b] * total))
    return pairs


def split2(x):
    high = x.astype(BF16)
    return high, (x - high.astype(F32)).astype(BF16)


def split3(x):
    high = x.astype(BF16)
    rest = x - high.astype(F32)
    middle = rest.astype(BF16)
    return high, middle, (rest - middle.astype(F32)).astype(BF16)


def kernel(
    nb,
    ns,
    pop_hbm,
    solid_hbm,
    bp_hbm,
    col_hbm,
    dest_hbm,
    seg_hbm,
    segp_hbm,
    rate_hbm,
    leak_hbm,
    w_hbm,
    mem_hbm,
    arity_hbm,
    res_hbm,
    cross_hbm,
    pop_out,
    seg_out,
    bp_out,
    pop_ref,
    solid_ref,
    bp_ref,
    col_ref,
    dest_ref,
    seg_ref,
    segp_ref,
    w_ref,
    mem_ref,
    arity_ref,
    res_ref,
    cross_ref,
    load_s,
    post,
    mask_ref,
    imposed_ref,
    sxu,
    sxd,
    syu,
    syd,
    sc,
    rxu,
    rxd,
    ryu,
    ryd,
    rc,
    ptab,
    stage,
    rates,
    inflow_all,
    flow,
    other_mem,
    gbuf,
    row_at,
    oh_c,
    oh_r,
    part,
    msg,
    arrived,
    pick,
    ids_ref,
    w_parts,
    ret_out,
    ret_in,
    halo_s,
    halo_r,
    first_s,
    first_r,
    rates_s,
    rates_r,
    inflow_s,
    inflow_r,
    pair_s,
    pair_r,
    part_s,
    part_r,
    msg_s,
    msg_r,
    ret_s,
    ret_r,
):
    ny = ns // 2
    rows = segp_ref.shape[0]
    junctions = mem_ref.shape[1]
    links = 4 * junctions
    blocks = col_ref.shape[1]
    cells_x, cells_y, cells_z = solid_ref.shape
    b, s = lax.axis_index("brick"), lax.axis_index("sub")
    hi, y = s // ny, lax.rem(s, ny)
    other = 1 - hi
    partner = (b, other * ny + y)

    def at(db, ds):
        return (lax.rem(b + db + nb, nb), lax.rem(s + ds + ns, ns))

    def ring(k):
        return (b, hi * ny + lax.rem(y + k, ny))

    def copy(src, dst, send, recv, device):
        return pltpu.make_async_remote_copy(
            src_ref=src, dst_ref=dst, send_sem=send, recv_sem=recv, device_id=device, device_id_type=MESH
        )

    barrier = pltpu.get_barrier_semaphore()

    def greet(k, carry):
        pl.semaphore_signal(barrier, inc=1, device_id=at(k, 0), device_id_type=MESH)
        return carry

    lax.fori_loop(1, nb, greet, 0)
    for k in range(1, ns):
        pl.semaphore_signal(barrier, inc=1, device_id=at(0, k), device_id_type=MESH)
    for _, cx, cy in CORNERS:
        pl.semaphore_signal(barrier, inc=1, device_id=at(cx, cy), device_id_type=MESH)

    loads = [
        pltpu.make_async_copy(src, dst, load_s.at[n])
        for n, (src, dst) in enumerate(
            [
                (pop_hbm, pop_ref),
                (solid_hbm, solid_ref),
                (bp_hbm, bp_ref),
                (col_hbm, col_ref),
                (dest_hbm, dest_ref),
                (seg_hbm, seg_ref),
                (segp_hbm, segp_ref),
                (rate_hbm, stage.at[0]),
                (leak_hbm, stage.at[1]),
                (w_hbm, w_ref),
                (mem_hbm, mem_ref),
                (arity_hbm, arity_ref),
                (res_hbm, res_ref),
                (cross_hbm, cross_ref),
            ]
        )
    ]
    for n in (11, 12, 13, 4, 5, 3, 2, 0, 10, 6, 7, 8, 1, 9):
        loads[n].start()

    def halo(parity):
        copies = [
            (sxu, rxu, (1, 0)),
            (sxd, rxd, (-1, 0)),
            (syu, ryu, (0, 1)),
            (syd, ryd, (0, -1)),
        ]
        out = [
            copy(src, dst.at[parity], halo_s.at[n], halo_r.at[parity, n], at(*to))
            for n, (src, dst, to) in enumerate(copies)
        ]
        for n, (_, cx, cy) in enumerate(CORNERS):
            out.append(
                copy(sc.at[n], rc.at[parity, n], halo_s.at[4 + n], halo_r.at[parity, 4 + n], at(cx, cy))
            )
        return out

    def start_halo(parity):
        copies = halo(parity)
        for n in (2, 3, 4, 5, 6, 7, 0, 1):
            copies[n].start()

    halves = cells_y // 8

    def collide(source):
        def tile(n, carry):
            x, first_row = n // halves, pl.multiple_of(lax.rem(n, halves) * 8, 8)
            span = pl.ds(first_row, 8)
            h = [source[i, x, span, :] for i in range(19)]
            out = collide_sites(
                h, solid_ref[x, span, :] > 0, mask_ref[x, span, :] > 0.5, imposed_ref[x, span, :]
            )
            for i in range(19):
                post[i, x, span, :] = out[i]
            return carry

        lax.fori_loop(0, cells_x * halves, tile, 0)

    def pack():
        for n, i in enumerate(Y_UP):
            for x in range(cells_x):
                syu[n, x : x + 1, :] = post[i, x, cells_y - 1 : cells_y, :]
        for n, i in enumerate(Y_DOWN):
            for x in range(cells_x):
                syd[n, x : x + 1, :] = post[i, x, 0:1, :]
        for n, (i, cx, cy) in enumerate(CORNERS):
            x = cells_x - 1 if cx > 0 else 0
            row = cells_y - 1 if cy > 0 else 0
            sc[n] = jnp.broadcast_to(post[i, x, row : row + 1, :], (8, cells_z))
        for n, i in enumerate(X_UP):
            sxu[n] = post[i, cells_x - 1]
        for n, i in enumerate(X_DOWN):
            sxd[n] = post[i, 0]

    def stream(parity):
        edge = iota((cells_y, cells_z), 0)
        for i, (cx, cy, cz) in enumerate(VELOCITIES):
            for x in range(cells_x):
                xs = x - cx
                inside = 0 <= xs < cells_x
                if inside:
                    value = post[i, xs]
                elif cx > 0:
                    value = rxu[parity, X_UP.index(i)]
                else:
                    value = rxd[parity, X_DOWN.index(i)]
                if cy:
                    if not inside:
                        n = [c[0] for c in CORNERS].index(i)
                        row = rc[parity, n, 0:1, :]
                    elif cy > 0:
                        row = ryu[parity, Y_UP.index(i), xs : xs + 1, :]
                    else:
                        row = ryd[parity, Y_DOWN.index(i), xs : xs + 1, :]
                    value = pltpu.roll(value, cy % cells_y, 0)
                    value = jnp.where(edge == (0 if cy > 0 else cells_y - 1), row, value)
                if cz:
                    value = pltpu.roll(value, cz % cells_z, 1)
                pop_out[i, x] = value

    def build(n, ref):
        m = jnp.concatenate([ref[k : k + 1, :] for k in range(4)], axis=1)
        row = m >> 7
        row_at[n] = row
        lines = iota((128, links), 0)
        oh_c[n] = jnp.where(lines == (m & 127), 1.0, 0.0).astype(BF16)
        oh_r[n] = jnp.where(iota((ns * rows, links), 0) == row, 1.0, 0.0).astype(BF16)

    columns = cells_x * cells_y

    def hit():
        return iota((columns, blocks), 0) == col_ref[...]

    def prepare_junctions():
        for n in (11, 12, 13):
            loads[n].wait()
        live = [jnp.where(arity_ref[...] > k, 1.0, 0.0) for k in range(4)]
        pairs = off_diagonals(
            live,
            [res_ref[k : k + 1, :] for k in range(4)],
            [[cross_ref[k, l : l + 1, :] for l in range(4)] for k in range(4)],
        )
        for n, value in enumerate(pairs):
            gbuf[0, n : n + 1, :] = value
        gbuf[0, 6:8, :] = jnp.zeros((2, junctions), F32)

    def prepare_lattice():
        for n in (0, 1, 2, 3):
            loads[n].wait()
        hits = hit()
        found = jnp.sum(jnp.where(hits, 1.0, 0.0), axis=1, keepdims=True)
        pressed = jnp.sum(jnp.where(hits, bp_ref[...], 0.0), axis=1, keepdims=True)
        mask_ref[...] = jnp.broadcast_to(found, (columns, cells_z)).reshape(cells_x, cells_y, cells_z)
        imposed_ref[...] = jnp.broadcast_to(1.0 + DENSITY_SCALE * pressed, (columns, cells_z)).reshape(
            cells_x, cells_y, cells_z
        )
        collide(pop_ref)
        pack()

    def prepare_messages():
        for n in (4, 5):
            loads[n].wait()
        dest = dest_ref[...]
        eye = iota((blocks, blocks), 0) == iota((blocks, blocks), 1)
        dest_column = jnp.sum(jnp.where(eye, dest, 0), axis=1, keepdims=True)
        earlier = jnp.logical_and(dest_column == dest, iota((blocks, blocks), 0) < iota((blocks, blocks), 1))
        slot = jnp.sum(jnp.where(earlier, 1, 0), axis=0, keepdims=True)
        slot_column = jnp.sum(jnp.where(eye, slot, 0), axis=1, keepdims=True)
        number_column = jnp.sum(jnp.where(eye, seg_ref[...] + 1, 0), axis=1, keepdims=True)
        r = iota((nb * 4, blocks), 0)
        aimed = (r >> 2) == dest
        chosen = jnp.where(jnp.logical_and(aimed, (r & 3) == slot), 1.0, 0.0)
        pick[...] = chosen
        hits = hit()
        selector = lax.dot_general(
            chosen.astype(BF16),
            jnp.where(hits, 1.0, 0.0).astype(BF16),
            (((1,), (1,)), ((), ())),
            preferred_element_type=F32,
        ).astype(BF16)
        axial = jnp.zeros((columns, cells_z), F32)
        for i, c in enumerate(VELOCITIES):
            if c[0]:
                weight = c[0] * (1.0 / 18.0 if i < 7 else 1.0 / 36.0)
                axial = axial + weight * pop_ref[i].reshape(columns, cells_z)
        profiles = jnp.dot(
            jnp.concatenate([selector] * 3, axis=1),
            jnp.concatenate(split3(axial), axis=0),
            preferred_element_type=F32,
        )
        number = jnp.where(iota((blocks, cells_z), 1) == slot_column, number_column, 0)
        numbers = jnp.dot(
            jnp.concatenate([jnp.where(aimed, 1.0, 0.0).astype(BF16)] * 2, axis=1),
            jnp.concatenate([(number >> 6).astype(F32) * 64.0, (number & 63).astype(F32)], axis=0).astype(BF16),
            preferred_element_type=F32,
        )
        is_label = (iota((nb * 4, cells_z), 0) & 3) == 3
        msg[...] = jnp.where(is_label, numbers - 1.0, profiles).reshape(nb, 4, cells_z)

    def prepare_network():
        for n in (6, 7, 8, 10):
            loads[n].wait()
        ptab[s] = segp_ref[...]
        rates[s] = stage[...]
        build(0, mem_ref)
        loads[9].wait()
        high, low = split2(w_ref[...])
        w_parts[:, 0:cells_z] = high
        w_parts[:, cells_z : 2 * cells_z] = low
        w_parts[:, 2 * cells_z : 3 * cells_z] = high

    pair = [
        copy(mem_hbm, other_mem, pair_s.at[0], pair_r.at[0], partner),
        copy(gbuf.at[0], gbuf.at[1], pair_s.at[1], pair_r.at[1], partner),
    ]
    first = [
        copy(segp_hbm, ptab.at[s], first_s.at[k - 1], first_r.at[k - 1], at(0, k)) for k in range(1, ns)
    ]
    second = [
        copy(stage, rates.at[s], rates_s.at[k - 1], rates_r.at[k - 1], at(0, k)) for k in range(1, ns)
    ]

    def message(k):
        target = lax.rem(b + k, nb)
        return copy(msg.at[target], arrived.at[b], msg_s, msg_r, (target, s))

    def answer(k):
        target = lax.rem(b + k, nb)
        return copy(ret_out.at[target], ret_in.at[b], ret_s, ret_r, (target, s))

    def start_message(k, carry):
        message(lax.rem(k + nb // 4, nb - 1) + 1).start()
        return carry

    early, late = hi == 0, hi != 0

    @pl.when(early)
    def _():
        prepare_junctions()
        prepare_lattice()
        prepare_messages()
        prepare_network()

    pl.semaphore_wait(barrier, nb - 1 + ns - 1 + len(CORNERS))

    pair[0].start()
    for c in first:
        c.start()

    @pl.when(late)
    def _():
        prepare_junctions()

    pair[1].start()

    @pl.when(late)
    def _():
        prepare_lattice()

    start_halo(0)

    @pl.when(late)
    def _():
        prepare_messages()

    lax.fori_loop(1, nb, start_message, 0)
    arrived[b] = msg[b]

    @pl.when(late)
    def _():
        prepare_network()

    def flows(n, table):
        members = oh_c[n]
        found = jnp.dot(table, jnp.concatenate([members, members], axis=0), preferred_element_type=F32)
        q = jnp.sum(jnp.where(iota((ns * rows, links), 0) == row_at[n], found, 0.0), axis=0, keepdims=True)
        q = [q[:, k * junctions : (k + 1) * junctions] for k in range(4)]
        f = [None] * 4
        count = 0
        for k in range(4):
            for l in range(k + 1, 4):
                term = gbuf[n, count : count + 1, :] * (q[l] - q[k])
                f[k] = term if f[k] is None else f[k] + term
                f[l] = -term if f[l] is None else f[l] - term
                count += 1
        high, low = split2(jnp.concatenate(f, axis=1))
        return lax.dot_general(
            oh_r[n],
            jnp.concatenate([members * high, members * low], axis=0),
            (((1,), (1,)), ((), ())),
            preferred_element_type=F32,
        )

    def inflows():
        whole = pl.ds(0, nb - 1)
        copy(msg.at[whole], arrived.at[whole], msg_s, msg_r, at(1, 0)).wait()
        got = arrived[...].reshape(nb * 4, cells_z)
        at_row = iota((nb * 4, cells_z), 0) & 3
        labels = jnp.where(
            at_row == 0,
            pltpu.roll(got, nb * 4 - 3, 0),
            jnp.where(at_row == 1, pltpu.roll(got, nb * 4 - 2, 0), pltpu.roll(got, nb * 4 - 1, 0)),
        )
        labels = jnp.where(iota((nb * 4, cells_z), 1) == at_row, labels, 0.0)
        numbers = jnp.sum(labels, axis=1, keepdims=True).astype(jnp.int32)
        numbers = jnp.where(at_row < SLOTS, jnp.broadcast_to(numbers, (nb * 4, 128)), -1)
        ids_ref[...] = numbers
        lane = iota((nb * 4, 128), 1)
        high, low = split2(got)
        value = lax.dot_general(
            jnp.concatenate([high, high, low], axis=1),
            w_parts[...],
            (((1,), (1,)), ((), ())),
            preferred_element_type=F32,
        )
        for n in range(rows):
            mine = jnp.where(numbers == lane + n * 128, value[:, n * 128 : (n + 1) * 128], 0.0)
            flow[n : n + 1, :] = jnp.sum(mine, axis=0, keepdims=True)
        third = [
            copy(flow, inflow_all.at[s], inflow_s.at[k - 1], inflow_r.at[k - 1], at(0, k))
            for k in range(1, ns)
        ]
        for c in third:
            c.start()
        inflow_all[s] = flow[...]
        for c in second:
            c.wait()
        for c in third:
            c.wait()

    def table_of():
        return jnp.concatenate(split2(ptab[...].reshape(ns * rows, 128)), axis=1)

    def joined(both):
        return both[:, :128] + both[:, 128:]

    for c in first:
        c.wait()
    table = table_of()
    both = flows(0, table)
    pair[0].wait()
    build(1, other_mem)
    pair[1].wait()
    for c in second:
        c.start()
    both = both + flows(1, table)
    part[0, y] = joined(both)

    def step(t, carry):
        parity = lax.rem(t, 2)
        partial = [
            copy(part.at[parity, y], part.at[parity, y], part_s.at[k - 1], part_r.at[parity, k - 1], ring(k))
            for k in range(1, ny)
        ]
        for c in partial:
            c.start()

        now = halo(parity)
        for c in now:
            c.wait_recv()
        stream(parity)
        for c in now:
            c.wait_send()

        @pl.when(t < STEPS - 1)
        def _():
            collide(pop_out)
            pack()
            start_halo(1 - parity)

        @pl.when(t == 0)
        def _():
            inflows()

        for c in partial:
            c.wait()
        balance = part[parity, 0]
        for k in range(1, ny):
            balance = balance + part[parity, k]
        p = ptab[...].reshape(ns * rows, 128)
        rate = rates[:, 0].reshape(ns * rows, 128)
        leak = rates[:, 1].reshape(ns * rows, 128)
        source = inflow_all[...].reshape(ns * rows, 128)
        ptab[...] = (p + rate * (source - balance - leak * p)).reshape(ns, rows, 128)

        @pl.when(t < STEPS - 1)
        def _():
            table = table_of()
            part[1 - parity, y] = joined(flows(0, table) + flows(1, table))

        return carry

    lax.fori_loop(0, STEPS, step, 0)
    final = ptab[s]
    seg_out[...] = final

    numbers = ids_ref[...]
    lane = iota((nb * 4, 128), 1)
    value = jnp.zeros((nb * 4, 128), F32)
    for n in range(rows):
        value = value + jnp.where(numbers == lane + n * 128, final[n : n + 1, :], 0.0)
    value = jnp.sum(value, axis=1, keepdims=True)
    ret_out[...] = jnp.broadcast_to(value, (nb * 4, 128)).reshape(nb, 4, 128)

    def start_answer(k, carry):
        answer(lax.rem(k + nb // 4, nb - 1) + 1).start()
        return carry

    lax.fori_loop(1, nb, start_answer, 0)
    ret_in[b] = ret_out[b]
    whole = pl.ds(0, nb - 1)
    copy(ret_out.at[whole], ret_in.at[whole], ret_s, ret_r, at(1, 0)).wait()
    back = ret_in[...].reshape(nb * 4, 128)[:, :blocks]
    bp_out[...] = jnp.sum(jnp.where(pick[...] > 0.5, back, 0.0), axis=0, keepdims=True)


def finish(pop_in, seg_in, bp_in, pop_out, seg_out, bp_out, sems):
    copies = [pltpu.make_async_copy(pop_in.at[i], pop_out.at[i], sems.at[i]) for i in range(pop_in.shape[0])]
    copies.append(pltpu.make_async_copy(seg_in, seg_out, sems.at[len(copies)]))
    copies.append(pltpu.make_async_copy(bp_in, bp_out, sems.at[len(copies)]))
    for c in copies:
        c.start()
    for c in copies:
        c.wait()


def local(
    populations,
    solid,
    boundary_pressure,
    block_col,
    block_dest,
    block_seg,
    seg_pressure,
    seg_rate,
    seg_leak,
    profile_weights,
    junc_members,
    junc_arity,
    junc_res,
    junc_cross,
):
    nb, ns = lax.axis_size("brick"), lax.axis_size("sub")
    ny = ns // 2
    _, cx, cy, cz = populations.shape
    segs, blocks, junctions = seg_pressure.shape[0], block_col.shape[0], junc_arity.shape[0]
    rows, links = segs // 128, 4 * junctions
    vmem, dma = pltpu.VMEM, pltpu.SemaphoreType.DMA
    scratch = [
        vmem((19, cx, cy, cz), F32),
        vmem((cx, cy, cz), jnp.int32),
        vmem((1, blocks), F32),
        vmem((1, blocks), jnp.int32),
        vmem((1, blocks), jnp.int32),
        vmem((1, blocks), jnp.int32),
        vmem((rows, 128), F32),
        vmem((segs, cz), F32),
        vmem((4, junctions), jnp.int32),
        vmem((1, junctions), jnp.int32),
        vmem((4, junctions), F32),
        vmem((4, 4, junctions), F32),
        dma((14,)),
        vmem((19, cx, cy, cz), F32),
        vmem((cx, cy, cz), F32),
        vmem((cx, cy, cz), F32),
        vmem((5, cy, cz), F32),
        vmem((5, cy, cz), F32),
        vmem((5, cx, cz), F32),
        vmem((5, cx, cz), F32),
        vmem((4, 8, cz), F32),
        vmem((2, 5, cy, cz), F32),
        vmem((2, 5, cy, cz), F32),
        vmem((2, 5, cx, cz), F32),
        vmem((2, 5, cx, cz), F32),
        vmem((2, 4, 8, cz), F32),
        vmem((ns, rows, 128), F32),
        vmem((2, rows, 128), F32),
        vmem((ns, 2, rows, 128), F32),
        vmem((ns, rows, 128), F32),
        vmem((rows, 128), F32),
        vmem((4, junctions), jnp.int32),
        vmem((2, 8, junctions), F32),
        vmem((2, 1, links), jnp.int32),
        vmem((2, 128, links), BF16),
        vmem((2, ns * rows, links), BF16),
        vmem((2, ny, ns * rows, 128), F32),
        vmem((nb, 4, cz), F32),
        vmem((nb, 4, cz), F32),
        vmem((nb * 4, blocks), F32),
        vmem((nb * 4, cz), jnp.int32),
        vmem((segs, 3 * cz), BF16),
        vmem((nb, 4, 128), F32),
        vmem((nb, 4, 128), F32),
        dma((8,)),
        dma((2, 8)),
        dma((ns - 1,)),
        dma((ns - 1,)),
        dma((ns - 1,)),
        dma((ns - 1,)),
        dma((ns - 1,)),
        dma((ns - 1,)),
        dma((2,)),
        dma((2,)),
        dma((ny - 1,)),
        dma((2, ny - 1)),
        dma,
        dma,
        dma,
        dma,
    ]
    spec = pl.BlockSpec(memory_space=vmem)
    lattice, pressure, back = pl.pallas_call(
        functools.partial(kernel, nb, ns),
        out_shape=(
            pltpu.VMEM(populations.shape, F32),
            pltpu.VMEM((rows, 128), F32),
            pltpu.VMEM((1, blocks), F32),
        ),
        in_specs=[pl.BlockSpec(memory_space=pltpu.HBM)] * 14,
        out_specs=(spec, spec, spec),
        scratch_shapes=scratch,
        compiler_params=pltpu.CompilerParams(
            collective_id=0, has_side_effects=True, vmem_limit_bytes=56 * 2**20
        ),
        name="coupled",
    )(
        populations,
        solid,
        boundary_pressure.reshape(1, blocks),
        block_col.reshape(1, blocks),
        block_dest.reshape(1, blocks),
        block_seg.reshape(1, blocks),
        seg_pressure.reshape(rows, 128),
        seg_rate.reshape(rows, 128),
        seg_leak.reshape(rows, 128),
        profile_weights,
        junc_members,
        junc_arity.reshape(1, junctions),
        junc_res,
        junc_cross,
    )
    hbm = pl.BlockSpec(memory_space=pltpu.HBM)
    lattice, pressure, back = pl.pallas_call(
        finish,
        out_shape=(
            jax.ShapeDtypeStruct(populations.shape, F32),
            jax.ShapeDtypeStruct((rows, 128), F32),
            jax.ShapeDtypeStruct((1, blocks), F32),
        ),
        in_specs=[spec] * 3,
        out_specs=(hbm, hbm, hbm),
        scratch_shapes=[
            dma((21,)),
        ],
        compiler_params=pltpu.CompilerParams(vmem_limit_bytes=2**20),
        name="finish",
    )(lattice, pressure, back)
    return lattice, pressure.reshape(segs), back.reshape(blocks)


def solution(mesh):
    return jax.shard_map(
        local,
        mesh=mesh,
        in_specs=(
            P(None, "brick", "sub", None),
            P("brick", "sub", None),
            P(("brick", "sub")),
            P(("brick", "sub")),
            P(("brick", "sub"), None),
            P(("brick", "sub")),
            P(("brick", "sub")),
            P(("brick", "sub")),
            P(("brick", "sub")),
            P(("brick", "sub"), None),
            P(None, ("brick", "sub")),
            P(("brick", "sub")),
            P(None, ("brick", "sub")),
            P(None, None, ("brick", "sub")),
        ),
        out_specs=(P(None, "brick", "sub", None), P(("brick", "sub")), P(("brick", "sub"))),
        check_vma=False,
    )
```

```python
import functools

import jax
import jax.numpy as jnp
import numpy as np
from jax import lax
from jax.experimental import pallas as pl
from jax.experimental.pallas import tpu as pltpu
from jax.sharding import PartitionSpec as P

STEPS = 6
SLOTS = 3
MESH = pl.DeviceIdType.MESH
F32 = jnp.float32
BF16 = jnp.bfloat16
HIGHEST = lax.Precision.HIGHEST

VELOCITIES = [
    (0, 0, 0),
    (1, 0, 0),
    (-1, 0, 0),
    (0, 1, 0),
    (0, -1, 0),
    (0, 0, 1),
    (0, 0, -1),
    (1, 1, 0),
    (-1, -1, 0),
    (1, -1, 0),
    (-1, 1, 0),
    (1, 0, 1),
    (-1, 0, -1),
    (1, 0, -1),
    (-1, 0, 1),
    (0, 1, 1),
    (0, -1, -1),
    (0, 1, -1),
    (0, -1, 1),
]
OPPOSITE = [0, 2, 1, 4, 3, 6, 5, 8, 7, 10, 9, 12, 11, 14, 13, 16, 15, 18, 17]
RELAXATION = 1.25
DENSITY_SCALE = 0.1
X_UP = [i for i, c in enumerate(VELOCITIES) if c[0] == 1]
X_DOWN = [i for i, c in enumerate(VELOCITIES) if c[0] == -1]
Y_UP = [i for i, c in enumerate(VELOCITIES) if c[1] == 1]
Y_DOWN = [i for i, c in enumerate(VELOCITIES) if c[1] == -1]
CORNERS = [(7, 1, 1), (8, -1, -1), (9, 1, -1), (10, -1, 1)]


def iota(shape, axis):
    return lax.broadcasted_iota(jnp.int32, shape, axis)


def collide_sites(h, solid, mask, imposed):
    w0, w1, w2 = 1.0 / 3.0, 1.0 / 18.0, 1.0 / 36.0
    plus = {i: h[i] + h[i + 1] for i in range(1, 19, 2)}
    minus = {i: h[i] - h[i + 1] for i in range(1, 19, 2)}
    near = plus[1] + plus[3] + plus[5]
    far = (plus[7] + plus[9]) + (plus[11] + plus[13]) + (plus[15] + plus[17])
    density = 1.0 + (w0 * h[0] + w1 * near + w2 * far)
    inverse = 1.0 / density
    ux = (w1 * minus[1] + w2 * ((minus[7] + minus[9]) + (minus[11] + minus[13]))) * inverse
    uy = (w1 * minus[3] + w2 * ((minus[7] - minus[9]) + (minus[15] + minus[17]))) * inverse
    uz = (w1 * minus[5] + w2 * ((minus[11] - minus[13]) + (minus[15] - minus[17]))) * inverse
    base = 1.0 - 1.5 * (ux * ux + uy * uy + uz * uz)
    along = {1: ux, 3: uy, 5: uz, 7: ux + uy, 9: ux - uy, 11: ux + uz, 13: ux - uz, 15: uy + uz, 17: uy - uz}
    scale = jnp.where(mask, imposed, RELAXATION * density)
    shift = jnp.where(mask, -1.0, -RELAXATION)
    keep = jnp.where(mask, 0.0, 1.0 - RELAXATION)
    bounce = jnp.logical_and(solid, jnp.logical_not(mask))
    post = [None] * 19
    post[0] = jnp.where(bounce, h[0], scale * base + (shift + keep * h[0]))
    for i in range(1, 19, 2):
        c = along[i]
        even = base + 4.5 * (c * c)
        odd = 3.0 * c
        post[i] = jnp.where(bounce, h[i + 1], scale * (even + odd) + (shift + keep * h[i]))
        post[i + 1] = jnp.where(bounce, h[i], scale * (even - odd) + (shift + keep * h[i + 1]))
    return post


def off_diagonals(live, res, cross):
    rows = [[None] * 4 for _ in range(4)]
    sides = [[None] * 4 for _ in range(4)]
    zero = jnp.zeros_like(live[0])
    for k in range(4):
        for l in range(4):
            if k == l:
                rows[k][l] = res[k]
                sides[k][l] = live[k]
            else:
                rows[k][l] = live[k] * live[l] * (0.5 * (cross[k][l] + cross[l][k]))
                sides[k][l] = zero
    for c in range(4):
        inverse = 1.0 / rows[c][c]
        for r in range(c + 1, 4):
            factor = rows[r][c] * inverse
            for l in range(c + 1, 4):
                rows[r][l] = rows[r][l] - factor * rows[c][l]
            for l in range(c + 1):
                sides[r][l] = sides[r][l] - factor * sides[c][l]
    answer = [None] * 4
    for r in reversed(range(4)):
        inverse = 1.0 / rows[r][r]
        answer[r] = []
        for l in range(4):
            running = sides[r][l]
            for c in range(r + 1, 4):
                running = running - rows[r][c] * answer[c][l]
            answer[r].append(running * inverse)
    ones = [answer[k][0] + answer[k][1] + answer[k][2] + answer[k][3] for k in range(4)]
    total = 1.0 / (live[0] * ones[0] + live[1] * ones[1] + live[2] * ones[2] + live[3] * ones[3])
    pairs = []
    for a in range(4):
        for b in range(a + 1, 4):
            pairs.append(live[a] * live[b] * (answer[a][b] - ones[a] * ones[b] * total))
    return pairs


def split2(x):
    high = x.astype(BF16)
    return high, (x - high.astype(F32)).astype(BF16)


def split3(x):
    high = x.astype(BF16)
    rest = x - high.astype(F32)
    middle = rest.astype(BF16)
    return high, middle, (rest - middle.astype(F32)).astype(BF16)


def kernel(
    nb,
    ns,
    pop_hbm,
    solid_hbm,
    bp_hbm,
    col_hbm,
    dest_hbm,
    seg_hbm,
    segp_hbm,
    rate_hbm,
    leak_hbm,
    w_hbm,
    mem_hbm,
    arity_hbm,
    res_hbm,
    cross_hbm,
    pop_out,
    seg_out,
    bp_out,
    pop_ref,
    solid_ref,
    bp_ref,
    col_ref,
    dest_ref,
    seg_ref,
    segp_ref,
    w_ref,
    mem_ref,
    arity_ref,
    res_ref,
    cross_ref,
    load_s,
    post,
    mask_ref,
    imposed_ref,
    sxu,
    sxd,
    syu,
    syd,
    sc,
    rxu,
    rxd,
    ryu,
    ryd,
    rc,
    ptab,
    stage,
    rates,
    inflow_all,
    flow,
    other_mem,
    gbuf,
    row_at,
    oh_c,
    oh_r,
    part,
    msg,
    arrived,
    pick,
    labels,
    last,
    w_parts,
    ret_out,
    ret_in,
    halo_s,
    halo_r,
    first_s,
    first_r,
    rates_s,
    rates_r,
    inflow_s,
    inflow_r,
    pair_s,
    pair_r,
    part_s,
    part_r,
    msg_s,
    msg_r,
    ret_s,
    ret_r,
):
    ny = ns // 2
    rows = segp_ref.shape[0]
    junctions = mem_ref.shape[1]
    links = 4 * junctions
    blocks = col_ref.shape[1]
    cells_x, cells_y, cells_z = solid_ref.shape
    b, s = lax.axis_index("brick"), lax.axis_index("sub")
    hi, y = s // ny, lax.rem(s, ny)
    partner = (b, (1 - hi) * ny + y)
    lead, late = hi == 0, hi != 0

    def at(db, ds):
        return (lax.rem(b + db + nb, nb), lax.rem(s + ds + ns, ns))

    def ring(k):
        return (b, lax.rem(y + k, ny))

    def copy(src, dst, send, recv, device):
        return pltpu.make_async_remote_copy(
            src_ref=src, dst_ref=dst, send_sem=send, recv_sem=recv, device_id=device, device_id_type=MESH
        )

    barrier = pltpu.get_barrier_semaphore()

    def greet(k, carry):
        pl.semaphore_signal(barrier, inc=1, device_id=at(k, 0), device_id_type=MESH)
        return carry

    lax.fori_loop(1, nb, greet, 0)
    for k in range(1, ns):
        pl.semaphore_signal(barrier, inc=1, device_id=at(0, k), device_id_type=MESH)
    for _, cx, cy in CORNERS:
        pl.semaphore_signal(barrier, inc=1, device_id=at(cx, cy), device_id_type=MESH)

    @pl.when(late)
    def _():
        def greet_lead(k, carry):
            pl.semaphore_signal(barrier, inc=1, device_id=(lax.rem(b + k, nb), y), device_id_type=MESH)
            return carry

        lax.fori_loop(1, nb, greet_lead, 0)

    loads = [
        pltpu.make_async_copy(src, dst, load_s.at[n])
        for n, (src, dst) in enumerate(
            [
                (pop_hbm, pop_ref),
                (solid_hbm, solid_ref),
                (bp_hbm, bp_ref),
                (col_hbm, col_ref),
                (dest_hbm, dest_ref),
                (seg_hbm, seg_ref),
                (segp_hbm, segp_ref),
                (rate_hbm, stage.at[0]),
                (leak_hbm, stage.at[1]),
                (w_hbm, w_ref),
                (mem_hbm, mem_ref),
                (arity_hbm, arity_ref),
                (res_hbm, res_ref),
                (cross_hbm, cross_ref),
            ]
        )
    ]
    for n in (11, 12, 13, 4, 5, 3, 2, 0, 10, 6, 7, 8, 1, 9):
        loads[n].start()

    def halo(parity):
        copies = [
            (sxu, rxu, (1, 0)),
            (sxd, rxd, (-1, 0)),
            (syu, ryu, (0, 1)),
            (syd, ryd, (0, -1)),
        ]
        out = [
            copy(src, dst.at[parity], halo_s.at[n], halo_r.at[parity, n], at(*to))
            for n, (src, dst, to) in enumerate(copies)
        ]
        for n, (_, cx, cy) in enumerate(CORNERS):
            out.append(
                copy(sc.at[n], rc.at[parity, n], halo_s.at[4 + n], halo_r.at[parity, 4 + n], at(cx, cy))
            )
        return out

    def start_halo(parity):
        copies = halo(parity)
        for n in (2, 3, 4, 5, 6, 7, 0, 1):
            copies[n].start()

    halves = cells_y // 8

    def collide(source):
        def tile(n, carry):
            x, first_row = n // halves, pl.multiple_of(lax.rem(n, halves) * 8, 8)
            span = pl.ds(first_row, 8)
            h = [source[i, x, span, :] for i in range(19)]
            out = collide_sites(
                h, solid_ref[x, span, :] > 0, mask_ref[x, span, :] > 0.5, imposed_ref[x, span, :]
            )
            for i in range(19):
                post[i, x, span, :] = out[i]
            return carry

        lax.fori_loop(0, cells_x * halves, tile, 0)

    def pack():
        for n, i in enumerate(Y_UP):
            for x in range(cells_x):
                syu[n, x : x + 1, :] = post[i, x, cells_y - 1 : cells_y, :]
        for n, i in enumerate(Y_DOWN):
            for x in range(cells_x):
                syd[n, x : x + 1, :] = post[i, x, 0:1, :]
        for n, (i, cx, cy) in enumerate(CORNERS):
            x = cells_x - 1 if cx > 0 else 0
            row = cells_y - 1 if cy > 0 else 0
            sc[n] = jnp.broadcast_to(post[i, x, row : row + 1, :], (8, cells_z))
        for n, i in enumerate(X_UP):
            sxu[n] = post[i, cells_x - 1]
        for n, i in enumerate(X_DOWN):
            sxd[n] = post[i, 0]

    def stream(parity):
        edge = iota((cells_y, cells_z), 0)
        for i, (cx, cy, cz) in enumerate(VELOCITIES):
            for x in range(cells_x):
                xs = x - cx
                inside = 0 <= xs < cells_x
                if inside:
                    value = post[i, xs]
                elif cx > 0:
                    value = rxu[parity, X_UP.index(i)]
                else:
                    value = rxd[parity, X_DOWN.index(i)]
                if cy:
                    if not inside:
                        n = [c[0] for c in CORNERS].index(i)
                        row = rc[parity, n, 0:1, :]
                    elif cy > 0:
                        row = ryu[parity, Y_UP.index(i), xs : xs + 1, :]
                    else:
                        row = ryd[parity, Y_DOWN.index(i), xs : xs + 1, :]
                    value = pltpu.roll(value, cy % cells_y, 0)
                    value = jnp.where(edge == (0 if cy > 0 else cells_y - 1), row, value)
                if cz:
                    value = pltpu.roll(value, cz % cells_z, 1)
                pop_out[i, x] = value

    def build(n, ref):
        m = jnp.concatenate([ref[k : k + 1, :] for k in range(4)], axis=1)
        row = m >> 7
        row_at[n] = row
        lines = iota((128, links), 0)
        oh_c[n] = jnp.where(lines == (m & 127), 1.0, 0.0).astype(BF16)
        oh_r[n] = jnp.where(iota((ns * rows, links), 0) == row, 1.0, 0.0).astype(BF16)

    columns = cells_x * cells_y

    def hit():
        return iota((columns, blocks), 0) == col_ref[...]

    def prepare_junctions():
        for n in (11, 12, 13):
            loads[n].wait()
        live = [jnp.where(arity_ref[...] > k, 1.0, 0.0) for k in range(4)]
        pairs = off_diagonals(
            live,
            [res_ref[k : k + 1, :] for k in range(4)],
            [[cross_ref[k, l : l + 1, :] for l in range(4)] for k in range(4)],
        )
        for n, value in enumerate(pairs):
            gbuf[0, n : n + 1, :] = value
        gbuf[0, 6:8, :] = jnp.zeros((2, junctions), F32)

    def prepare_lattice():
        for n in (1, 2):
            loads[n].wait()
        hits = hit()
        found = jnp.sum(jnp.where(hits, 1.0, 0.0), axis=1, keepdims=True)
        pressed = jnp.sum(jnp.where(hits, bp_ref[...], 0.0), axis=1, keepdims=True)
        mask_ref[...] = jnp.broadcast_to(found, (columns, cells_z)).reshape(cells_x, cells_y, cells_z)
        imposed_ref[...] = jnp.broadcast_to(1.0 + DENSITY_SCALE * pressed, (columns, cells_z)).reshape(
            cells_x, cells_y, cells_z
        )
        collide(pop_ref)
        pack()

    def prepare_messages():
        for n in (3, 4, 5, 0):
            loads[n].wait()
        dest = dest_ref[...]
        eye = iota((blocks, blocks), 0) == iota((blocks, blocks), 1)
        dest_column = jnp.sum(jnp.where(eye, dest, 0), axis=1, keepdims=True)
        earlier = jnp.logical_and(dest_column == dest, iota((blocks, blocks), 0) < iota((blocks, blocks), 1))
        slot = jnp.sum(jnp.where(earlier, 1, 0), axis=0, keepdims=True)
        slot_column = jnp.sum(jnp.where(eye, slot, 0), axis=1, keepdims=True)
        number_column = jnp.sum(jnp.where(eye, seg_ref[...] + 1, 0), axis=1, keepdims=True)
        r = iota((nb * 4, blocks), 0)
        aimed = (r >> 2) == dest
        chosen = jnp.where(jnp.logical_and(aimed, (r & 3) == slot), 1.0, 0.0)
        pick[...] = chosen
        hits = hit()
        selector = lax.dot_general(
            chosen.astype(BF16),
            jnp.where(hits, 1.0, 0.0).astype(BF16),
            (((1,), (1,)), ((), ())),
            preferred_element_type=F32,
        ).astype(BF16)
        axial = jnp.zeros((columns, cells_z), F32)
        for i, c in enumerate(VELOCITIES):
            if c[0]:
                weight = c[0] * (1.0 / 18.0 if i < 7 else 1.0 / 36.0)
                axial = axial + weight * pop_ref[i].reshape(columns, cells_z)
        profiles = jnp.dot(
            jnp.concatenate([selector] * 3, axis=1),
            jnp.concatenate(split3(axial), axis=0),
            preferred_element_type=F32,
        )
        number = jnp.where(iota((blocks, cells_z), 1) == slot_column, number_column, 0)
        numbers = jnp.dot(
            jnp.concatenate([jnp.where(aimed, 1.0, 0.0).astype(BF16)] * 2, axis=1),
            jnp.concatenate([(number >> 6).astype(F32) * 64.0, (number & 63).astype(F32)], axis=0).astype(BF16),
            preferred_element_type=F32,
        )
        is_label = (iota((nb * 4, cells_z), 0) & 3) == 3
        msg[...] = jnp.where(is_label, numbers - 1.0, profiles).reshape(nb, 4, cells_z)

    def prepare_network():
        for n in (6, 7, 8, 10):
            loads[n].wait()

        @pl.when(lead)
        def _():
            build(0, mem_ref)

        loads[9].wait()
        high, low = split2(w_ref[...])
        w_parts[:, 0:cells_z] = high
        w_parts[:, cells_z : 2 * cells_z] = low
        w_parts[:, 2 * cells_z : 3 * cells_z] = high

    def spread(src, dst, send, recv):
        near = [copy(src, dst, send.at[k], recv.at[k], ring(k)) for k in range(1, ny)]
        far = [copy(src, dst, send.at[k], recv.at[ny + k], ring(k)) for k in range(ny)]
        return near, far

    pair = [
        copy(mem_hbm, other_mem, pair_s.at[0], pair_r.at[0], partner),
        copy(gbuf.at[0], gbuf.at[1], pair_s.at[1], pair_r.at[1], partner),
        copy(labels.at[0], labels.at[1], pair_s.at[2], pair_r.at[2], partner),
        copy(ptab.at[ny + y], last, pair_s.at[3], pair_r.at[3], partner),
    ]
    first = spread(segp_hbm, ptab.at[s], first_s, first_r)
    second = spread(stage, rates.at[s], rates_s, rates_r)
    third = spread(flow, inflow_all.at[s], inflow_s, inflow_r)

    def message(k):
        target = lax.rem(b + k, nb)
        return copy(msg.at[target], arrived.at[b], msg_s, msg_r, (target, s))

    def answer(k, n):
        target = lax.rem(b + k, nb)
        return copy(ret_out.at[n, target], ret_in.at[b], ret_s.at[n], ret_r, (target, n * ny + y))

    def start_message(k, carry):
        message(lax.rem(k + nb // 4, nb - 1) + 1).start()
        return carry

    @pl.when(lead)
    def _():
        prepare_messages()
        prepare_junctions()
        prepare_lattice()
        prepare_network()
        ptab[s] = segp_ref[...]
        rates[s] = stage[...]

    pl.semaphore_wait(barrier, nb - 1 + ns - 1 + len(CORNERS) + jnp.where(lead, nb - 1, 0))

    @pl.when(late)
    def _():
        pair[0].start()
        for c in first[1]:
            c.start()
        prepare_junctions()
        pair[1].start()
        prepare_messages()

    lax.fori_loop(1, nb, start_message, 0)
    arrived[b] = msg[b]

    @pl.when(lead)
    def _():
        for c in first[0]:
            c.start()

    @pl.when(late)
    def _():
        prepare_lattice()

    start_halo(0)

    @pl.when(lead)
    def _():
        for c in second[0]:
            c.start()

    @pl.when(late)
    def _():
        prepare_network()
        for c in second[1]:
            c.start()

    def flows(n, table):
        members = oh_c[n]
        found = jnp.dot(table, jnp.concatenate([members, members], axis=0), preferred_element_type=F32)
        q = jnp.sum(jnp.where(iota((ns * rows, links), 0) == row_at[n], found, 0.0), axis=0, keepdims=True)
        q = [q[:, k * junctions : (k + 1) * junctions] for k in range(4)]
        f = [None] * 4
        count = 0
        for k in range(4):
            for l in range(k + 1, 4):
                term = gbuf[n, count : count + 1, :] * (q[l] - q[k])
                f[k] = term if f[k] is None else f[k] + term
                f[l] = -term if f[l] is None else f[l] - term
                count += 1
        high, low = split2(jnp.concatenate(f, axis=1))
        return lax.dot_general(
            oh_r[n],
            jnp.concatenate([members * high, members * low], axis=0),
            (((1,), (1,)), ((), ())),
            preferred_element_type=F32,
        )

    def numbers_of(n):
        rows_of = jnp.broadcast_to(labels[n], (nb, 4, 128)).reshape(nb * 4, 128)
        at_row = iota((nb * 4, 128), 0) & 3
        number = jnp.sum(jnp.where(iota((nb * 4, 128), 1) == at_row, rows_of, 0.0), axis=1, keepdims=True)
        return jnp.where(at_row < SLOTS, jnp.broadcast_to(number.astype(jnp.int32), (nb * 4, 128)), -1)

    def inflows():
        whole = pl.ds(0, nb - 1)
        copy(msg.at[whole], arrived.at[whole], msg_s, msg_r, at(1, 0)).wait()
        got = arrived[...].reshape(nb * 4, cells_z)
        labels[0] = arrived[:, 3:4, :]
        numbers = numbers_of(0)
        lane = iota((nb * 4, 128), 1)
        high, low = split2(got)
        value = lax.dot_general(
            jnp.concatenate([high, high, low], axis=1),
            w_parts[...],
            (((1,), (1,)), ((), ())),
            preferred_element_type=F32,
        )
        for n in range(rows):
            mine = jnp.where(numbers == lane + n * 128, value[:, n * 128 : (n + 1) * 128], 0.0)
            flow[n : n + 1, :] = jnp.sum(mine, axis=0, keepdims=True)

        @pl.when(lead)
        def _():
            for c in third[0]:
                c.start()
            inflow_all[s] = flow[...]

        @pl.when(late)
        def _():
            for c in third[1]:
                c.start()
            pair[2].start()

    def table_of():
        return jnp.concatenate(split2(ptab[...].reshape(ns * rows, 128)), axis=1)

    def joined(both):
        return both[:, :128] + both[:, 128:]

    def arrive(copies):
        for c in copies[0]:
            c.wait()
        for c in copies[1]:
            c.wait_recv()

    @pl.when(lead)
    def _():
        arrive(first)
        table = table_of()
        both = flows(0, table)
        pair[0].wait_recv()
        build(1, other_mem)
        pair[1].wait_recv()
        both = both + flows(1, table)
        part[0, y] = joined(both)

    def step(t, carry):
        parity = lax.rem(t, 2)
        partial = [
            copy(part.at[parity, y], part.at[parity, y], part_s.at[k - 1], part_r.at[parity, k - 1], ring(k))
            for k in range(1, ny)
        ]

        @pl.when(lead)
        def _():
            for c in partial:
                c.start()

        @pl.when(t == 0)
        def _():
            inflows()

        now = halo(parity)
        for c in now:
            c.wait_recv()
        stream(parity)
        for c in now:
            c.wait_send()

        @pl.when(t < STEPS - 1)
        def _():
            collide(pop_out)
            pack()
            start_halo(1 - parity)

        @pl.when(lead)
        def _():
            for c in partial:
                c.wait()

            @pl.when(t == 0)
            def _():
                arrive(second)
                arrive(third)

            balance = part[parity, 0]
            for k in range(1, ny):
                balance = balance + part[parity, k]
            p = ptab[...].reshape(ns * rows, 128)
            rate = rates[:, 0].reshape(ns * rows, 128)
            leak = rates[:, 1].reshape(ns * rows, 128)
            source = inflow_all[...].reshape(ns * rows, 128)
            ptab[...] = (p + rate * (source - balance - leak * p)).reshape(ns, rows, 128)

            @pl.when(t < STEPS - 1)
            def _():
                table = table_of()
                part[1 - parity, y] = joined(flows(0, table) + flows(1, table))

        return carry

    lax.fori_loop(0, STEPS, step, 0)

    whole = pl.ds(0, nb - 1)

    @pl.when(lead)
    def _():
        pair[3].start()
        pair[2].wait_recv()
        lane = iota((nb * 4, 128), 1)
        for n in (1, 0):
            final = ptab[n * ny + y]
            numbers = numbers_of(n)
            value = jnp.zeros((nb * 4, 128), F32)
            for line in range(rows):
                value = value + jnp.where(numbers == lane + line * 128, final[line : line + 1, :], 0.0)
            value = jnp.sum(value, axis=1, keepdims=True)
            ret_out[n] = jnp.broadcast_to(value, (nb * 4, 128)).reshape(nb, 4, 128)

            def start_answer(k, carry):
                answer(lax.rem(k + nb // 4, nb - 1) + 1, n).start()
                return carry

            lax.fori_loop(1, nb, start_answer, 0)
        answer(0, 1).start()
        ret_in[b] = ret_out[0, b]
        seg_out[...] = ptab[y]
        copy(ret_out.at[0, whole], ret_in.at[whole], ret_s.at[0], ret_r, at(1, 0)).wait()
        copy(ret_out.at[1], ret_in, ret_s.at[1], ret_r, at(1, 0)).wait_send()
        pair[3].wait_send()

    @pl.when(late)
    def _():
        for copies in (first, second, third):
            for c in copies[1]:
                c.wait_send()
        for c in pair[:3]:
            c.wait_send()
        pair[3].wait_recv()
        seg_out[...] = last[...]
        copy(ret_out.at[1], ret_in, ret_s.at[1], ret_r, at(1, 0)).wait_recv()

    back = ret_in[...].reshape(nb * 4, 128)[:, :blocks]
    bp_out[...] = jnp.sum(jnp.where(pick[...] > 0.5, back, 0.0), axis=0, keepdims=True)


def finish(pop_in, seg_in, bp_in, pop_out, seg_out, bp_out, sems):
    copies = [pltpu.make_async_copy(pop_in.at[i], pop_out.at[i], sems.at[i]) for i in range(pop_in.shape[0])]
    copies.append(pltpu.make_async_copy(seg_in, seg_out, sems.at[len(copies)]))
    copies.append(pltpu.make_async_copy(bp_in, bp_out, sems.at[len(copies)]))
    for c in copies:
        c.start()
    for c in copies:
        c.wait()


def local(
    populations,
    solid,
    boundary_pressure,
    block_col,
    block_dest,
    block_seg,
    seg_pressure,
    seg_rate,
    seg_leak,
    profile_weights,
    junc_members,
    junc_arity,
    junc_res,
    junc_cross,
):
    nb, ns = lax.axis_size("brick"), lax.axis_size("sub")
    ny = ns // 2
    _, cx, cy, cz = populations.shape
    segs, blocks, junctions = seg_pressure.shape[0], block_col.shape[0], junc_arity.shape[0]
    rows, links = segs // 128, 4 * junctions
    vmem, dma = pltpu.VMEM, pltpu.SemaphoreType.DMA
    scratch = [
        vmem((19, cx, cy, cz), F32),
        vmem((cx, cy, cz), jnp.int32),
        vmem((1, blocks), F32),
        vmem((1, blocks), jnp.int32),
        vmem((1, blocks), jnp.int32),
        vmem((1, blocks), jnp.int32),
        vmem((rows, 128), F32),
        vmem((segs, cz), F32),
        vmem((4, junctions), jnp.int32),
        vmem((1, junctions), jnp.int32),
        vmem((4, junctions), F32),
        vmem((4, 4, junctions), F32),
        dma((14,)),
        vmem((19, cx, cy, cz), F32),
        vmem((cx, cy, cz), F32),
        vmem((cx, cy, cz), F32),
        vmem((5, cy, cz), F32),
        vmem((5, cy, cz), F32),
        vmem((5, cx, cz), F32),
        vmem((5, cx, cz), F32),
        vmem((4, 8, cz), F32),
        vmem((2, 5, cy, cz), F32),
        vmem((2, 5, cy, cz), F32),
        vmem((2, 5, cx, cz), F32),
        vmem((2, 5, cx, cz), F32),
        vmem((2, 4, 8, cz), F32),
        vmem((ns, rows, 128), F32),
        vmem((2, rows, 128), F32),
        vmem((ns, 2, rows, 128), F32),
        vmem((ns, rows, 128), F32),
        vmem((rows, 128), F32),
        vmem((4, junctions), jnp.int32),
        vmem((2, 8, junctions), F32),
        vmem((2, 1, links), jnp.int32),
        vmem((2, 128, links), BF16),
        vmem((2, ns * rows, links), BF16),
        vmem((2, ny, ns * rows, 128), F32),
        vmem((nb, 4, cz), F32),
        vmem((nb, 4, cz), F32),
        vmem((nb * 4, blocks), F32),
        vmem((2, nb, 1, 128), F32),
        vmem((rows, 128), F32),
        vmem((segs, 3 * cz), BF16),
        vmem((2, nb, 4, 128), F32),
        vmem((nb, 4, 128), F32),
        dma((8,)),
        dma((2, 8)),
        dma((ny,)),
        dma((ns,)),
        dma((ny,)),
        dma((ns,)),
        dma((ny,)),
        dma((ns,)),
        dma((4,)),
        dma((4,)),
        dma((ny - 1,)),
        dma((2, ny - 1)),
        dma,
        dma,
        dma((2,)),
        dma,
    ]
    spec = pl.BlockSpec(memory_space=vmem)
    lattice, pressure, back = pl.pallas_call(
        functools.partial(kernel, nb, ns),
        out_shape=(
            pltpu.VMEM(populations.shape, F32),
            pltpu.VMEM((rows, 128), F32),
            pltpu.VMEM((1, blocks), F32),
        ),
        in_specs=[pl.BlockSpec(memory_space=pltpu.HBM)] * 14,
        out_specs=(spec, spec, spec),
        scratch_shapes=scratch,
        compiler_params=pltpu.CompilerParams(
            collective_id=0, has_side_effects=True, vmem_limit_bytes=56 * 2**20
        ),
        name="coupled",
    )(
        populations,
        solid,
        boundary_pressure.reshape(1, blocks),
        block_col.reshape(1, blocks),
        block_dest.reshape(1, blocks),
        block_seg.reshape(1, blocks),
        seg_pressure.reshape(rows, 128),
        seg_rate.reshape(rows, 128),
        seg_leak.reshape(rows, 128),
        profile_weights,
        junc_members,
        junc_arity.reshape(1, junctions),
        junc_res,
        junc_cross,
    )
    hbm = pl.BlockSpec(memory_space=pltpu.HBM)
    lattice, pressure, back = pl.pallas_call(
        finish,
        out_shape=(
            jax.ShapeDtypeStruct(populations.shape, F32),
            jax.ShapeDtypeStruct((rows, 128), F32),
            jax.ShapeDtypeStruct((1, blocks), F32),
        ),
        in_specs=[spec] * 3,
        out_specs=(hbm, hbm, hbm),
        scratch_shapes=[
            dma((21,)),
        ],
        compiler_params=pltpu.CompilerParams(vmem_limit_bytes=2**20),
        name="finish",
    )(lattice, pressure, back)
    return lattice, pressure.reshape(segs), back.reshape(blocks)


def solution(mesh):
    return jax.shard_map(
        local,
        mesh=mesh,
        in_specs=(
            P(None, "brick", "sub", None),
            P("brick", "sub", None),
            P(("brick", "sub")),
            P(("brick", "sub")),
            P(("brick", "sub"), None),
            P(("brick", "sub")),
            P(("brick", "sub")),
            P(("brick", "sub")),
            P(("brick", "sub")),
            P(("brick", "sub"), None),
            P(None, ("brick", "sub")),
            P(("brick", "sub")),
            P(None, ("brick", "sub")),
            P(None, None, ("brick", "sub")),
        ),
        out_specs=(P(None, "brick", "sub", None), P(("brick", "sub")), P(("brick", "sub"))),
        check_vma=False,
    )
```

```python
import functools

import jax
import jax.numpy as jnp
import numpy as np
from jax import lax
from jax.experimental import pallas as pl
from jax.experimental.pallas import tpu as pltpu
from jax.sharding import PartitionSpec as P

STEPS = 6
SLOTS = 3
MESH = pl.DeviceIdType.MESH
F32 = jnp.float32
BF16 = jnp.bfloat16
HIGHEST = lax.Precision.HIGHEST

VELOCITIES = [
    (0, 0, 0),
    (1, 0, 0),
    (-1, 0, 0),
    (0, 1, 0),
    (0, -1, 0),
    (0, 0, 1),
    (0, 0, -1),
    (1, 1, 0),
    (-1, -1, 0),
    (1, -1, 0),
    (-1, 1, 0),
    (1, 0, 1),
    (-1, 0, -1),
    (1, 0, -1),
    (-1, 0, 1),
    (0, 1, 1),
    (0, -1, -1),
    (0, 1, -1),
    (0, -1, 1),
]
OPPOSITE = [0, 2, 1, 4, 3, 6, 5, 8, 7, 10, 9, 12, 11, 14, 13, 16, 15, 18, 17]
RELAXATION = 1.25
DENSITY_SCALE = 0.1
X_UP = [i for i, c in enumerate(VELOCITIES) if c[0] == 1]
X_DOWN = [i for i, c in enumerate(VELOCITIES) if c[0] == -1]
Y_UP = [i for i, c in enumerate(VELOCITIES) if c[1] == 1]
Y_DOWN = [i for i, c in enumerate(VELOCITIES) if c[1] == -1]
CORNERS = [(7, 1, 1), (8, -1, -1), (9, 1, -1), (10, -1, 1)]


def iota(shape, axis):
    return lax.broadcasted_iota(jnp.int32, shape, axis)


def collide_sites(h, solid, mask, imposed):
    w0, w1, w2 = 1.0 / 3.0, 1.0 / 18.0, 1.0 / 36.0
    plus = {i: h[i] + h[i + 1] for i in range(1, 19, 2)}
    minus = {i: h[i] - h[i + 1] for i in range(1, 19, 2)}
    near = plus[1] + plus[3] + plus[5]
    far = (plus[7] + plus[9]) + (plus[11] + plus[13]) + (plus[15] + plus[17])
    density = 1.0 + (w0 * h[0] + w1 * near + w2 * far)
    inverse = 1.0 / density
    ux = (w1 * minus[1] + w2 * ((minus[7] + minus[9]) + (minus[11] + minus[13]))) * inverse
    uy = (w1 * minus[3] + w2 * ((minus[7] - minus[9]) + (minus[15] + minus[17]))) * inverse
    uz = (w1 * minus[5] + w2 * ((minus[11] - minus[13]) + (minus[15] - minus[17]))) * inverse
    base = 1.0 - 1.5 * (ux * ux + uy * uy + uz * uz)
    along = {1: ux, 3: uy, 5: uz, 7: ux + uy, 9: ux - uy, 11: ux + uz, 13: ux - uz, 15: uy + uz, 17: uy - uz}
    scale = jnp.where(mask, imposed, RELAXATION * density)
    shift = jnp.where(mask, -1.0, -RELAXATION)
    keep = jnp.where(mask, 0.0, 1.0 - RELAXATION)
    bounce = jnp.logical_and(solid, jnp.logical_not(mask))
    post = [None] * 19
    post[0] = jnp.where(bounce, h[0], scale * base + (shift + keep * h[0]))
    for i in range(1, 19, 2):
        c = along[i]
        even = base + 4.5 * (c * c)
        odd = 3.0 * c
        post[i] = jnp.where(bounce, h[i + 1], scale * (even + odd) + (shift + keep * h[i]))
        post[i + 1] = jnp.where(bounce, h[i], scale * (even - odd) + (shift + keep * h[i + 1]))
    return post


def off_diagonals(live, res, cross):
    rows = [[None] * 4 for _ in range(4)]
    sides = [[None] * 4 for _ in range(4)]
    zero = jnp.zeros_like(live[0])
    for k in range(4):
        for l in range(4):
            if k == l:
                rows[k][l] = res[k]
                sides[k][l] = live[k]
            else:
                rows[k][l] = live[k] * live[l] * (0.5 * (cross[k][l] + cross[l][k]))
                sides[k][l] = zero
    for c in range(4):
        inverse = 1.0 / rows[c][c]
        for r in range(c + 1, 4):
            factor = rows[r][c] * inverse
            for l in range(c + 1, 4):
                rows[r][l] = rows[r][l] - factor * rows[c][l]
            for l in range(c + 1):
                sides[r][l] = sides[r][l] - factor * sides[c][l]
    answer = [None] * 4
    for r in reversed(range(4)):
        inverse = 1.0 / rows[r][r]
        answer[r] = []
        for l in range(4):
            running = sides[r][l]
            for c in range(r + 1, 4):
                running = running - rows[r][c] * answer[c][l]
            answer[r].append(running * inverse)
    ones = [answer[k][0] + answer[k][1] + answer[k][2] + answer[k][3] for k in range(4)]
    total = 1.0 / (live[0] * ones[0] + live[1] * ones[1] + live[2] * ones[2] + live[3] * ones[3])
    pairs = []
    for a in range(4):
        for b in range(a + 1, 4):
            pairs.append(live[a] * live[b] * (answer[a][b] - ones[a] * ones[b] * total))
    return pairs


def split2(x):
    high = x.astype(BF16)
    return high, (x - high.astype(F32)).astype(BF16)


def split3(x):
    high = x.astype(BF16)
    rest = x - high.astype(F32)
    middle = rest.astype(BF16)
    return high, middle, (rest - middle.astype(F32)).astype(BF16)


def kernel(
    nb,
    ns,
    pop_hbm,
    solid_hbm,
    bp_hbm,
    col_hbm,
    dest_hbm,
    seg_hbm,
    segp_hbm,
    rate_hbm,
    leak_hbm,
    w_hbm,
    mem_hbm,
    arity_hbm,
    res_hbm,
    cross_hbm,
    pop_out,
    seg_out,
    bp_out,
    pop_ref,
    solid_ref,
    bp_ref,
    col_ref,
    dest_ref,
    seg_ref,
    segp_ref,
    w_ref,
    mem_ref,
    arity_ref,
    res_ref,
    cross_ref,
    load_s,
    post,
    mask_ref,
    imposed_ref,
    sxu,
    sxd,
    syu,
    syd,
    sc,
    rxu,
    rxd,
    ryu,
    ryd,
    rc,
    ptab,
    stage,
    rates,
    inflow_all,
    flow,
    other_mem,
    gbuf,
    row_at,
    oh_c,
    oh_r,
    part,
    msg,
    arrived,
    pick,
    labels,
    numbers_ref,
    last,
    w_parts,
    ret_out,
    ret_in,
    halo_s,
    halo_r,
    first_s,
    first_r,
    rates_s,
    rates_r,
    inflow_s,
    inflow_r,
    pair_s,
    pair_r,
    part_s,
    part_r,
    msg_s,
    msg_r,
    ret_s,
    ret_r,
):
    ny = ns // 2
    rows = segp_ref.shape[0]
    junctions = mem_ref.shape[1]
    links = 4 * junctions
    blocks = col_ref.shape[1]
    cells_x, cells_y, cells_z = solid_ref.shape
    b, s = lax.axis_index("brick"), lax.axis_index("sub")
    hi, y = s // ny, s & (ny - 1)
    partner = (b, (1 - hi) * ny + y)
    lead, late = hi == 0, hi != 0

    def at(db, ds):
        return ((b + db) & (nb - 1), (s + ds) & (ns - 1))

    def ring(k):
        return (b, (y + k) & (ny - 1))

    def copy(src, dst, send, recv, device):
        return pltpu.make_async_remote_copy(
            src_ref=src, dst_ref=dst, send_sem=send, recv_sem=recv, device_id=device, device_id_type=MESH
        )

    loads = [
        pltpu.make_async_copy(src, dst, load_s.at[n])
        for n, (src, dst) in enumerate(
            [
                (pop_hbm, pop_ref),
                (solid_hbm, solid_ref),
                (bp_hbm, bp_ref),
                (col_hbm, col_ref),
                (dest_hbm, dest_ref),
                (seg_hbm, seg_ref),
                (segp_hbm, segp_ref),
                (rate_hbm, stage.at[0]),
                (leak_hbm, stage.at[1]),
                (w_hbm, w_ref),
                (mem_hbm, mem_ref),
                (arity_hbm, arity_ref),
                (res_hbm, res_ref),
                (cross_hbm, cross_ref),
            ]
        )
    ]
    for n in (11, 12, 13, 4, 5, 3, 2, 0, 10, 6, 7, 8, 1, 9):
        loads[n].start()

    barrier = pltpu.get_barrier_semaphore()

    for k in range(1, nb):
        pl.semaphore_signal(barrier, inc=1, device_id=at(k, 0), device_id_type=MESH)
    for k in range(1, ns):
        pl.semaphore_signal(barrier, inc=1, device_id=at(0, k), device_id_type=MESH)
    for _, cx, cy in CORNERS:
        pl.semaphore_signal(barrier, inc=1, device_id=at(cx, cy), device_id_type=MESH)

    @pl.when(late)
    def _():
        for k in range(1, nb):
            pl.semaphore_signal(barrier, inc=1, device_id=(at(k, 0)[0], y), device_id_type=MESH)


    def halo(parity):
        copies = [
            (sxu, rxu, (1, 0)),
            (sxd, rxd, (-1, 0)),
            (syu, ryu, (0, 1)),
            (syd, ryd, (0, -1)),
        ]
        out = [
            copy(src, dst.at[parity], halo_s.at[n], halo_r.at[parity, n], at(*to))
            for n, (src, dst, to) in enumerate(copies)
        ]
        for n, (_, cx, cy) in enumerate(CORNERS):
            out.append(
                copy(sc.at[n], rc.at[parity, n], halo_s.at[4 + n], halo_r.at[parity, 4 + n], at(cx, cy))
            )
        return out

    def start_halo(parity):
        copies = halo(parity)
        for n in (2, 3, 4, 5, 6, 7, 0, 1):
            copies[n].start()

    halves = cells_y // 8

    def collide(source):
        def tile(n, carry):
            x, first_row = n // halves, pl.multiple_of(lax.rem(n, halves) * 8, 8)
            span = pl.ds(first_row, 8)
            h = [source[i, x, span, :] for i in range(19)]
            out = collide_sites(
                h, solid_ref[x, span, :] > 0, mask_ref[x, span, :] > 0.5, imposed_ref[x, span, :]
            )
            for i in range(19):
                post[i, x, span, :] = out[i]
            return carry

        lax.fori_loop(0, cells_x * halves, tile, 0)

    def pack():
        for n, i in enumerate(Y_UP):
            for x in range(cells_x):
                syu[n, x : x + 1, :] = post[i, x, cells_y - 1 : cells_y, :]
        for n, i in enumerate(Y_DOWN):
            for x in range(cells_x):
                syd[n, x : x + 1, :] = post[i, x, 0:1, :]
        for n, (i, cx, cy) in enumerate(CORNERS):
            x = cells_x - 1 if cx > 0 else 0
            row = cells_y - 1 if cy > 0 else 0
            sc[n] = jnp.broadcast_to(post[i, x, row : row + 1, :], (8, cells_z))
        for n, i in enumerate(X_UP):
            sxu[n] = post[i, cells_x - 1]
        for n, i in enumerate(X_DOWN):
            sxd[n] = post[i, 0]

    def stream(parity):
        edge = iota((cells_y, cells_z), 0)
        for i, (cx, cy, cz) in enumerate(VELOCITIES):
            for x in range(cells_x):
                xs = x - cx
                inside = 0 <= xs < cells_x
                if inside:
                    value = post[i, xs]
                elif cx > 0:
                    value = rxu[parity, X_UP.index(i)]
                else:
                    value = rxd[parity, X_DOWN.index(i)]
                if cy:
                    if not inside:
                        n = [c[0] for c in CORNERS].index(i)
                        row = rc[parity, n, 0:1, :]
                    elif cy > 0:
                        row = ryu[parity, Y_UP.index(i), xs : xs + 1, :]
                    else:
                        row = ryd[parity, Y_DOWN.index(i), xs : xs + 1, :]
                    value = pltpu.roll(value, cy % cells_y, 0)
                    value = jnp.where(edge == (0 if cy > 0 else cells_y - 1), row, value)
                if cz:
                    value = pltpu.roll(value, cz % cells_z, 1)
                pop_out[i, x] = value

    def build(n, ref):
        m = jnp.concatenate([ref[k : k + 1, :] for k in range(4)], axis=1)
        row = m >> 7
        row_at[n] = row
        lines = iota((128, links), 0)
        oh_c[n] = jnp.where(lines == (m & 127), 1.0, 0.0).astype(BF16)
        oh_r[n] = jnp.where(iota((ns * rows, links), 0) == row, 1.0, 0.0).astype(BF16)

    columns = cells_x * cells_y

    def hit():
        return iota((columns, blocks), 0) == col_ref[...]

    def prepare_junctions():
        for n in (11, 12, 13):
            loads[n].wait()
        live = [jnp.where(arity_ref[...] > k, 1.0, 0.0) for k in range(4)]
        pairs = off_diagonals(
            live,
            [res_ref[k : k + 1, :] for k in range(4)],
            [[cross_ref[k, l : l + 1, :] for l in range(4)] for k in range(4)],
        )
        for n, value in enumerate(pairs):
            gbuf[0, n : n + 1, :] = value
        gbuf[0, 6:8, :] = jnp.zeros((2, junctions), F32)

    def prepare_lattice():
        for n in (1, 2):
            loads[n].wait()
        hits = hit()
        found = jnp.sum(jnp.where(hits, 1.0, 0.0), axis=1, keepdims=True)
        pressed = jnp.sum(jnp.where(hits, bp_ref[...], 0.0), axis=1, keepdims=True)
        mask_ref[...] = jnp.broadcast_to(found, (columns, cells_z)).reshape(cells_x, cells_y, cells_z)
        imposed_ref[...] = jnp.broadcast_to(1.0 + DENSITY_SCALE * pressed, (columns, cells_z)).reshape(
            cells_x, cells_y, cells_z
        )
        collide(pop_ref)
        pack()

    def prepare_messages():
        for n in (3, 4, 5, 0):
            loads[n].wait()
        dest = dest_ref[...]
        eye = iota((blocks, blocks), 0) == iota((blocks, blocks), 1)
        dest_column = jnp.sum(jnp.where(eye, dest, 0), axis=1, keepdims=True)
        earlier = jnp.logical_and(dest_column == dest, iota((blocks, blocks), 0) < iota((blocks, blocks), 1))
        slot = jnp.sum(jnp.where(earlier, 1, 0), axis=0, keepdims=True)
        slot_column = jnp.sum(jnp.where(eye, slot, 0), axis=1, keepdims=True)
        number_column = jnp.sum(jnp.where(eye, seg_ref[...] + 1, 0), axis=1, keepdims=True)
        r = iota((nb * 4, blocks), 0)
        aimed = (r >> 2) == dest
        chosen = jnp.where(jnp.logical_and(aimed, (r & 3) == slot), 1.0, 0.0)
        pick[...] = chosen
        hits = hit()
        selector = lax.dot_general(
            chosen.astype(BF16),
            jnp.where(hits, 1.0, 0.0).astype(BF16),
            (((1,), (1,)), ((), ())),
            preferred_element_type=F32,
        ).astype(BF16)
        axial = jnp.zeros((columns, cells_z), F32)
        for i, c in enumerate(VELOCITIES):
            if c[0]:
                weight = c[0] * (1.0 / 18.0 if i < 7 else 1.0 / 36.0)
                axial = axial + weight * pop_ref[i].reshape(columns, cells_z)
        profiles = jnp.dot(
            jnp.concatenate([selector] * 3, axis=1),
            jnp.concatenate(split3(axial), axis=0),
            preferred_element_type=F32,
        )
        number = jnp.where(iota((blocks, cells_z), 1) == slot_column, number_column, 0)
        numbers = jnp.dot(
            jnp.concatenate([jnp.where(aimed, 1.0, 0.0).astype(BF16)] * 2, axis=1),
            jnp.concatenate([(number >> 6).astype(F32) * 64.0, (number & 63).astype(F32)], axis=0).astype(BF16),
            preferred_element_type=F32,
        )
        is_label = (iota((nb * 4, cells_z), 0) & 3) == 3
        msg[...] = jnp.where(is_label, numbers - 1.0, profiles).reshape(nb, 4, cells_z)

    def prepare_network():
        for n in (6, 7, 8, 10):
            loads[n].wait()

        @pl.when(lead)
        def _():
            build(0, mem_ref)

        loads[9].wait()
        high, low = split2(w_ref[...])
        w_parts[:, 0:cells_z] = high
        w_parts[:, cells_z : 2 * cells_z] = low
        w_parts[:, 2 * cells_z : 3 * cells_z] = high

    def spread(src, dst, send, recv):
        near = [copy(src, dst, send.at[k], recv.at[k], ring(k)) for k in range(1, ny)]
        far = [copy(src, dst, send.at[k], recv.at[ny + k], ring(k)) for k in range(ny)]
        return near, far

    pair = [
        copy(mem_hbm, other_mem, pair_s.at[0], pair_r.at[0], partner),
        copy(gbuf.at[0], gbuf.at[1], pair_s.at[1], pair_r.at[1], partner),
        copy(labels.at[0], labels.at[1], pair_s.at[2], pair_r.at[2], partner),
        copy(ptab.at[ny + y], last, pair_s.at[3], pair_r.at[3], partner),
    ]
    first = spread(segp_hbm, ptab.at[s], first_s, first_r)
    second = spread(stage, rates.at[s], rates_s, rates_r)
    third = spread(flow, inflow_all.at[s], inflow_s, inflow_r)

    def message(k):
        target = (b + k) & (nb - 1)
        return copy(msg.at[target], arrived.at[b], msg_s, msg_r, (target, s))

    def answer(k, n):
        target = (b + k) & (nb - 1)
        return copy(ret_out.at[n, target], ret_in.at[b], ret_s.at[n], ret_r, (target, n * ny + y))

    order = [(k + nb // 4) % (nb - 1) + 1 for k in range(1, nb)]

    @pl.when(lead)
    def _():
        prepare_messages()
        prepare_junctions()
        prepare_lattice()
        prepare_network()
        ptab[s] = segp_ref[...]
        rates[s] = stage[...]

    pl.semaphore_wait(barrier, nb - 1 + ns - 1 + len(CORNERS) + jnp.where(lead, nb - 1, 0))

    @pl.when(late)
    def _():
        pair[0].start()
        for c in first[1]:
            c.start()
        prepare_junctions()
        pair[1].start()
        prepare_messages()

    for k in order:
        message(k).start()
    arrived[b] = msg[b]

    @pl.when(lead)
    def _():
        for c in first[0]:
            c.start()

    @pl.when(late)
    def _():
        prepare_lattice()

    start_halo(0)

    @pl.when(lead)
    def _():
        for c in second[0]:
            c.start()

    @pl.when(late)
    def _():
        prepare_network()
        for c in second[1]:
            c.start()

    def flows(n, table):
        members = oh_c[n]
        found = jnp.dot(table, jnp.concatenate([members, members], axis=0), preferred_element_type=F32)
        q = jnp.sum(jnp.where(iota((ns * rows, links), 0) == row_at[n], found, 0.0), axis=0, keepdims=True)
        q = [q[:, k * junctions : (k + 1) * junctions] for k in range(4)]
        f = [None] * 4
        count = 0
        for k in range(4):
            for l in range(k + 1, 4):
                term = gbuf[n, count : count + 1, :] * (q[l] - q[k])
                f[k] = term if f[k] is None else f[k] + term
                f[l] = -term if f[l] is None else f[l] - term
                count += 1
        high, low = split2(jnp.concatenate(f, axis=1))
        return lax.dot_general(
            oh_r[n],
            jnp.concatenate([members * high, members * low], axis=0),
            (((1,), (1,)), ((), ())),
            preferred_element_type=F32,
        )

    def numbers_of(n):
        rows_of = jnp.broadcast_to(labels[n], (nb, 4, 128)).reshape(nb * 4, 128)
        at_row = iota((nb * 4, 128), 0) & 3
        number = jnp.sum(jnp.where(iota((nb * 4, 128), 1) == at_row, rows_of, 0.0), axis=1, keepdims=True)
        return jnp.where(at_row < SLOTS, jnp.broadcast_to(number.astype(jnp.int32), (nb * 4, 128)), -1)

    def inflows():
        whole = pl.ds(0, nb - 1)
        copy(msg.at[whole], arrived.at[whole], msg_s, msg_r, at(1, 0)).wait()
        got = arrived[...].reshape(nb * 4, cells_z)
        labels[0] = arrived[:, 3:4, :]
        numbers = numbers_of(0)
        numbers_ref[0] = numbers
        lane = iota((nb * 4, 128), 1)
        high, low = split2(got)
        value = lax.dot_general(
            jnp.concatenate([high, high, low], axis=1),
            w_parts[...],
            (((1,), (1,)), ((), ())),
            preferred_element_type=F32,
        )
        for n in range(rows):
            mine = jnp.where(numbers == lane + n * 128, value[:, n * 128 : (n + 1) * 128], 0.0)
            flow[n : n + 1, :] = jnp.sum(mine, axis=0, keepdims=True)

        @pl.when(lead)
        def _():
            for c in third[0]:
                c.start()
            inflow_all[s] = flow[...]

        @pl.when(late)
        def _():
            for c in third[1]:
                c.start()
            pair[2].start()

    def table_of():
        return jnp.concatenate(split2(ptab[...].reshape(ns * rows, 128)), axis=1)

    def joined(both):
        return both[:, :128] + both[:, 128:]

    def arrive(copies):
        for c in copies[0]:
            c.wait()
        for c in copies[1]:
            c.wait_recv()

    @pl.when(lead)
    def _():
        arrive(first)
        table = table_of()
        both = flows(0, table)
        pair[0].wait_recv()
        build(1, other_mem)
        pair[1].wait_recv()
        both = both + flows(1, table)
        part[0, y] = joined(both)

    def step(t, carry):
        parity = lax.rem(t, 2)
        partial = [
            copy(part.at[parity, y], part.at[parity, y], part_s.at[k - 1], part_r.at[parity, k - 1], ring(k))
            for k in range(1, ny)
        ]

        @pl.when(lead)
        def _():
            for c in partial:
                c.start()

        @pl.when(t == 0)
        def _():
            inflows()

        now = halo(parity)
        for c in now:
            c.wait_recv()
        stream(parity)
        for c in now:
            c.wait_send()

        @pl.when(t < STEPS - 1)
        def _():
            collide(pop_out)
            pack()
            start_halo(1 - parity)

        @pl.when(jnp.logical_and(lead, t == 1))
        def _():
            pair[2].wait_recv()
            numbers_ref[1] = numbers_of(1)

        @pl.when(lead)
        def _():
            for c in partial:
                c.wait()

            @pl.when(t == 0)
            def _():
                arrive(second)
                arrive(third)

            balance = part[parity, 0]
            for k in range(1, ny):
                balance = balance + part[parity, k]
            p = ptab[...].reshape(ns * rows, 128)
            rate = rates[:, 0].reshape(ns * rows, 128)
            leak = rates[:, 1].reshape(ns * rows, 128)
            source = inflow_all[...].reshape(ns * rows, 128)
            ptab[...] = (p + rate * (source - balance - leak * p)).reshape(ns, rows, 128)

            @pl.when(t < STEPS - 1)
            def _():
                table = table_of()
                part[1 - parity, y] = joined(flows(0, table) + flows(1, table))

        return carry

    lax.fori_loop(0, STEPS, step, 0)

    whole = pl.ds(0, nb - 1)

    @pl.when(lead)
    def _():
        pair[3].start()
        lane = iota((nb * 4, 128), 1)
        for n in (1, 0):
            final = ptab[n * ny + y]
            numbers = numbers_ref[n]
            value = jnp.zeros((nb * 4, 128), F32)
            for line in range(rows):
                value = value + jnp.where(numbers == lane + line * 128, final[line : line + 1, :], 0.0)
            value = jnp.sum(value, axis=1, keepdims=True)
            ret_out[n] = jnp.broadcast_to(value, (nb * 4, 128)).reshape(nb, 4, 128)

            for k in order:
                answer(k, n).start()
        answer(0, 1).start()
        ret_in[b] = ret_out[0, b]
        seg_out[...] = ptab[y]
        copy(ret_out.at[0, whole], ret_in.at[whole], ret_s.at[0], ret_r, at(1, 0)).wait()
        copy(ret_out.at[1], ret_in, ret_s.at[1], ret_r, at(1, 0)).wait_send()
        pair[3].wait_send()

    @pl.when(late)
    def _():
        for copies in (first, second, third):
            for c in copies[1]:
                c.wait_send()
        for c in pair[:3]:
            c.wait_send()
        pair[3].wait_recv()
        seg_out[...] = last[...]
        copy(ret_out.at[1], ret_in, ret_s.at[1], ret_r, at(1, 0)).wait_recv()

    back = ret_in[...].reshape(nb * 4, 128)[:, :blocks]
    bp_out[...] = jnp.sum(jnp.where(pick[...] > 0.5, back, 0.0), axis=0, keepdims=True)


def finish(pop_in, seg_in, bp_in, pop_out, seg_out, bp_out, sems):
    copies = [pltpu.make_async_copy(pop_in.at[i], pop_out.at[i], sems.at[i]) for i in range(pop_in.shape[0])]
    copies.append(pltpu.make_async_copy(seg_in, seg_out, sems.at[len(copies)]))
    copies.append(pltpu.make_async_copy(bp_in, bp_out, sems.at[len(copies)]))
    for c in copies:
        c.start()
    for c in copies:
        c.wait()


def local(
    populations,
    solid,
    boundary_pressure,
    block_col,
    block_dest,
    block_seg,
    seg_pressure,
    seg_rate,
    seg_leak,
    profile_weights,
    junc_members,
    junc_arity,
    junc_res,
    junc_cross,
):
    nb, ns = lax.axis_size("brick"), lax.axis_size("sub")
    ny = ns // 2
    _, cx, cy, cz = populations.shape
    segs, blocks, junctions = seg_pressure.shape[0], block_col.shape[0], junc_arity.shape[0]
    rows, links = segs // 128, 4 * junctions
    vmem, dma = pltpu.VMEM, pltpu.SemaphoreType.DMA
    scratch = [
        vmem((19, cx, cy, cz), F32),
        vmem((cx, cy, cz), jnp.int32),
        vmem((1, blocks), F32),
        vmem((1, blocks), jnp.int32),
        vmem((1, blocks), jnp.int32),
        vmem((1, blocks), jnp.int32),
        vmem((rows, 128), F32),
        vmem((segs, cz), F32),
        vmem((4, junctions), jnp.int32),
        vmem((1, junctions), jnp.int32),
        vmem((4, junctions), F32),
        vmem((4, 4, junctions), F32),
        dma((14,)),
        vmem((19, cx, cy, cz), F32),
        vmem((cx, cy, cz), F32),
        vmem((cx, cy, cz), F32),
        vmem((5, cy, cz), F32),
        vmem((5, cy, cz), F32),
        vmem((5, cx, cz), F32),
        vmem((5, cx, cz), F32),
        vmem((4, 8, cz), F32),
        vmem((2, 5, cy, cz), F32),
        vmem((2, 5, cy, cz), F32),
        vmem((2, 5, cx, cz), F32),
        vmem((2, 5, cx, cz), F32),
        vmem((2, 4, 8, cz), F32),
        vmem((ns, rows, 128), F32),
        vmem((2, rows, 128), F32),
        vmem((ns, 2, rows, 128), F32),
        vmem((ns, rows, 128), F32),
        vmem((rows, 128), F32),
        vmem((4, junctions), jnp.int32),
        vmem((2, 8, junctions), F32),
        vmem((2, 1, links), jnp.int32),
        vmem((2, 128, links), BF16),
        vmem((2, ns * rows, links), BF16),
        vmem((2, ny, ns * rows, 128), F32),
        vmem((nb, 4, cz), F32),
        vmem((nb, 4, cz), F32),
        vmem((nb * 4, blocks), F32),
        vmem((2, nb, 1, 128), F32),
        vmem((2, nb * 4, 128), jnp.int32),
        vmem((rows, 128), F32),
        vmem((segs, 3 * cz), BF16),
        vmem((2, nb, 4, 128), F32),
        vmem((nb, 4, 128), F32),
        dma((8,)),
        dma((2, 8)),
        dma((ny,)),
        dma((ns,)),
        dma((ny,)),
        dma((ns,)),
        dma((ny,)),
        dma((ns,)),
        dma((4,)),
        dma((4,)),
        dma((ny - 1,)),
        dma((2, ny - 1)),
        dma,
        dma,
        dma((2,)),
        dma,
    ]
    spec = pl.BlockSpec(memory_space=vmem)
    lattice, pressure, back = pl.pallas_call(
        functools.partial(kernel, nb, ns),
        out_shape=(
            pltpu.VMEM(populations.shape, F32),
            pltpu.VMEM((rows, 128), F32),
            pltpu.VMEM((1, blocks), F32),
        ),
        in_specs=[pl.BlockSpec(memory_space=pltpu.HBM)] * 14,
        out_specs=(spec, spec, spec),
        scratch_shapes=scratch,
        compiler_params=pltpu.CompilerParams(
            collective_id=0, has_side_effects=True, vmem_limit_bytes=56 * 2**20
        ),
        name="coupled",
    )(
        populations,
        solid,
        boundary_pressure.reshape(1, blocks),
        block_col.reshape(1, blocks),
        block_dest.reshape(1, blocks),
        block_seg.reshape(1, blocks),
        seg_pressure.reshape(rows, 128),
        seg_rate.reshape(rows, 128),
        seg_leak.reshape(rows, 128),
        profile_weights,
        junc_members,
        junc_arity.reshape(1, junctions),
        junc_res,
        junc_cross,
    )
    hbm = pl.BlockSpec(memory_space=pltpu.HBM)
    lattice, pressure, back = pl.pallas_call(
        finish,
        out_shape=(
            jax.ShapeDtypeStruct(populations.shape, F32),
            jax.ShapeDtypeStruct((rows, 128), F32),
            jax.ShapeDtypeStruct((1, blocks), F32),
        ),
        in_specs=[spec] * 3,
        out_specs=(hbm, hbm, hbm),
        scratch_shapes=[
            dma((21,)),
        ],
        compiler_params=pltpu.CompilerParams(vmem_limit_bytes=2**20),
        name="finish",
    )(lattice, pressure, back)
    return lattice, pressure.reshape(segs), back.reshape(blocks)


def solution(mesh):
    return jax.shard_map(
        local,
        mesh=mesh,
        in_specs=(
            P(None, "brick", "sub", None),
            P("brick", "sub", None),
            P(("brick", "sub")),
            P(("brick", "sub")),
            P(("brick", "sub"), None),
            P(("brick", "sub")),
            P(("brick", "sub")),
            P(("brick", "sub")),
            P(("brick", "sub")),
            P(("brick", "sub"), None),
            P(None, ("brick", "sub")),
            P(("brick", "sub")),
            P(None, ("brick", "sub")),
            P(None, None, ("brick", "sub")),
        ),
        out_specs=(P(None, "brick", "sub", None), P(("brick", "sub")), P(("brick", "sub"))),
        check_vma=False,
    )
```

```python
import functools

import jax
import jax.numpy as jnp
import numpy as np
from jax import lax
from jax.experimental import pallas as pl
from jax.experimental.pallas import tpu as pltpu
from jax.sharding import PartitionSpec as P

STEPS = 6
SLOTS = 3
MESH = pl.DeviceIdType.MESH
F32 = jnp.float32
BF16 = jnp.bfloat16
HIGHEST = lax.Precision.HIGHEST

VELOCITIES = [
    (0, 0, 0),
    (1, 0, 0),
    (-1, 0, 0),
    (0, 1, 0),
    (0, -1, 0),
    (0, 0, 1),
    (0, 0, -1),
    (1, 1, 0),
    (-1, -1, 0),
    (1, -1, 0),
    (-1, 1, 0),
    (1, 0, 1),
    (-1, 0, -1),
    (1, 0, -1),
    (-1, 0, 1),
    (0, 1, 1),
    (0, -1, -1),
    (0, 1, -1),
    (0, -1, 1),
]
OPPOSITE = [0, 2, 1, 4, 3, 6, 5, 8, 7, 10, 9, 12, 11, 14, 13, 16, 15, 18, 17]
RELAXATION = 1.25
DENSITY_SCALE = 0.1
X_UP = [i for i, c in enumerate(VELOCITIES) if c[0] == 1]
X_DOWN = [i for i, c in enumerate(VELOCITIES) if c[0] == -1]
Y_UP = [i for i, c in enumerate(VELOCITIES) if c[1] == 1]
Y_DOWN = [i for i, c in enumerate(VELOCITIES) if c[1] == -1]
CORNERS = [(7, 1, 1), (8, -1, -1), (9, 1, -1), (10, -1, 1)]


def iota(shape, axis):
    return lax.broadcasted_iota(jnp.int32, shape, axis)


def collide_sites(h, solid, mask, imposed):
    w0, w1, w2 = 1.0 / 3.0, 1.0 / 18.0, 1.0 / 36.0
    plus = {i: h[i] + h[i + 1] for i in range(1, 19, 2)}
    minus = {i: h[i] - h[i + 1] for i in range(1, 19, 2)}
    near = plus[1] + plus[3] + plus[5]
    far = (plus[7] + plus[9]) + (plus[11] + plus[13]) + (plus[15] + plus[17])
    density = 1.0 + (w0 * h[0] + w1 * near + w2 * far)
    inverse = 1.0 / density
    ux = (w1 * minus[1] + w2 * ((minus[7] + minus[9]) + (minus[11] + minus[13]))) * inverse
    uy = (w1 * minus[3] + w2 * ((minus[7] - minus[9]) + (minus[15] + minus[17]))) * inverse
    uz = (w1 * minus[5] + w2 * ((minus[11] - minus[13]) + (minus[15] - minus[17]))) * inverse
    base = 1.0 - 1.5 * (ux * ux + uy * uy + uz * uz)
    along = {1: ux, 3: uy, 5: uz, 7: ux + uy, 9: ux - uy, 11: ux + uz, 13: ux - uz, 15: uy + uz, 17: uy - uz}
    scale = jnp.where(mask, imposed, RELAXATION * density)
    shift = jnp.where(mask, -1.0, -RELAXATION)
    keep = jnp.where(mask, 0.0, 1.0 - RELAXATION)
    bounce = jnp.logical_and(solid, jnp.logical_not(mask))
    post = [None] * 19
    post[0] = jnp.where(bounce, h[0], scale * base + (shift + keep * h[0]))
    for i in range(1, 19, 2):
        c = along[i]
        even = base + 4.5 * (c * c)
        odd = 3.0 * c
        post[i] = jnp.where(bounce, h[i + 1], scale * (even + odd) + (shift + keep * h[i]))
        post[i + 1] = jnp.where(bounce, h[i], scale * (even - odd) + (shift + keep * h[i + 1]))
    return post


def off_diagonals(live, res, cross):
    rows = [[None] * 4 for _ in range(4)]
    sides = [[None] * 4 for _ in range(4)]
    zero = jnp.zeros_like(live[0])
    for k in range(4):
        for l in range(4):
            if k == l:
                rows[k][l] = res[k]
                sides[k][l] = live[k]
            else:
                rows[k][l] = live[k] * live[l] * (0.5 * (cross[k][l] + cross[l][k]))
                sides[k][l] = zero
    for c in range(4):
        inverse = 1.0 / rows[c][c]
        for r in range(c + 1, 4):
            factor = rows[r][c] * inverse
            for l in range(c + 1, 4):
                rows[r][l] = rows[r][l] - factor * rows[c][l]
            for l in range(c + 1):
                sides[r][l] = sides[r][l] - factor * sides[c][l]
    answer = [None] * 4
    for r in reversed(range(4)):
        inverse = 1.0 / rows[r][r]
        answer[r] = []
        for l in range(4):
            running = sides[r][l]
            for c in range(r + 1, 4):
                running = running - rows[r][c] * answer[c][l]
            answer[r].append(running * inverse)
    ones = [answer[k][0] + answer[k][1] + answer[k][2] + answer[k][3] for k in range(4)]
    total = 1.0 / (live[0] * ones[0] + live[1] * ones[1] + live[2] * ones[2] + live[3] * ones[3])
    pairs = []
    for a in range(4):
        for b in range(a + 1, 4):
            pairs.append(live[a] * live[b] * (answer[a][b] - ones[a] * ones[b] * total))
    return pairs


def split2(x):
    high = x.astype(BF16)
    return high, (x - high.astype(F32)).astype(BF16)


def split3(x):
    high = x.astype(BF16)
    rest = x - high.astype(F32)
    middle = rest.astype(BF16)
    return high, middle, (rest - middle.astype(F32)).astype(BF16)


def kernel(
    nb,
    ns,
    pop_hbm,
    solid_hbm,
    bp_hbm,
    col_hbm,
    dest_hbm,
    seg_hbm,
    segp_hbm,
    rate_hbm,
    leak_hbm,
    w_hbm,
    mem_hbm,
    arity_hbm,
    res_hbm,
    cross_hbm,
    pop_out,
    seg_out,
    bp_out,
    pop_ref,
    solid_ref,
    bp_ref,
    col_ref,
    dest_ref,
    seg_ref,
    segp_ref,
    w_ref,
    mem_ref,
    arity_ref,
    res_ref,
    cross_ref,
    load_s,
    post,
    mask_ref,
    imposed_ref,
    sxu,
    sxd,
    syu,
    syd,
    sc,
    rxu,
    rxd,
    ryu,
    ryd,
    rc,
    ptab,
    stage,
    rates,
    inflow_all,
    flow,
    other_mem,
    gbuf,
    row_at,
    oh_c,
    oh_r,
    part,
    msg,
    arrived,
    pick,
    labels,
    numbers_ref,
    last,
    w_parts,
    ret_out,
    ret_in,
    halo_s,
    halo_r,
    first_s,
    first_r,
    rates_s,
    rates_r,
    inflow_s,
    inflow_r,
    pair_s,
    pair_r,
    part_s,
    part_r,
    tail_s,
    tail_r,
    msg_s,
    msg_r,
    ret_s,
    ret_r,
):
    ny = ns // 2
    rows = segp_ref.shape[0]
    junctions = mem_ref.shape[1]
    links = 4 * junctions
    blocks = col_ref.shape[1]
    cells_x, cells_y, cells_z = solid_ref.shape
    b, s = lax.axis_index("brick"), lax.axis_index("sub")
    hi, y = s // ny, s & (ny - 1)
    partner = (b, (1 - hi) * ny + y)
    lead, late = hi == 0, hi != 0

    def at(db, ds):
        return ((b + db) & (nb - 1), (s + ds) & (ns - 1))

    def ring(k):
        return (b, (y + k) & (ny - 1))

    def copy(src, dst, send, recv, device):
        return pltpu.make_async_remote_copy(
            src_ref=src, dst_ref=dst, send_sem=send, recv_sem=recv, device_id=device, device_id_type=MESH
        )

    loads = [
        pltpu.make_async_copy(src, dst, load_s.at[n])
        for n, (src, dst) in enumerate(
            [
                (pop_hbm, pop_ref),
                (solid_hbm, solid_ref),
                (bp_hbm, bp_ref),
                (col_hbm, col_ref),
                (dest_hbm, dest_ref),
                (seg_hbm, seg_ref),
                (segp_hbm, segp_ref),
                (rate_hbm, stage.at[0]),
                (leak_hbm, stage.at[1]),
                (w_hbm, w_ref),
                (mem_hbm, mem_ref),
                (arity_hbm, arity_ref),
                (res_hbm, res_ref),
                (cross_hbm, cross_ref),
            ]
        )
    ]
    for n in (11, 12, 13, 4, 5, 3, 2, 0, 10, 6, 7, 8, 1, 9):
        loads[n].start()

    barrier = pltpu.get_barrier_semaphore()

    for k in range(1, nb):
        pl.semaphore_signal(barrier, inc=1, device_id=at(k, 0), device_id_type=MESH)
    for k in range(1, ns):
        pl.semaphore_signal(barrier, inc=1, device_id=at(0, k), device_id_type=MESH)
    for _, cx, cy in CORNERS:
        pl.semaphore_signal(barrier, inc=1, device_id=at(cx, cy), device_id_type=MESH)

    @pl.when(late)
    def _():
        for k in range(1, nb):
            pl.semaphore_signal(barrier, inc=1, device_id=(at(k, 0)[0], y), device_id_type=MESH)


    def halo(parity):
        copies = [
            (sxu, rxu, (1, 0)),
            (sxd, rxd, (-1, 0)),
            (syu, ryu, (0, 1)),
            (syd, ryd, (0, -1)),
        ]
        out = [
            copy(src, dst.at[parity], halo_s.at[n], halo_r.at[parity, n], at(*to))
            for n, (src, dst, to) in enumerate(copies)
        ]
        for n, (_, cx, cy) in enumerate(CORNERS):
            out.append(
                copy(sc.at[n], rc.at[parity, n], halo_s.at[4 + n], halo_r.at[parity, 4 + n], at(cx, cy))
            )
        return out

    def start_halo(parity):
        copies = halo(parity)
        for n in (2, 3, 4, 5, 6, 7, 0, 1):
            copies[n].start()

    halves = cells_y // 8

    def collide(source):
        def tile(n, carry):
            x, first_row = n // halves, pl.multiple_of(lax.rem(n, halves) * 8, 8)
            span = pl.ds(first_row, 8)
            h = [source[i, x, span, :] for i in range(19)]
            out = collide_sites(
                h, solid_ref[x, span, :] > 0, mask_ref[x, span, :] > 0.5, imposed_ref[x, span, :]
            )
            for i in range(19):
                post[i, x, span, :] = out[i]
            return carry

        lax.fori_loop(0, cells_x * halves, tile, 0)

    def pack():
        for n, i in enumerate(Y_UP):
            for x in range(cells_x):
                syu[n, x : x + 1, :] = post[i, x, cells_y - 1 : cells_y, :]
        for n, i in enumerate(Y_DOWN):
            for x in range(cells_x):
                syd[n, x : x + 1, :] = post[i, x, 0:1, :]
        for n, (i, cx, cy) in enumerate(CORNERS):
            x = cells_x - 1 if cx > 0 else 0
            row = cells_y - 1 if cy > 0 else 0
            sc[n] = jnp.broadcast_to(post[i, x, row : row + 1, :], (8, cells_z))
        for n, i in enumerate(X_UP):
            sxu[n] = post[i, cells_x - 1]
        for n, i in enumerate(X_DOWN):
            sxd[n] = post[i, 0]

    def stream(parity):
        edge = iota((cells_y, cells_z), 0)
        for i, (cx, cy, cz) in enumerate(VELOCITIES):
            for x in range(cells_x):
                xs = x - cx
                inside = 0 <= xs < cells_x
                if inside:
                    value = post[i, xs]
                elif cx > 0:
                    value = rxu[parity, X_UP.index(i)]
                else:
                    value = rxd[parity, X_DOWN.index(i)]
                if cy:
                    if not inside:
                        n = [c[0] for c in CORNERS].index(i)
                        row = rc[parity, n, 0:1, :]
                    elif cy > 0:
                        row = ryu[parity, Y_UP.index(i), xs : xs + 1, :]
                    else:
                        row = ryd[parity, Y_DOWN.index(i), xs : xs + 1, :]
                    value = pltpu.roll(value, cy % cells_y, 0)
                    value = jnp.where(edge == (0 if cy > 0 else cells_y - 1), row, value)
                if cz:
                    value = pltpu.roll(value, cz % cells_z, 1)
                pop_out[i, x] = value

    def build(n, ref):
        m = jnp.concatenate([ref[k : k + 1, :] for k in range(4)], axis=1)
        row = m >> 7
        row_at[n] = row
        lines = iota((128, links), 0)
        oh_c[n] = jnp.where(lines == (m & 127), 1.0, 0.0).astype(BF16)
        oh_r[n] = jnp.where(iota((ns * rows, links), 0) == row, 1.0, 0.0).astype(BF16)

    columns = cells_x * cells_y

    def hit():
        return iota((columns, blocks), 0) == col_ref[...]

    def prepare_junctions():
        for n in (11, 12, 13):
            loads[n].wait()
        live = [jnp.where(arity_ref[...] > k, 1.0, 0.0) for k in range(4)]
        pairs = off_diagonals(
            live,
            [res_ref[k : k + 1, :] for k in range(4)],
            [[cross_ref[k, l : l + 1, :] for l in range(4)] for k in range(4)],
        )
        for n, value in enumerate(pairs):
            gbuf[0, n : n + 1, :] = value
        gbuf[0, 6:8, :] = jnp.zeros((2, junctions), F32)

    def prepare_lattice():
        for n in (1, 2):
            loads[n].wait()
        hits = hit()
        found = jnp.sum(jnp.where(hits, 1.0, 0.0), axis=1, keepdims=True)
        pressed = jnp.sum(jnp.where(hits, bp_ref[...], 0.0), axis=1, keepdims=True)
        mask_ref[...] = jnp.broadcast_to(found, (columns, cells_z)).reshape(cells_x, cells_y, cells_z)
        imposed_ref[...] = jnp.broadcast_to(1.0 + DENSITY_SCALE * pressed, (columns, cells_z)).reshape(
            cells_x, cells_y, cells_z
        )
        collide(pop_ref)
        pack()

    def prepare_messages():
        for n in (3, 4, 5, 0):
            loads[n].wait()
        dest = dest_ref[...]
        eye = iota((blocks, blocks), 0) == iota((blocks, blocks), 1)
        dest_column = jnp.sum(jnp.where(eye, dest, 0), axis=1, keepdims=True)
        earlier = jnp.logical_and(dest_column == dest, iota((blocks, blocks), 0) < iota((blocks, blocks), 1))
        slot = jnp.sum(jnp.where(earlier, 1, 0), axis=0, keepdims=True)
        slot_column = jnp.sum(jnp.where(eye, slot, 0), axis=1, keepdims=True)
        number_column = jnp.sum(jnp.where(eye, seg_ref[...] + 1, 0), axis=1, keepdims=True)
        r = iota((nb * 4, blocks), 0)
        aimed = (r >> 2) == dest
        chosen = jnp.where(jnp.logical_and(aimed, (r & 3) == slot), 1.0, 0.0)
        pick[...] = chosen
        hits = hit()
        selector = lax.dot_general(
            chosen.astype(BF16),
            jnp.where(hits, 1.0, 0.0).astype(BF16),
            (((1,), (1,)), ((), ())),
            preferred_element_type=F32,
        ).astype(BF16)
        axial = jnp.zeros((columns, cells_z), F32)
        for i, c in enumerate(VELOCITIES):
            if c[0]:
                weight = c[0] * (1.0 / 18.0 if i < 7 else 1.0 / 36.0)
                axial = axial + weight * pop_ref[i].reshape(columns, cells_z)
        profiles = jnp.dot(
            jnp.concatenate([selector] * 3, axis=1),
            jnp.concatenate(split3(axial), axis=0),
            preferred_element_type=F32,
        )
        number = jnp.where(iota((blocks, cells_z), 1) == slot_column, number_column, 0)
        numbers = jnp.dot(
            jnp.concatenate([jnp.where(aimed, 1.0, 0.0).astype(BF16)] * 2, axis=1),
            jnp.concatenate([(number >> 6).astype(F32) * 64.0, (number & 63).astype(F32)], axis=0).astype(BF16),
            preferred_element_type=F32,
        )
        is_label = (iota((nb * 4, cells_z), 0) & 3) == 3
        msg[...] = jnp.where(is_label, numbers - 1.0, profiles).reshape(nb, 4, cells_z)

    def prepare_network():
        for n in (6, 7, 8, 10):
            loads[n].wait()

        @pl.when(lead)
        def _():
            build(0, mem_ref)

        loads[9].wait()
        high, low = split2(w_ref[...])
        w_parts[:, 0:cells_z] = high
        w_parts[:, cells_z : 2 * cells_z] = low
        w_parts[:, 2 * cells_z : 3 * cells_z] = high

    def spread(src, dst, send, recv):
        near = [copy(src, dst, send.at[k], recv.at[k], ring(k)) for k in range(1, ny)]
        far = [copy(src, dst, send.at[k], recv.at[ny + k], ring(k)) for k in range(ny)]
        return near, far

    pair = [
        copy(mem_hbm, other_mem, pair_s.at[0], pair_r.at[0], partner),
        copy(gbuf.at[0], gbuf.at[1], pair_s.at[1], pair_r.at[1], partner),
        copy(labels.at[0], labels.at[1], pair_s.at[2], pair_r.at[2], partner),
        copy(ptab.at[ny + y], last, pair_s.at[3], pair_r.at[3], partner),
    ]
    first = spread(segp_hbm, ptab.at[s], first_s, first_r)
    second = spread(stage, rates.at[s], rates_s, rates_r)
    third = spread(flow, inflow_all.at[s], inflow_s, inflow_r)

    def message(k):
        target = (b + k) & (nb - 1)
        return copy(msg.at[target], arrived.at[b], msg_s, msg_r, (target, s))

    def answer(k, n):
        target = (b + k) & (nb - 1)
        return copy(ret_out.at[n, target], ret_in.at[b], ret_s.at[n], ret_r, (target, n * ny + y))

    order = [(k + nb // 4) % (nb - 1) + 1 for k in range(1, nb)]

    @pl.when(lead)
    def _():
        prepare_messages()
        prepare_junctions()
        prepare_lattice()
        prepare_network()
        ptab[s] = segp_ref[...]
        rates[s] = stage[...]

    pl.semaphore_wait(barrier, nb - 1 + ns - 1 + len(CORNERS) + jnp.where(lead, nb - 1, 0))

    @pl.when(late)
    def _():
        pair[0].start()
        for c in first[1]:
            c.start()
        prepare_junctions()
        pair[1].start()
        prepare_messages()

    for k in order:
        message(k).start()
    arrived[b] = msg[b]

    @pl.when(lead)
    def _():
        for c in first[0]:
            c.start()

    @pl.when(late)
    def _():
        prepare_lattice()

    start_halo(0)

    @pl.when(lead)
    def _():
        for c in second[0]:
            c.start()

    @pl.when(late)
    def _():
        prepare_network()
        for c in second[1]:
            c.start()

    def flows(n, table):
        members = oh_c[n]
        found = jnp.dot(table, jnp.concatenate([members, members], axis=0), preferred_element_type=F32)
        q = jnp.sum(jnp.where(iota((ns * rows, links), 0) == row_at[n], found, 0.0), axis=0, keepdims=True)
        q = [q[:, k * junctions : (k + 1) * junctions] for k in range(4)]
        f = [None] * 4
        count = 0
        for k in range(4):
            for l in range(k + 1, 4):
                term = gbuf[n, count : count + 1, :] * (q[l] - q[k])
                f[k] = term if f[k] is None else f[k] + term
                f[l] = -term if f[l] is None else f[l] - term
                count += 1
        high, low = split2(jnp.concatenate(f, axis=1))
        return lax.dot_general(
            oh_r[n],
            jnp.concatenate([members * high, members * low], axis=0),
            (((1,), (1,)), ((), ())),
            preferred_element_type=F32,
        )

    def numbers_of(n):
        rows_of = jnp.broadcast_to(labels[n], (nb, 4, 128)).reshape(nb * 4, 128)
        at_row = iota((nb * 4, 128), 0) & 3
        number = jnp.sum(jnp.where(iota((nb * 4, 128), 1) == at_row, rows_of, 0.0), axis=1, keepdims=True)
        return jnp.where(at_row < SLOTS, jnp.broadcast_to(number.astype(jnp.int32), (nb * 4, 128)), -1)

    def inflows():
        whole = pl.ds(0, nb - 1)
        copy(msg.at[whole], arrived.at[whole], msg_s, msg_r, at(1, 0)).wait()
        got = arrived[...].reshape(nb * 4, cells_z)
        labels[0] = arrived[:, 3:4, :]
        numbers = numbers_of(0)
        numbers_ref[0] = numbers
        lane = iota((nb * 4, 128), 1)
        high, low = split2(got)
        value = lax.dot_general(
            jnp.concatenate([high, high, low], axis=1),
            w_parts[...],
            (((1,), (1,)), ((), ())),
            preferred_element_type=F32,
        )
        for n in range(rows):
            mine = jnp.where(numbers == lane + n * 128, value[:, n * 128 : (n + 1) * 128], 0.0)
            flow[n : n + 1, :] = jnp.sum(mine, axis=0, keepdims=True)

        @pl.when(lead)
        def _():
            for c in third[0]:
                c.start()
            inflow_all[s] = flow[...]

        @pl.when(late)
        def _():
            for c in third[1]:
                c.start()
            pair[2].start()

    def table_of():
        return jnp.concatenate(split2(ptab[...].reshape(ns * rows, 128)), axis=1)

    def joined(both):
        return both[:, :128] + both[:, 128:]

    def arrive(copies):
        for c in copies[0]:
            c.wait()
        for c in copies[1]:
            c.wait_recv()

    @pl.when(lead)
    def _():
        arrive(first)
        table = table_of()
        both = flows(0, table)
        pair[0].wait_recv()
        build(1, other_mem)
        pair[1].wait_recv()
        both = both + flows(1, table)
        part[0, y] = joined(both)

    def step(t, carry):
        parity = lax.rem(t, 2)
        partial = [
            copy(part.at[parity, y], part.at[parity, y], part_s.at[k - 1], part_r.at[parity, k - 1], ring(k))
            for k in range(1, ny)
        ]

        tail = []
        for k in range(1, ny):
            target = (y + k) & (ny - 1)
            for n in range(2):
                lines = pl.ds(pl.multiple_of((n * ny + target) * rows, rows), rows)
                piece = part.at[parity, y, lines]
                tail.append(copy(piece, piece, tail_s.at[k - 1, n], tail_r.at[k - 1, n], ring(k)))

        @pl.when(jnp.logical_and(lead, t < STEPS - 1))
        def _():
            for c in partial:
                c.start()

        @pl.when(jnp.logical_and(lead, t == STEPS - 1))
        def _():
            for c in tail:
                c.start()

        @pl.when(t == 0)
        def _():
            inflows()

        now = halo(parity)
        for c in now:
            c.wait_recv()
        stream(parity)
        for c in now:
            c.wait_send()

        @pl.when(t < STEPS - 1)
        def _():
            collide(pop_out)
            pack()
            start_halo(1 - parity)

        @pl.when(jnp.logical_and(lead, t == 1))
        def _():
            pair[2].wait_recv()
            numbers_ref[1] = numbers_of(1)

        @pl.when(jnp.logical_and(lead, t < STEPS - 1))
        def _():
            for c in partial:
                c.wait()

        @pl.when(jnp.logical_and(lead, t == STEPS - 1))
        def _():
            for c in tail:
                c.wait()

        @pl.when(lead)
        def _():
            @pl.when(t == 0)
            def _():
                arrive(second)
                arrive(third)

            balance = part[parity, 0]
            for k in range(1, ny):
                balance = balance + part[parity, k]
            p = ptab[...].reshape(ns * rows, 128)
            rate = rates[:, 0].reshape(ns * rows, 128)
            leak = rates[:, 1].reshape(ns * rows, 128)
            source = inflow_all[...].reshape(ns * rows, 128)
            ptab[...] = (p + rate * (source - balance - leak * p)).reshape(ns, rows, 128)

            @pl.when(t < STEPS - 1)
            def _():
                table = table_of()
                part[1 - parity, y] = joined(flows(0, table) + flows(1, table))

        return carry

    lax.fori_loop(0, STEPS, step, 0)

    whole = pl.ds(0, nb - 1)

    @pl.when(lead)
    def _():
        pair[3].start()
        lane = iota((nb * 4, 128), 1)
        for n in (1, 0):
            final = ptab[n * ny + y]
            numbers = numbers_ref[n]
            value = jnp.zeros((nb * 4, 128), F32)
            for line in range(rows):
                value = value + jnp.where(numbers == lane + line * 128, final[line : line + 1, :], 0.0)
            value = jnp.sum(value, axis=1, keepdims=True)
            ret_out[n] = jnp.broadcast_to(value, (nb * 4, 128)).reshape(nb, 4, 128)

            for k in order:
                answer(k, n).start()
        answer(0, 1).start()
        ret_in[b] = ret_out[0, b]
        seg_out[...] = ptab[y]
        copy(ret_out.at[0, whole], ret_in.at[whole], ret_s.at[0], ret_r, at(1, 0)).wait()
        copy(ret_out.at[1], ret_in, ret_s.at[1], ret_r, at(1, 0)).wait_send()
        pair[3].wait_send()

    @pl.when(late)
    def _():
        for copies in (first, second, third):
            for c in copies[1]:
                c.wait_send()
        for c in pair[:3]:
            c.wait_send()
        pair[3].wait_recv()
        seg_out[...] = last[...]
        copy(ret_out.at[1], ret_in, ret_s.at[1], ret_r, at(1, 0)).wait_recv()

    back = ret_in[...].reshape(nb * 4, 128)[:, :blocks]
    bp_out[...] = jnp.sum(jnp.where(pick[...] > 0.5, back, 0.0), axis=0, keepdims=True)


def finish(pop_in, seg_in, bp_in, pop_out, seg_out, bp_out, sems):
    copies = [pltpu.make_async_copy(pop_in.at[i], pop_out.at[i], sems.at[i]) for i in range(pop_in.shape[0])]
    copies.append(pltpu.make_async_copy(seg_in, seg_out, sems.at[len(copies)]))
    copies.append(pltpu.make_async_copy(bp_in, bp_out, sems.at[len(copies)]))
    for c in copies:
        c.start()
    for c in copies:
        c.wait()


def local(
    populations,
    solid,
    boundary_pressure,
    block_col,
    block_dest,
    block_seg,
    seg_pressure,
    seg_rate,
    seg_leak,
    profile_weights,
    junc_members,
    junc_arity,
    junc_res,
    junc_cross,
):
    nb, ns = lax.axis_size("brick"), lax.axis_size("sub")
    ny = ns // 2
    _, cx, cy, cz = populations.shape
    segs, blocks, junctions = seg_pressure.shape[0], block_col.shape[0], junc_arity.shape[0]
    rows, links = segs // 128, 4 * junctions
    vmem, dma = pltpu.VMEM, pltpu.SemaphoreType.DMA
    scratch = [
        vmem((19, cx, cy, cz), F32),
        vmem((cx, cy, cz), jnp.int32),
        vmem((1, blocks), F32),
        vmem((1, blocks), jnp.int32),
        vmem((1, blocks), jnp.int32),
        vmem((1, blocks), jnp.int32),
        vmem((rows, 128), F32),
        vmem((segs, cz), F32),
        vmem((4, junctions), jnp.int32),
        vmem((1, junctions), jnp.int32),
        vmem((4, junctions), F32),
        vmem((4, 4, junctions), F32),
        dma((14,)),
        vmem((19, cx, cy, cz), F32),
        vmem((cx, cy, cz), F32),
        vmem((cx, cy, cz), F32),
        vmem((5, cy, cz), F32),
        vmem((5, cy, cz), F32),
        vmem((5, cx, cz), F32),
        vmem((5, cx, cz), F32),
        vmem((4, 8, cz), F32),
        vmem((2, 5, cy, cz), F32),
        vmem((2, 5, cy, cz), F32),
        vmem((2, 5, cx, cz), F32),
        vmem((2, 5, cx, cz), F32),
        vmem((2, 4, 8, cz), F32),
        vmem((ns, rows, 128), F32),
        vmem((2, rows, 128), F32),
        vmem((ns, 2, rows, 128), F32),
        vmem((ns, rows, 128), F32),
        vmem((rows, 128), F32),
        vmem((4, junctions), jnp.int32),
        vmem((2, 8, junctions), F32),
        vmem((2, 1, links), jnp.int32),
        vmem((2, 128, links), BF16),
        vmem((2, ns * rows, links), BF16),
        vmem((2, ny, ns * rows, 128), F32),
        vmem((nb, 4, cz), F32),
        vmem((nb, 4, cz), F32),
        vmem((nb * 4, blocks), F32),
        vmem((2, nb, 1, 128), F32),
        vmem((2, nb * 4, 128), jnp.int32),
        vmem((rows, 128), F32),
        vmem((segs, 3 * cz), BF16),
        vmem((2, nb, 4, 128), F32),
        vmem((nb, 4, 128), F32),
        dma((8,)),
        dma((2, 8)),
        dma((ny,)),
        dma((ns,)),
        dma((ny,)),
        dma((ns,)),
        dma((ny,)),
        dma((ns,)),
        dma((4,)),
        dma((4,)),
        dma((ny - 1,)),
        dma((2, ny - 1)),
        dma((ny - 1, 2)),
        dma((ny - 1, 2)),
        dma,
        dma,
        dma((2,)),
        dma,
    ]
    spec = pl.BlockSpec(memory_space=vmem)
    lattice, pressure, back = pl.pallas_call(
        functools.partial(kernel, nb, ns),
        out_shape=(
            pltpu.VMEM(populations.shape, F32),
            pltpu.VMEM((rows, 128), F32),
            pltpu.VMEM((1, blocks), F32),
        ),
        in_specs=[pl.BlockSpec(memory_space=pltpu.HBM)] * 14,
        out_specs=(spec, spec, spec),
        scratch_shapes=scratch,
        compiler_params=pltpu.CompilerParams(
            collective_id=0, has_side_effects=True, vmem_limit_bytes=56 * 2**20
        ),
        name="coupled",
    )(
        populations,
        solid,
        boundary_pressure.reshape(1, blocks),
        block_col.reshape(1, blocks),
        block_dest.reshape(1, blocks),
        block_seg.reshape(1, blocks),
        seg_pressure.reshape(rows, 128),
        seg_rate.reshape(rows, 128),
        seg_leak.reshape(rows, 128),
        profile_weights,
        junc_members,
        junc_arity.reshape(1, junctions),
        junc_res,
        junc_cross,
    )
    hbm = pl.BlockSpec(memory_space=pltpu.HBM)
    lattice, pressure, back = pl.pallas_call(
        finish,
        out_shape=(
            jax.ShapeDtypeStruct(populations.shape, F32),
            jax.ShapeDtypeStruct((rows, 128), F32),
            jax.ShapeDtypeStruct((1, blocks), F32),
        ),
        in_specs=[spec] * 3,
        out_specs=(hbm, hbm, hbm),
        scratch_shapes=[
            dma((21,)),
        ],
        compiler_params=pltpu.CompilerParams(vmem_limit_bytes=2**20),
        name="finish",
    )(lattice, pressure, back)
    return lattice, pressure.reshape(segs), back.reshape(blocks)


def solution(mesh):
    return jax.shard_map(
        local,
        mesh=mesh,
        in_specs=(
            P(None, "brick", "sub", None),
            P("brick", "sub", None),
            P(("brick", "sub")),
            P(("brick", "sub")),
            P(("brick", "sub"), None),
            P(("brick", "sub")),
            P(("brick", "sub")),
            P(("brick", "sub")),
            P(("brick", "sub")),
            P(("brick", "sub"), None),
            P(None, ("brick", "sub")),
            P(("brick", "sub")),
            P(None, ("brick", "sub")),
            P(None, None, ("brick", "sub")),
        ),
        out_specs=(P(None, "brick", "sub", None), P(("brick", "sub")), P(("brick", "sub"))),
        check_vma=False,
    )
```

```python
import functools

import jax
import jax.numpy as jnp
import numpy as np
from jax import lax
from jax.experimental import pallas as pl
from jax.experimental.pallas import tpu as pltpu
from jax.sharding import PartitionSpec as P

STEPS = 6
SLOTS = 3
MESH = pl.DeviceIdType.MESH
F32 = jnp.float32
BF16 = jnp.bfloat16
HIGHEST = lax.Precision.HIGHEST

VELOCITIES = [
    (0, 0, 0),
    (1, 0, 0),
    (-1, 0, 0),
    (0, 1, 0),
    (0, -1, 0),
    (0, 0, 1),
    (0, 0, -1),
    (1, 1, 0),
    (-1, -1, 0),
    (1, -1, 0),
    (-1, 1, 0),
    (1, 0, 1),
    (-1, 0, -1),
    (1, 0, -1),
    (-1, 0, 1),
    (0, 1, 1),
    (0, -1, -1),
    (0, 1, -1),
    (0, -1, 1),
]
OPPOSITE = [0, 2, 1, 4, 3, 6, 5, 8, 7, 10, 9, 12, 11, 14, 13, 16, 15, 18, 17]
RELAXATION = 1.25
DENSITY_SCALE = 0.1
X_UP = [i for i, c in enumerate(VELOCITIES) if c[0] == 1]
X_DOWN = [i for i, c in enumerate(VELOCITIES) if c[0] == -1]
Y_UP = [i for i, c in enumerate(VELOCITIES) if c[1] == 1]
Y_DOWN = [i for i, c in enumerate(VELOCITIES) if c[1] == -1]
CORNERS = [(7, 1, 1), (8, -1, -1), (9, 1, -1), (10, -1, 1)]


def iota(shape, axis):
    return lax.broadcasted_iota(jnp.int32, shape, axis)


def collide_sites(h, solid, mask, imposed):
    w0, w1, w2 = 1.0 / 3.0, 1.0 / 18.0, 1.0 / 36.0
    plus = {i: h[i] + h[i + 1] for i in range(1, 19, 2)}
    minus = {i: h[i] - h[i + 1] for i in range(1, 19, 2)}
    near = plus[1] + plus[3] + plus[5]
    far = (plus[7] + plus[9]) + (plus[11] + plus[13]) + (plus[15] + plus[17])
    density = 1.0 + (w0 * h[0] + w1 * near + w2 * far)
    inverse = 1.0 / density
    ux = (w1 * minus[1] + w2 * ((minus[7] + minus[9]) + (minus[11] + minus[13]))) * inverse
    uy = (w1 * minus[3] + w2 * ((minus[7] - minus[9]) + (minus[15] + minus[17]))) * inverse
    uz = (w1 * minus[5] + w2 * ((minus[11] - minus[13]) + (minus[15] - minus[17]))) * inverse
    base = 1.0 - 1.5 * (ux * ux + uy * uy + uz * uz)
    along = {1: ux, 3: uy, 5: uz, 7: ux + uy, 9: ux - uy, 11: ux + uz, 13: ux - uz, 15: uy + uz, 17: uy - uz}
    scale = jnp.where(mask, imposed, RELAXATION * density)
    shift = jnp.where(mask, -1.0, -RELAXATION)
    keep = jnp.where(mask, 0.0, 1.0 - RELAXATION)
    bounce = jnp.logical_and(solid, jnp.logical_not(mask))
    post = [None] * 19
    post[0] = jnp.where(bounce, h[0], scale * base + (shift + keep * h[0]))
    for i in range(1, 19, 2):
        c = along[i]
        even = base + 4.5 * (c * c)
        odd = 3.0 * c
        post[i] = jnp.where(bounce, h[i + 1], scale * (even + odd) + (shift + keep * h[i]))
        post[i + 1] = jnp.where(bounce, h[i], scale * (even - odd) + (shift + keep * h[i + 1]))
    return post


def off_diagonals(live, res, cross):
    rows = [[None] * 4 for _ in range(4)]
    sides = [[None] * 4 for _ in range(4)]
    zero = jnp.zeros_like(live[0])
    for k in range(4):
        for l in range(4):
            if k == l:
                rows[k][l] = res[k]
                sides[k][l] = live[k]
            else:
                rows[k][l] = live[k] * live[l] * (0.5 * (cross[k][l] + cross[l][k]))
                sides[k][l] = zero
    for c in range(4):
        inverse = 1.0 / rows[c][c]
        for r in range(c + 1, 4):
            factor = rows[r][c] * inverse
            for l in range(c + 1, 4):
                rows[r][l] = rows[r][l] - factor * rows[c][l]
            for l in range(c + 1):
                sides[r][l] = sides[r][l] - factor * sides[c][l]
    answer = [None] * 4
    for r in reversed(range(4)):
        inverse = 1.0 / rows[r][r]
        answer[r] = []
        for l in range(4):
            running = sides[r][l]
            for c in range(r + 1, 4):
                running = running - rows[r][c] * answer[c][l]
            answer[r].append(running * inverse)
    ones = [answer[k][0] + answer[k][1] + answer[k][2] + answer[k][3] for k in range(4)]
    total = 1.0 / (live[0] * ones[0] + live[1] * ones[1] + live[2] * ones[2] + live[3] * ones[3])
    pairs = []
    for a in range(4):
        for b in range(a + 1, 4):
            pairs.append(live[a] * live[b] * (answer[a][b] - ones[a] * ones[b] * total))
    return pairs


def split2(x):
    high = x.astype(BF16)
    return high, (x - high.astype(F32)).astype(BF16)


def split3(x):
    high = x.astype(BF16)
    rest = x - high.astype(F32)
    middle = rest.astype(BF16)
    return high, middle, (rest - middle.astype(F32)).astype(BF16)


def kernel(
    nb,
    ns,
    pop_hbm,
    solid_hbm,
    bp_hbm,
    col_hbm,
    dest_hbm,
    seg_hbm,
    segp_hbm,
    rate_hbm,
    leak_hbm,
    w_hbm,
    mem_hbm,
    arity_hbm,
    res_hbm,
    cross_hbm,
    pop_out,
    seg_out,
    bp_out,
    pop_ref,
    solid_ref,
    bp_ref,
    col_ref,
    dest_ref,
    seg_ref,
    segp_ref,
    w_ref,
    mem_ref,
    arity_ref,
    res_ref,
    cross_ref,
    load_s,
    post,
    mask_ref,
    imposed_ref,
    sxu,
    sxd,
    syu,
    syd,
    sc,
    rxu,
    rxd,
    ryu,
    ryd,
    rc,
    ptab,
    stage,
    rates,
    inflow_all,
    flow,
    other_mem,
    gbuf,
    row_at,
    oh_c,
    oh_r,
    part,
    msg,
    arrived,
    pick,
    labels,
    numbers_ref,
    last,
    w_parts,
    ret_out,
    ret_in,
    halo_s,
    halo_r,
    first_s,
    first_r,
    rates_s,
    rates_r,
    inflow_s,
    inflow_r,
    pair_s,
    pair_r,
    part_s,
    part_r,
    tail_s,
    tail_r,
    msg_s,
    msg_r,
    ret_s,
    ret_r,
):
    ny = ns // 2
    rows = segp_ref.shape[0]
    junctions = mem_ref.shape[1]
    links = 4 * junctions
    blocks = col_ref.shape[1]
    cells_x, cells_y, cells_z = solid_ref.shape
    b, s = lax.axis_index("brick"), lax.axis_index("sub")
    hi, y = s // ny, s & (ny - 1)
    partner = (b, (1 - hi) * ny + y)
    lead, late = hi == 0, hi != 0

    def at(db, ds):
        return ((b + db) & (nb - 1), (s + ds) & (ns - 1))

    def ring(k):
        return (b, (y + k) & (ny - 1))

    def copy(src, dst, send, recv, device):
        return pltpu.make_async_remote_copy(
            src_ref=src, dst_ref=dst, send_sem=send, recv_sem=recv, device_id=device, device_id_type=MESH
        )

    loads = [
        pltpu.make_async_copy(src, dst, load_s.at[n])
        for n, (src, dst) in enumerate(
            [
                (pop_hbm, pop_ref),
                (solid_hbm, solid_ref),
                (bp_hbm, bp_ref),
                (col_hbm, col_ref),
                (dest_hbm, dest_ref),
                (seg_hbm, seg_ref),
                (segp_hbm, segp_ref),
                (rate_hbm, stage.at[0]),
                (leak_hbm, stage.at[1]),
                (w_hbm, w_ref),
                (mem_hbm, mem_ref),
                (arity_hbm, arity_ref),
                (res_hbm, res_ref),
                (cross_hbm, cross_ref),
            ]
        )
    ]
    for n in (11, 12, 13, 4, 5, 3, 2, 0, 10, 6, 7, 8, 1, 9):
        loads[n].start()

    barrier = pltpu.get_barrier_semaphore()

    for k in range(1, nb):
        pl.semaphore_signal(barrier, inc=1, device_id=at(k, 0), device_id_type=MESH)
    for k in range(1, ns):
        pl.semaphore_signal(barrier, inc=1, device_id=at(0, k), device_id_type=MESH)
    for _, cx, cy in CORNERS:
        pl.semaphore_signal(barrier, inc=1, device_id=at(cx, cy), device_id_type=MESH)

    @pl.when(late)
    def _():
        for k in range(1, nb):
            pl.semaphore_signal(barrier, inc=1, device_id=(at(k, 0)[0], y), device_id_type=MESH)


    def halo(parity):
        copies = [
            (sxu, rxu, (1, 0)),
            (sxd, rxd, (-1, 0)),
            (syu, ryu, (0, 1)),
            (syd, ryd, (0, -1)),
        ]
        out = [
            copy(src, dst.at[parity], halo_s.at[n], halo_r.at[parity, n], at(*to))
            for n, (src, dst, to) in enumerate(copies)
        ]
        for n, (_, cx, cy) in enumerate(CORNERS):
            out.append(
                copy(sc.at[n], rc.at[parity, n], halo_s.at[4 + n], halo_r.at[parity, 4 + n], at(cx, cy))
            )
        return out

    def start_halo(parity):
        copies = halo(parity)
        for n in (2, 3, 4, 5, 6, 7, 0, 1):
            copies[n].start()

    halves = cells_y // 8

    def collide(source):
        def tile(n, carry):
            x, first_row = n // halves, pl.multiple_of(lax.rem(n, halves) * 8, 8)
            span = pl.ds(first_row, 8)
            h = [source[i, x, span, :] for i in range(19)]
            out = collide_sites(
                h, solid_ref[x, span, :] > 0, mask_ref[x, span, :] > 0.5, imposed_ref[x, span, :]
            )
            for i in range(19):
                post[i, x, span, :] = out[i]
            return carry

        lax.fori_loop(0, cells_x * halves, tile, 0)

    def pack():
        for n, i in enumerate(Y_UP):
            for x in range(cells_x):
                syu[n, x : x + 1, :] = post[i, x, cells_y - 1 : cells_y, :]
        for n, i in enumerate(Y_DOWN):
            for x in range(cells_x):
                syd[n, x : x + 1, :] = post[i, x, 0:1, :]
        for n, (i, cx, cy) in enumerate(CORNERS):
            x = cells_x - 1 if cx > 0 else 0
            row = cells_y - 1 if cy > 0 else 0
            sc[n] = jnp.broadcast_to(post[i, x, row : row + 1, :], (8, cells_z))
        for n, i in enumerate(X_UP):
            sxu[n] = post[i, cells_x - 1]
        for n, i in enumerate(X_DOWN):
            sxd[n] = post[i, 0]

    def stream(parity):
        edge = iota((cells_y, cells_z), 0)
        for i, (cx, cy, cz) in enumerate(VELOCITIES):
            for x in range(cells_x):
                xs = x - cx
                inside = 0 <= xs < cells_x
                if inside:
                    value = post[i, xs]
                elif cx > 0:
                    value = rxu[parity, X_UP.index(i)]
                else:
                    value = rxd[parity, X_DOWN.index(i)]
                if cy:
                    if not inside:
                        n = [c[0] for c in CORNERS].index(i)
                        row = rc[parity, n, 0:1, :]
                    elif cy > 0:
                        row = ryu[parity, Y_UP.index(i), xs : xs + 1, :]
                    else:
                        row = ryd[parity, Y_DOWN.index(i), xs : xs + 1, :]
                    value = pltpu.roll(value, cy % cells_y, 0)
                    value = jnp.where(edge == (0 if cy > 0 else cells_y - 1), row, value)
                if cz:
                    value = pltpu.roll(value, cz % cells_z, 1)
                pop_out[i, x] = value

    def build(n, ref):
        m = jnp.concatenate([ref[k : k + 1, :] for k in range(4)], axis=1)
        row = m >> 7
        row_at[n] = row
        lines = iota((128, links), 0)
        oh_c[n] = jnp.where(lines == (m & 127), 1.0, 0.0).astype(BF16)
        oh_r[n] = jnp.where(iota((ns * rows, links), 0) == row, 1.0, 0.0).astype(BF16)

    columns = cells_x * cells_y

    def hit():
        return iota((columns, blocks), 0) == col_ref[...]

    def prepare_junctions():
        for n in (11, 12, 13):
            loads[n].wait()
        live = [jnp.where(arity_ref[...] > k, 1.0, 0.0) for k in range(4)]
        pairs = off_diagonals(
            live,
            [res_ref[k : k + 1, :] for k in range(4)],
            [[cross_ref[k, l : l + 1, :] for l in range(4)] for k in range(4)],
        )
        for n, value in enumerate(pairs):
            gbuf[0, n : n + 1, :] = value
        gbuf[0, 6:8, :] = jnp.zeros((2, junctions), F32)

    def prepare_lattice():
        for n in (1, 2):
            loads[n].wait()
        hits = hit()
        found = jnp.sum(jnp.where(hits, 1.0, 0.0), axis=1, keepdims=True)
        pressed = jnp.sum(jnp.where(hits, bp_ref[...], 0.0), axis=1, keepdims=True)
        mask_ref[...] = jnp.broadcast_to(found, (columns, cells_z)).reshape(cells_x, cells_y, cells_z)
        imposed_ref[...] = jnp.broadcast_to(1.0 + DENSITY_SCALE * pressed, (columns, cells_z)).reshape(
            cells_x, cells_y, cells_z
        )
        collide(pop_ref)
        pack()

    def prepare_messages():
        for n in (3, 4, 5, 0):
            loads[n].wait()
        dest = dest_ref[...]
        eye = iota((blocks, blocks), 0) == iota((blocks, blocks), 1)
        dest_column = jnp.sum(jnp.where(eye, dest, 0), axis=1, keepdims=True)
        earlier = jnp.logical_and(dest_column == dest, iota((blocks, blocks), 0) < iota((blocks, blocks), 1))
        slot = jnp.sum(jnp.where(earlier, 1, 0), axis=0, keepdims=True)
        slot_column = jnp.sum(jnp.where(eye, slot, 0), axis=1, keepdims=True)
        number_column = jnp.sum(jnp.where(eye, seg_ref[...] + 1, 0), axis=1, keepdims=True)
        r = iota((nb * 4, blocks), 0)
        aimed = (r >> 2) == dest
        chosen = jnp.where(jnp.logical_and(aimed, (r & 3) == slot), 1.0, 0.0)
        pick[...] = chosen
        hits = hit()
        selector = lax.dot_general(
            chosen.astype(BF16),
            jnp.where(hits, 1.0, 0.0).astype(BF16),
            (((1,), (1,)), ((), ())),
            preferred_element_type=F32,
        ).astype(BF16)
        axial = jnp.zeros((columns, cells_z), F32)
        for i, c in enumerate(VELOCITIES):
            if c[0]:
                weight = c[0] * (1.0 / 18.0 if i < 7 else 1.0 / 36.0)
                axial = axial + weight * pop_ref[i].reshape(columns, cells_z)
        profiles = jnp.dot(
            jnp.concatenate([selector] * 3, axis=1),
            jnp.concatenate(split3(axial), axis=0),
            preferred_element_type=F32,
        )
        number = jnp.where(iota((blocks, cells_z), 1) == slot_column, number_column, 0)
        numbers = jnp.dot(
            jnp.concatenate([jnp.where(aimed, 1.0, 0.0).astype(BF16)] * 2, axis=1),
            jnp.concatenate([(number >> 6).astype(F32) * 64.0, (number & 63).astype(F32)], axis=0).astype(BF16),
            preferred_element_type=F32,
        )
        is_label = (iota((nb * 4, cells_z), 0) & 3) == 3
        msg[...] = jnp.where(is_label, numbers - 1.0, profiles).reshape(nb, 4, cells_z)

    def prepare_network():
        for n in (6, 7, 8, 10):
            loads[n].wait()

        @pl.when(lead)
        def _():
            build(0, mem_ref)

        loads[9].wait()
        high, low = split2(w_ref[...])
        w_parts[:, 0:cells_z] = high
        w_parts[:, cells_z : 2 * cells_z] = low
        w_parts[:, 2 * cells_z : 3 * cells_z] = high

    def spread(src, dst, send, recv):
        near = [copy(src, dst, send.at[k], recv.at[k], ring(k)) for k in range(1, ny)]
        far = [copy(src, dst, send.at[k], recv.at[ny + k], ring(k)) for k in range(ny)]
        return near, far

    pair = [
        copy(mem_hbm, other_mem, pair_s.at[0], pair_r.at[0], partner),
        copy(gbuf.at[0], gbuf.at[1], pair_s.at[1], pair_r.at[1], partner),
        copy(labels.at[0], labels.at[1], pair_s.at[2], pair_r.at[2], partner),
        copy(ptab.at[ny + y], last, pair_s.at[3], pair_r.at[3], partner),
    ]
    first = spread(segp_hbm, ptab.at[s], first_s, first_r)
    second = spread(stage, rates.at[s], rates_s, rates_r)
    third = spread(flow, inflow_all.at[s], inflow_s, inflow_r)

    def message(k):
        target = (b + k) & (nb - 1)
        return copy(msg.at[target], arrived.at[b], msg_s, msg_r, (target, s))

    def answer(k, n):
        target = (b + k) & (nb - 1)
        return copy(ret_out.at[n, target], ret_in.at[b], ret_s.at[n], ret_r, (target, n * ny + y))

    order = [(k + nb // 4) % (nb - 1) + 1 for k in range(1, nb)]

    @pl.when(lead)
    def _():
        prepare_messages()
        prepare_junctions()
        prepare_lattice()
        prepare_network()
        ptab[s] = segp_ref[...]
        rates[s] = stage[...]

    pl.semaphore_wait(barrier, nb - 1 + ns - 1 + len(CORNERS) + jnp.where(lead, nb - 1, 0))

    @pl.when(late)
    def _():
        pair[0].start()
        for c in first[1]:
            c.start()
        prepare_junctions()
        pair[1].start()
        prepare_messages()

    for k in order:
        message(k).start()
    arrived[b] = msg[b]

    @pl.when(lead)
    def _():
        for c in first[0]:
            c.start()

    @pl.when(late)
    def _():
        prepare_lattice()

    start_halo(0)

    @pl.when(lead)
    def _():
        for c in second[0]:
            c.start()

    @pl.when(late)
    def _():
        prepare_network()
        for c in second[1]:
            c.start()

    def flows(n, table):
        members = oh_c[n]
        found = jnp.dot(table, jnp.concatenate([members, members], axis=0), preferred_element_type=F32)
        q = jnp.sum(jnp.where(iota((ns * rows, links), 0) == row_at[n], found, 0.0), axis=0, keepdims=True)
        q = [q[:, k * junctions : (k + 1) * junctions] for k in range(4)]
        f = [None] * 4
        count = 0
        for k in range(4):
            for l in range(k + 1, 4):
                term = gbuf[n, count : count + 1, :] * (q[l] - q[k])
                f[k] = term if f[k] is None else f[k] + term
                f[l] = -term if f[l] is None else f[l] - term
                count += 1
        high, low = split2(jnp.concatenate(f, axis=1))
        return lax.dot_general(
            oh_r[n],
            jnp.concatenate([members * high, members * low], axis=0),
            (((1,), (1,)), ((), ())),
            preferred_element_type=F32,
        )

    def numbers_of(n):
        rows_of = jnp.broadcast_to(labels[n], (nb, 4, 128)).reshape(nb * 4, 128)
        at_row = iota((nb * 4, 128), 0) & 3
        number = jnp.sum(jnp.where(iota((nb * 4, 128), 1) == at_row, rows_of, 0.0), axis=1, keepdims=True)
        return jnp.where(at_row < SLOTS, jnp.broadcast_to(number.astype(jnp.int32), (nb * 4, 128)), -1)

    def inflows():
        whole = pl.ds(0, nb - 1)
        copy(msg.at[whole], arrived.at[whole], msg_s, msg_r, at(1, 0)).wait()
        got = arrived[...].reshape(nb * 4, cells_z)
        labels[0] = arrived[:, 3:4, :]
        numbers = numbers_of(0)
        numbers_ref[0] = numbers
        lane = iota((nb * 4, 128), 1)
        high, low = split2(got)
        value = lax.dot_general(
            jnp.concatenate([high, high, low], axis=1),
            w_parts[...],
            (((1,), (1,)), ((), ())),
            preferred_element_type=F32,
        )
        for n in range(rows):
            mine = jnp.where(numbers == lane + n * 128, value[:, n * 128 : (n + 1) * 128], 0.0)
            flow[n : n + 1, :] = jnp.sum(mine, axis=0, keepdims=True)

        @pl.when(lead)
        def _():
            for c in third[0]:
                c.start()
            inflow_all[s] = flow[...]

        @pl.when(late)
        def _():
            for c in third[1]:
                c.start()
            pair[2].start()

    def table_of():
        return jnp.concatenate(split2(ptab[...].reshape(ns * rows, 128)), axis=1)

    def joined(both):
        return both[:, :128] + both[:, 128:]

    def arrive(copies):
        for c in copies[0]:
            c.wait()
        for c in copies[1]:
            c.wait_recv()

    @pl.when(lead)
    def _():
        arrive(first)
        table = table_of()
        both = flows(0, table)
        pair[0].wait_recv()
        build(1, other_mem)
        pair[1].wait_recv()
        both = both + flows(1, table)
        part[0, y] = joined(both)

    def step(t, carry):
        parity = lax.rem(t, 2)
        partial = [
            copy(part.at[parity, y], part.at[parity, y], part_s.at[k - 1], part_r.at[parity, k - 1], ring(k))
            for k in range(1, ny)
        ]

        tail = []
        for k in range(1, ny):
            target = (y + k) & (ny - 1)
            for n in range(2):
                lines = pl.ds(pl.multiple_of((n * ny + target) * rows, rows), rows)
                piece = part.at[parity, y, lines]
                tail.append(copy(piece, piece, tail_s.at[k - 1, n], tail_r.at[k - 1, n], ring(k)))

        @pl.when(jnp.logical_and(lead, t < STEPS - 1))
        def _():
            for k in (1, 0, 2):
                partial[k].start()

        @pl.when(jnp.logical_and(lead, t == STEPS - 1))
        def _():
            for c in tail:
                c.start()

        @pl.when(t == 0)
        def _():
            inflows()

        now = halo(parity)
        for c in now:
            c.wait_recv()
        stream(parity)
        for c in now:
            c.wait_send()

        @pl.when(t < STEPS - 1)
        def _():
            collide(pop_out)
            pack()
            start_halo(1 - parity)

        @pl.when(jnp.logical_and(lead, t == 1))
        def _():
            pair[2].wait_recv()
            numbers_ref[1] = numbers_of(1)

        @pl.when(jnp.logical_and(lead, t < STEPS - 1))
        def _():
            for c in partial:
                c.wait()

        @pl.when(jnp.logical_and(lead, t == STEPS - 1))
        def _():
            for c in tail:
                c.wait()

        @pl.when(lead)
        def _():
            @pl.when(t == 0)
            def _():
                arrive(second)
                arrive(third)

            balance = part[parity, 0]
            for k in range(1, ny):
                balance = balance + part[parity, k]
            p = ptab[...].reshape(ns * rows, 128)
            rate = rates[:, 0].reshape(ns * rows, 128)
            leak = rates[:, 1].reshape(ns * rows, 128)
            source = inflow_all[...].reshape(ns * rows, 128)
            ptab[...] = (p + rate * (source - balance - leak * p)).reshape(ns, rows, 128)

            @pl.when(t < STEPS - 1)
            def _():
                table = table_of()
                part[1 - parity, y] = joined(flows(0, table) + flows(1, table))

        return carry

    lax.fori_loop(0, STEPS, step, 0)

    whole = pl.ds(0, nb - 1)

    @pl.when(lead)
    def _():
        pair[3].start()
        lane = iota((nb * 4, 128), 1)
        for n in (1, 0):
            final = ptab[n * ny + y]
            numbers = numbers_ref[n]
            value = jnp.zeros((nb * 4, 128), F32)
            for line in range(rows):
                value = value + jnp.where(numbers == lane + line * 128, final[line : line + 1, :], 0.0)
            value = jnp.sum(value, axis=1, keepdims=True)
            ret_out[n] = jnp.broadcast_to(value, (nb * 4, 128)).reshape(nb, 4, 128)

            for k in order:
                answer(k, n).start()
        answer(0, 1).start()
        ret_in[b] = ret_out[0, b]
        seg_out[...] = ptab[y]
        copy(ret_out.at[0, whole], ret_in.at[whole], ret_s.at[0], ret_r, at(1, 0)).wait()
        copy(ret_out.at[1], ret_in, ret_s.at[1], ret_r, at(1, 0)).wait_send()
        pair[3].wait_send()

    @pl.when(late)
    def _():
        for copies in (first, second, third):
            for c in copies[1]:
                c.wait_send()
        for c in pair[:3]:
            c.wait_send()
        pair[3].wait_recv()
        seg_out[...] = last[...]
        copy(ret_out.at[1], ret_in, ret_s.at[1], ret_r, at(1, 0)).wait_recv()

    back = ret_in[...].reshape(nb * 4, 128)[:, :blocks]
    bp_out[...] = jnp.sum(jnp.where(pick[...] > 0.5, back, 0.0), axis=0, keepdims=True)


def finish(pop_in, seg_in, bp_in, pop_out, seg_out, bp_out, sems):
    copies = [pltpu.make_async_copy(pop_in.at[i], pop_out.at[i], sems.at[i]) for i in range(pop_in.shape[0])]
    copies.append(pltpu.make_async_copy(seg_in, seg_out, sems.at[len(copies)]))
    copies.append(pltpu.make_async_copy(bp_in, bp_out, sems.at[len(copies)]))
    for c in copies:
        c.start()
    for c in copies:
        c.wait()


def local(
    populations,
    solid,
    boundary_pressure,
    block_col,
    block_dest,
    block_seg,
    seg_pressure,
    seg_rate,
    seg_leak,
    profile_weights,
    junc_members,
    junc_arity,
    junc_res,
    junc_cross,
):
    nb, ns = lax.axis_size("brick"), lax.axis_size("sub")
    ny = ns // 2
    _, cx, cy, cz = populations.shape
    segs, blocks, junctions = seg_pressure.shape[0], block_col.shape[0], junc_arity.shape[0]
    rows, links = segs // 128, 4 * junctions
    vmem, dma = pltpu.VMEM, pltpu.SemaphoreType.DMA
    scratch = [
        vmem((19, cx, cy, cz), F32),
        vmem((cx, cy, cz), jnp.int32),
        vmem((1, blocks), F32),
        vmem((1, blocks), jnp.int32),
        vmem((1, blocks), jnp.int32),
        vmem((1, blocks), jnp.int32),
        vmem((rows, 128), F32),
        vmem((segs, cz), F32),
        vmem((4, junctions), jnp.int32),
        vmem((1, junctions), jnp.int32),
        vmem((4, junctions), F32),
        vmem((4, 4, junctions), F32),
        dma((14,)),
        vmem((19, cx, cy, cz), F32),
        vmem((cx, cy, cz), F32),
        vmem((cx, cy, cz), F32),
        vmem((5, cy, cz), F32),
        vmem((5, cy, cz), F32),
        vmem((5, cx, cz), F32),
        vmem((5, cx, cz), F32),
        vmem((4, 8, cz), F32),
        vmem((2, 5, cy, cz), F32),
        vmem((2, 5, cy, cz), F32),
        vmem((2, 5, cx, cz), F32),
        vmem((2, 5, cx, cz), F32),
        vmem((2, 4, 8, cz), F32),
        vmem((ns, rows, 128), F32),
        vmem((2, rows, 128), F32),
        vmem((ns, 2, rows, 128), F32),
        vmem((ns, rows, 128), F32),
        vmem((rows, 128), F32),
        vmem((4, junctions), jnp.int32),
        vmem((2, 8, junctions), F32),
        vmem((2, 1, links), jnp.int32),
        vmem((2, 128, links), BF16),
        vmem((2, ns * rows, links), BF16),
        vmem((2, ny, ns * rows, 128), F32),
        vmem((nb, 4, cz), F32),
        vmem((nb, 4, cz), F32),
        vmem((nb * 4, blocks), F32),
        vmem((2, nb, 1, 128), F32),
        vmem((2, nb * 4, 128), jnp.int32),
        vmem((rows, 128), F32),
        vmem((segs, 3 * cz), BF16),
        vmem((2, nb, 4, 128), F32),
        vmem((nb, 4, 128), F32),
        dma((8,)),
        dma((2, 8)),
        dma((ny,)),
        dma((ns,)),
        dma((ny,)),
        dma((ns,)),
        dma((ny,)),
        dma((ns,)),
        dma((4,)),
        dma((4,)),
        dma((ny - 1,)),
        dma((2, ny - 1)),
        dma((ny - 1, 2)),
        dma((ny - 1, 2)),
        dma,
        dma,
        dma((2,)),
        dma,
    ]
    spec = pl.BlockSpec(memory_space=vmem)
    lattice, pressure, back = pl.pallas_call(
        functools.partial(kernel, nb, ns),
        out_shape=(
            pltpu.VMEM(populations.shape, F32),
            pltpu.VMEM((rows, 128), F32),
            pltpu.VMEM((1, blocks), F32),
        ),
        in_specs=[pl.BlockSpec(memory_space=pltpu.HBM)] * 14,
        out_specs=(spec, spec, spec),
        scratch_shapes=scratch,
        compiler_params=pltpu.CompilerParams(
            collective_id=0, has_side_effects=True, vmem_limit_bytes=56 * 2**20
        ),
        name="coupled",
    )(
        populations,
        solid,
        boundary_pressure.reshape(1, blocks),
        block_col.reshape(1, blocks),
        block_dest.reshape(1, blocks),
        block_seg.reshape(1, blocks),
        seg_pressure.reshape(rows, 128),
        seg_rate.reshape(rows, 128),
        seg_leak.reshape(rows, 128),
        profile_weights,
        junc_members,
        junc_arity.reshape(1, junctions),
        junc_res,
        junc_cross,
    )
    hbm = pl.BlockSpec(memory_space=pltpu.HBM)
    lattice, pressure, back = pl.pallas_call(
        finish,
        out_shape=(
            jax.ShapeDtypeStruct(populations.shape, F32),
            jax.ShapeDtypeStruct((rows, 128), F32),
            jax.ShapeDtypeStruct((1, blocks), F32),
        ),
        in_specs=[spec] * 3,
        out_specs=(hbm, hbm, hbm),
        scratch_shapes=[
            dma((21,)),
        ],
        compiler_params=pltpu.CompilerParams(vmem_limit_bytes=2**20),
        name="finish",
    )(lattice, pressure, back)
    return lattice, pressure.reshape(segs), back.reshape(blocks)


def solution(mesh):
    return jax.shard_map(
        local,
        mesh=mesh,
        in_specs=(
            P(None, "brick", "sub", None),
            P("brick", "sub", None),
            P(("brick", "sub")),
            P(("brick", "sub")),
            P(("brick", "sub"), None),
            P(("brick", "sub")),
            P(("brick", "sub")),
            P(("brick", "sub")),
            P(("brick", "sub")),
            P(("brick", "sub"), None),
            P(None, ("brick", "sub")),
            P(("brick", "sub")),
            P(None, ("brick", "sub")),
            P(None, None, ("brick", "sub")),
        ),
        out_specs=(P(None, "brick", "sub", None), P(("brick", "sub")), P(("brick", "sub"))),
        check_vma=False,
    )
```

```python
import functools

import jax
import jax.numpy as jnp
import numpy as np
from jax import lax
from jax.experimental import pallas as pl
from jax.experimental.pallas import tpu as pltpu
from jax.sharding import PartitionSpec as P

STEPS = 6
SLOTS = 3
MESH = pl.DeviceIdType.MESH
F32 = jnp.float32
BF16 = jnp.bfloat16
HIGHEST = lax.Precision.HIGHEST

VELOCITIES = [
    (0, 0, 0),
    (1, 0, 0),
    (-1, 0, 0),
    (0, 1, 0),
    (0, -1, 0),
    (0, 0, 1),
    (0, 0, -1),
    (1, 1, 0),
    (-1, -1, 0),
    (1, -1, 0),
    (-1, 1, 0),
    (1, 0, 1),
    (-1, 0, -1),
    (1, 0, -1),
    (-1, 0, 1),
    (0, 1, 1),
    (0, -1, -1),
    (0, 1, -1),
    (0, -1, 1),
]
OPPOSITE = [0, 2, 1, 4, 3, 6, 5, 8, 7, 10, 9, 12, 11, 14, 13, 16, 15, 18, 17]
RELAXATION = 1.25
DENSITY_SCALE = 0.1
X_UP = [i for i, c in enumerate(VELOCITIES) if c[0] == 1]
X_DOWN = [i for i, c in enumerate(VELOCITIES) if c[0] == -1]
Y_UP = [i for i, c in enumerate(VELOCITIES) if c[1] == 1]
Y_DOWN = [i for i, c in enumerate(VELOCITIES) if c[1] == -1]
CORNERS = [(7, 1, 1), (8, -1, -1), (9, 1, -1), (10, -1, 1)]


def iota(shape, axis):
    return lax.broadcasted_iota(jnp.int32, shape, axis)


def collide_sites(h, solid, mask, imposed):
    w0, w1, w2 = 1.0 / 3.0, 1.0 / 18.0, 1.0 / 36.0
    plus = {i: h[i] + h[i + 1] for i in range(1, 19, 2)}
    minus = {i: h[i] - h[i + 1] for i in range(1, 19, 2)}
    near = plus[1] + plus[3] + plus[5]
    far = (plus[7] + plus[9]) + (plus[11] + plus[13]) + (plus[15] + plus[17])
    density = 1.0 + (w0 * h[0] + w1 * near + w2 * far)
    inverse = 1.0 / density
    ux = (w1 * minus[1] + w2 * ((minus[7] + minus[9]) + (minus[11] + minus[13]))) * inverse
    uy = (w1 * minus[3] + w2 * ((minus[7] - minus[9]) + (minus[15] + minus[17]))) * inverse
    uz = (w1 * minus[5] + w2 * ((minus[11] - minus[13]) + (minus[15] - minus[17]))) * inverse
    base = 1.0 - 1.5 * (ux * ux + uy * uy + uz * uz)
    along = {1: ux, 3: uy, 5: uz, 7: ux + uy, 9: ux - uy, 11: ux + uz, 13: ux - uz, 15: uy + uz, 17: uy - uz}
    scale = jnp.where(mask, imposed, RELAXATION * density)
    shift = jnp.where(mask, -1.0, -RELAXATION)
    keep = jnp.where(mask, 0.0, 1.0 - RELAXATION)
    bounce = jnp.logical_and(solid, jnp.logical_not(mask))
    post = [None] * 19
    post[0] = jnp.where(bounce, h[0], scale * base + (shift + keep * h[0]))
    for i in range(1, 19, 2):
        c = along[i]
        even = base + 4.5 * (c * c)
        odd = 3.0 * c
        post[i] = jnp.where(bounce, h[i + 1], scale * (even + odd) + (shift + keep * h[i]))
        post[i + 1] = jnp.where(bounce, h[i], scale * (even - odd) + (shift + keep * h[i + 1]))
    return post


def off_diagonals(live, res, cross):
    rows = [[None] * 4 for _ in range(4)]
    sides = [[None] * 4 for _ in range(4)]
    zero = jnp.zeros_like(live[0])
    for k in range(4):
        for l in range(4):
            if k == l:
                rows[k][l] = res[k]
                sides[k][l] = live[k]
            else:
                rows[k][l] = live[k] * live[l] * (0.5 * (cross[k][l] + cross[l][k]))
                sides[k][l] = zero
    for c in range(4):
        inverse = 1.0 / rows[c][c]
        for r in range(c + 1, 4):
            factor = rows[r][c] * inverse
            for l in range(c + 1, 4):
                rows[r][l] = rows[r][l] - factor * rows[c][l]
            for l in range(c + 1):
                sides[r][l] = sides[r][l] - factor * sides[c][l]
    answer = [None] * 4
    for r in reversed(range(4)):
        inverse = 1.0 / rows[r][r]
        answer[r] = []
        for l in range(4):
            running = sides[r][l]
            for c in range(r + 1, 4):
                running = running - rows[r][c] * answer[c][l]
            answer[r].append(running * inverse)
    ones = [answer[k][0] + answer[k][1] + answer[k][2] + answer[k][3] for k in range(4)]
    total = 1.0 / (live[0] * ones[0] + live[1] * ones[1] + live[2] * ones[2] + live[3] * ones[3])
    pairs = []
    for a in range(4):
        for b in range(a + 1, 4):
            pairs.append(live[a] * live[b] * (answer[a][b] - ones[a] * ones[b] * total))
    return pairs


def split2(x):
    high = x.astype(BF16)
    return high, (x - high.astype(F32)).astype(BF16)


def split3(x):
    high = x.astype(BF16)
    rest = x - high.astype(F32)
    middle = rest.astype(BF16)
    return high, middle, (rest - middle.astype(F32)).astype(BF16)


def kernel(
    nb,
    ns,
    pop_hbm,
    solid_hbm,
    bp_hbm,
    col_hbm,
    dest_hbm,
    seg_hbm,
    segp_hbm,
    rate_hbm,
    leak_hbm,
    w_hbm,
    mem_hbm,
    arity_hbm,
    res_hbm,
    cross_hbm,
    pop_out,
    seg_out,
    bp_out,
    pop_ref,
    solid_ref,
    bp_ref,
    col_ref,
    dest_ref,
    seg_ref,
    segp_ref,
    w_ref,
    mem_ref,
    arity_ref,
    res_ref,
    cross_ref,
    load_s,
    post,
    mask_ref,
    imposed_ref,
    sxu,
    sxd,
    syu,
    syd,
    sc,
    rxu,
    rxd,
    ryu,
    ryd,
    rc,
    ptab,
    stage,
    rates,
    inflow_all,
    flow,
    other_mem,
    gbuf,
    row_at,
    oh_c,
    oh_r,
    part,
    msg,
    arrived,
    pick,
    labels,
    numbers_ref,
    last,
    w_parts,
    ret_out,
    ret_in,
    halo_s,
    halo_r,
    first_s,
    first_r,
    rates_s,
    rates_r,
    inflow_s,
    inflow_r,
    pair_s,
    pair_r,
    part_s,
    part_r,
    tail_s,
    tail_r,
    msg_s,
    msg_r,
    ret_s,
    ret_r,
):
    ny = ns // 2
    rows = segp_ref.shape[0]
    junctions = mem_ref.shape[1]
    links = 4 * junctions
    blocks = col_ref.shape[1]
    cells_x, cells_y, cells_z = solid_ref.shape
    b, s = lax.axis_index("brick"), lax.axis_index("sub")
    hi, y = s // ny, s & (ny - 1)
    partner = (b, (1 - hi) * ny + y)
    lead, late = hi == 0, hi != 0

    def at(db, ds):
        return ((b + db) & (nb - 1), (s + ds) & (ns - 1))

    def ring(k):
        return (b, (y + k) & (ny - 1))

    def copy(src, dst, send, recv, device):
        return pltpu.make_async_remote_copy(
            src_ref=src, dst_ref=dst, send_sem=send, recv_sem=recv, device_id=device, device_id_type=MESH
        )

    loads = [
        pltpu.make_async_copy(src, dst, load_s.at[n])
        for n, (src, dst) in enumerate(
            [
                (pop_hbm, pop_ref),
                (solid_hbm, solid_ref),
                (bp_hbm, bp_ref),
                (col_hbm, col_ref),
                (dest_hbm, dest_ref),
                (seg_hbm, seg_ref),
                (segp_hbm, segp_ref),
                (rate_hbm, stage.at[0]),
                (leak_hbm, stage.at[1]),
                (w_hbm, w_ref),
                (mem_hbm, mem_ref),
                (arity_hbm, arity_ref),
                (res_hbm, res_ref),
                (cross_hbm, cross_ref),
            ]
        )
    ]
    for n in (11, 12, 13, 4, 5, 3, 2, 0, 10, 6, 7, 8, 1, 9):
        loads[n].start()

    barrier = pltpu.get_barrier_semaphore()

    for k in range(1, nb):
        pl.semaphore_signal(barrier, inc=1, device_id=at(k, 0), device_id_type=MESH)
    for k in range(1, ns):
        pl.semaphore_signal(barrier, inc=1, device_id=at(0, k), device_id_type=MESH)
    for _, cx, cy in CORNERS:
        pl.semaphore_signal(barrier, inc=1, device_id=at(cx, cy), device_id_type=MESH)

    @pl.when(late)
    def _():
        for k in range(1, nb):
            pl.semaphore_signal(barrier, inc=1, device_id=(at(k, 0)[0], y), device_id_type=MESH)


    def halo(parity):
        copies = [
            (sxu, rxu, (1, 0)),
            (sxd, rxd, (-1, 0)),
            (syu, ryu, (0, 1)),
            (syd, ryd, (0, -1)),
        ]
        out = [
            copy(src, dst.at[parity], halo_s.at[n], halo_r.at[parity, n], at(*to))
            for n, (src, dst, to) in enumerate(copies)
        ]
        for n, (_, cx, cy) in enumerate(CORNERS):
            out.append(
                copy(sc.at[n], rc.at[parity, n], halo_s.at[4 + n], halo_r.at[parity, 4 + n], at(cx, cy))
            )
        return out

    def start_halo(parity):
        copies = halo(parity)
        for n in (2, 3, 4, 5, 6, 7, 0, 1):
            copies[n].start()

    halves = cells_y // 8

    def collide(source):
        def tile(n, carry):
            x, first_row = n // halves, pl.multiple_of(lax.rem(n, halves) * 8, 8)
            span = pl.ds(first_row, 8)
            h = [source[i, x, span, :] for i in range(19)]
            out = collide_sites(
                h, solid_ref[x, span, :] > 0, mask_ref[x, span, :] > 0.5, imposed_ref[x, span, :]
            )
            for i in range(19):
                post[i, x, span, :] = out[i]
            return carry

        lax.fori_loop(0, cells_x * halves, tile, 0)

    def pack():
        for n, i in enumerate(Y_UP):
            for x in range(cells_x):
                syu[n, x : x + 1, :] = post[i, x, cells_y - 1 : cells_y, :]
        for n, i in enumerate(Y_DOWN):
            for x in range(cells_x):
                syd[n, x : x + 1, :] = post[i, x, 0:1, :]
        for n, (i, cx, cy) in enumerate(CORNERS):
            x = cells_x - 1 if cx > 0 else 0
            row = cells_y - 1 if cy > 0 else 0
            sc[n] = jnp.broadcast_to(post[i, x, row : row + 1, :], (8, cells_z))
        for n, i in enumerate(X_UP):
            sxu[n] = post[i, cells_x - 1]
        for n, i in enumerate(X_DOWN):
            sxd[n] = post[i, 0]

    def stream(parity):
        edge = iota((cells_y, cells_z), 0)
        for i, (cx, cy, cz) in enumerate(VELOCITIES):
            for x in range(cells_x):
                xs = x - cx
                inside = 0 <= xs < cells_x
                if inside:
                    value = post[i, xs]
                elif cx > 0:
                    value = rxu[parity, X_UP.index(i)]
                else:
                    value = rxd[parity, X_DOWN.index(i)]
                if cy:
                    if not inside:
                        n = [c[0] for c in CORNERS].index(i)
                        row = rc[parity, n, 0:1, :]
                    elif cy > 0:
                        row = ryu[parity, Y_UP.index(i), xs : xs + 1, :]
                    else:
                        row = ryd[parity, Y_DOWN.index(i), xs : xs + 1, :]
                    value = pltpu.roll(value, cy % cells_y, 0)
                    value = jnp.where(edge == (0 if cy > 0 else cells_y - 1), row, value)
                if cz:
                    value = pltpu.roll(value, cz % cells_z, 1)
                pop_out[i, x] = value

    def build(n, ref):
        m = jnp.concatenate([ref[k : k + 1, :] for k in range(4)], axis=1)
        row = m >> 7
        row_at[n] = row
        lines = iota((128, links), 0)
        oh_c[n] = jnp.where(lines == (m & 127), 1.0, 0.0).astype(BF16)
        oh_r[n] = jnp.where(iota((ns * rows, links), 0) == row, 1.0, 0.0).astype(BF16)

    columns = cells_x * cells_y

    def hit():
        return iota((columns, blocks), 0) == col_ref[...]

    def prepare_junctions():
        for n in (11, 12, 13):
            loads[n].wait()
        live = [jnp.where(arity_ref[...] > k, 1.0, 0.0) for k in range(4)]
        pairs = off_diagonals(
            live,
            [res_ref[k : k + 1, :] for k in range(4)],
            [[cross_ref[k, l : l + 1, :] for l in range(4)] for k in range(4)],
        )
        for n, value in enumerate(pairs):
            gbuf[0, n : n + 1, :] = value
        gbuf[0, 6:8, :] = jnp.zeros((2, junctions), F32)

    def prepare_lattice():
        for n in (1, 2):
            loads[n].wait()
        hits = hit()
        found = jnp.sum(jnp.where(hits, 1.0, 0.0), axis=1, keepdims=True)
        pressed = jnp.sum(jnp.where(hits, bp_ref[...], 0.0), axis=1, keepdims=True)
        mask_ref[...] = jnp.broadcast_to(found, (columns, cells_z)).reshape(cells_x, cells_y, cells_z)
        imposed_ref[...] = jnp.broadcast_to(1.0 + DENSITY_SCALE * pressed, (columns, cells_z)).reshape(
            cells_x, cells_y, cells_z
        )
        collide(pop_ref)
        pack()

    def prepare_messages():
        for n in (3, 4, 5, 0):
            loads[n].wait()
        dest = dest_ref[...]
        eye = iota((blocks, blocks), 0) == iota((blocks, blocks), 1)
        dest_column = jnp.sum(jnp.where(eye, dest, 0), axis=1, keepdims=True)
        earlier = jnp.logical_and(dest_column == dest, iota((blocks, blocks), 0) < iota((blocks, blocks), 1))
        slot = jnp.sum(jnp.where(earlier, 1, 0), axis=0, keepdims=True)
        slot_column = jnp.sum(jnp.where(eye, slot, 0), axis=1, keepdims=True)
        number_column = jnp.sum(jnp.where(eye, seg_ref[...] + 1, 0), axis=1, keepdims=True)
        r = iota((nb * 4, blocks), 0)
        aimed = (r >> 2) == dest
        chosen = jnp.where(jnp.logical_and(aimed, (r & 3) == slot), 1.0, 0.0)
        pick[...] = chosen
        hits = hit()
        selector = lax.dot_general(
            chosen.astype(BF16),
            jnp.where(hits, 1.0, 0.0).astype(BF16),
            (((1,), (1,)), ((), ())),
            preferred_element_type=F32,
        ).astype(BF16)
        axial = jnp.zeros((columns, cells_z), F32)
        for i, c in enumerate(VELOCITIES):
            if c[0]:
                weight = c[0] * (1.0 / 18.0 if i < 7 else 1.0 / 36.0)
                axial = axial + weight * pop_ref[i].reshape(columns, cells_z)
        profiles = jnp.dot(
            jnp.concatenate([selector] * 3, axis=1),
            jnp.concatenate(split3(axial), axis=0),
            preferred_element_type=F32,
        )
        number = jnp.where(iota((blocks, cells_z), 1) == slot_column, number_column, 0)
        numbers = jnp.dot(
            jnp.concatenate([jnp.where(aimed, 1.0, 0.0).astype(BF16)] * 2, axis=1),
            jnp.concatenate([(number >> 6).astype(F32) * 64.0, (number & 63).astype(F32)], axis=0).astype(BF16),
            preferred_element_type=F32,
        )
        is_label = (iota((nb * 4, cells_z), 0) & 3) == 3
        msg[...] = jnp.where(is_label, numbers - 1.0, profiles).reshape(nb, 4, cells_z)

    def prepare_network():
        for n in (6, 7, 8, 10):
            loads[n].wait()

        @pl.when(lead)
        def _():
            build(0, mem_ref)

        loads[9].wait()
        high, low = split2(w_ref[...])
        w_parts[:, 0:cells_z] = high
        w_parts[:, cells_z : 2 * cells_z] = low
        w_parts[:, 2 * cells_z : 3 * cells_z] = high

    def spread(src, dst, send, recv):
        near = [copy(src, dst, send.at[k], recv.at[k], ring(k)) for k in range(1, ny)]
        far = [copy(src, dst, send.at[k], recv.at[ny + k], ring(k)) for k in range(ny)]
        return near, far

    pair = [
        copy(mem_hbm, other_mem, pair_s.at[0], pair_r.at[0], partner),
        copy(gbuf.at[0], gbuf.at[1], pair_s.at[1], pair_r.at[1], partner),
        copy(labels.at[0], labels.at[1], pair_s.at[2], pair_r.at[2], partner),
        copy(ptab.at[ny + y], last, pair_s.at[3], pair_r.at[3], partner),
    ]
    first = spread(segp_hbm, ptab.at[s], first_s, first_r)
    second = spread(stage, rates.at[s], rates_s, rates_r)
    third = spread(flow, inflow_all.at[s], inflow_s, inflow_r)

    def message(k):
        target = (b + k) & (nb - 1)
        return copy(msg.at[target], arrived.at[b], msg_s, msg_r, (target, s))

    def answer(k, n):
        target = (b + k) & (nb - 1)
        return copy(ret_out.at[n, target], ret_in.at[b], ret_s.at[n], ret_r, (target, n * ny + y))

    order = [(k + nb // 4) % (nb - 1) + 1 for k in range(1, nb)]

    @pl.when(lead)
    def _():
        prepare_messages()
        prepare_junctions()
        prepare_lattice()
        prepare_network()
        ptab[s] = segp_ref[...]
        rates[s] = stage[...]

    pl.semaphore_wait(barrier, nb - 1 + ns - 1 + len(CORNERS) + jnp.where(lead, nb - 1, 0))

    @pl.when(late)
    def _():
        pair[0].start()
        for c in first[1]:
            c.start()
        prepare_junctions()
        pair[1].start()
        prepare_messages()

    for k in order:
        message(k).start()
    arrived[b] = msg[b]

    @pl.when(lead)
    def _():
        for c in first[0]:
            c.start()

    @pl.when(late)
    def _():
        prepare_lattice()

    start_halo(0)

    @pl.when(lead)
    def _():
        for c in second[0]:
            c.start()

    @pl.when(late)
    def _():
        prepare_network()
        for c in second[1]:
            c.start()

    def flows(n, table):
        members = oh_c[n]
        found = jnp.dot(table, jnp.concatenate([members, members], axis=0), preferred_element_type=F32)
        q = jnp.sum(jnp.where(iota((ns * rows, links), 0) == row_at[n], found, 0.0), axis=0, keepdims=True)
        q = [q[:, k * junctions : (k + 1) * junctions] for k in range(4)]
        f = [None] * 4
        count = 0
        for k in range(4):
            for l in range(k + 1, 4):
                term = gbuf[n, count : count + 1, :] * (q[l] - q[k])
                f[k] = term if f[k] is None else f[k] + term
                f[l] = -term if f[l] is None else f[l] - term
                count += 1
        high, low = split2(jnp.concatenate(f, axis=1))
        return lax.dot_general(
            oh_r[n],
            jnp.concatenate([members * high, members * low], axis=0),
            (((1,), (1,)), ((), ())),
            preferred_element_type=F32,
        )

    def numbers_of(n):
        rows_of = jnp.broadcast_to(labels[n], (nb, 4, 128)).reshape(nb * 4, 128)
        at_row = iota((nb * 4, 128), 0) & 3
        number = jnp.sum(jnp.where(iota((nb * 4, 128), 1) == at_row, rows_of, 0.0), axis=1, keepdims=True)
        return jnp.where(at_row < SLOTS, jnp.broadcast_to(number.astype(jnp.int32), (nb * 4, 128)), -1)

    def inflows():
        whole = pl.ds(0, nb - 1)
        copy(msg.at[whole], arrived.at[whole], msg_s, msg_r, at(1, 0)).wait()
        got = arrived[...].reshape(nb * 4, cells_z)
        labels[0] = arrived[:, 3:4, :]
        numbers = numbers_of(0)
        numbers_ref[0] = numbers
        lane = iota((nb * 4, 128), 1)
        high, low = split2(got)
        value = lax.dot_general(
            jnp.concatenate([high, high, low], axis=1),
            w_parts[...],
            (((1,), (1,)), ((), ())),
            preferred_element_type=F32,
        )
        for n in range(rows):
            mine = jnp.where(numbers == lane + n * 128, value[:, n * 128 : (n + 1) * 128], 0.0)
            flow[n : n + 1, :] = jnp.sum(mine, axis=0, keepdims=True)

        @pl.when(lead)
        def _():
            for c in third[0]:
                c.start()
            inflow_all[s] = flow[...]

        @pl.when(late)
        def _():
            for c in third[1]:
                c.start()
            pair[2].start()

    def table_of():
        return jnp.concatenate(split2(ptab[...].reshape(ns * rows, 128)), axis=1)

    def joined(both):
        return both[:, :128] + both[:, 128:]

    def arrive(copies):
        for c in copies[0]:
            c.wait()
        for c in copies[1]:
            c.wait_recv()

    @pl.when(lead)
    def _():
        arrive(first)
        table = table_of()
        both = flows(0, table)
        pair[0].wait_recv()
        build(1, other_mem)
        pair[1].wait_recv()
        both = both + flows(1, table)
        part[0, y] = joined(both)

    def step(t, carry):
        parity = lax.rem(t, 2)
        partial = [
            copy(part.at[parity, y], part.at[parity, y], part_s.at[k - 1], part_r.at[parity, k - 1], ring(k))
            for k in range(1, ny)
        ]

        tail = []
        for k in range(1, ny):
            target = (y + k) & (ny - 1)
            for n in range(2):
                lines = pl.ds(pl.multiple_of((n * ny + target) * rows, rows), rows)
                piece = part.at[parity, y, lines]
                tail.append(copy(piece, piece, tail_s.at[k - 1, n], tail_r.at[k - 1, n], ring(k)))

        @pl.when(jnp.logical_and(lead, t < STEPS - 1))
        def _():
            for k in (1, 0, 2):
                partial[k].start()

        @pl.when(jnp.logical_and(lead, t == STEPS - 1))
        def _():
            for c in tail:
                c.start()

        @pl.when(t == 0)
        def _():
            inflows()

        now = halo(parity)
        for c in now:
            c.wait_recv()
        stream(parity)
        for c in now:
            c.wait_send()

        @pl.when(t < STEPS - 1)
        def _():
            collide(pop_out)
            pack()
            start_halo(1 - parity)

        @pl.when(jnp.logical_and(lead, t == 1))
        def _():
            pair[2].wait_recv()
            numbers_ref[1] = numbers_of(1)

        @pl.when(jnp.logical_and(lead, t < STEPS - 1))
        def _():
            for c in partial:
                c.wait_recv()

        @pl.when(jnp.logical_and(lead, t == STEPS - 1))
        def _():
            for c in tail:
                c.wait()

        @pl.when(lead)
        def _():
            @pl.when(t == 0)
            def _():
                arrive(second)
                arrive(third)

            balance = part[parity, 0]
            for k in range(1, ny):
                balance = balance + part[parity, k]
            p = ptab[...].reshape(ns * rows, 128)
            rate = rates[:, 0].reshape(ns * rows, 128)
            leak = rates[:, 1].reshape(ns * rows, 128)
            source = inflow_all[...].reshape(ns * rows, 128)
            ptab[...] = (p + rate * (source - balance - leak * p)).reshape(ns, rows, 128)

            @pl.when(t < STEPS - 1)
            def _():
                table = table_of()
                part[1 - parity, y] = joined(flows(0, table) + flows(1, table))
                for c in partial:
                    c.wait_send()

        return carry

    lax.fori_loop(0, STEPS, step, 0)

    whole = pl.ds(0, nb - 1)

    @pl.when(lead)
    def _():
        pair[3].start()
        lane = iota((nb * 4, 128), 1)
        for n in (1, 0):
            final = ptab[n * ny + y]
            numbers = numbers_ref[n]
            value = jnp.zeros((nb * 4, 128), F32)
            for line in range(rows):
                value = value + jnp.where(numbers == lane + line * 128, final[line : line + 1, :], 0.0)
            value = jnp.sum(value, axis=1, keepdims=True)
            ret_out[n] = jnp.broadcast_to(value, (nb * 4, 128)).reshape(nb, 4, 128)

            for k in order:
                answer(k, n).start()
        answer(0, 1).start()
        ret_in[b] = ret_out[0, b]
        seg_out[...] = ptab[y]
        copy(ret_out.at[0, whole], ret_in.at[whole], ret_s.at[0], ret_r, at(1, 0)).wait()
        copy(ret_out.at[1], ret_in, ret_s.at[1], ret_r, at(1, 0)).wait_send()
        pair[3].wait_send()

    @pl.when(late)
    def _():
        for copies in (first, second, third):
            for c in copies[1]:
                c.wait_send()
        for c in pair[:3]:
            c.wait_send()
        pair[3].wait_recv()
        seg_out[...] = last[...]
        copy(ret_out.at[1], ret_in, ret_s.at[1], ret_r, at(1, 0)).wait_recv()

    back = ret_in[...].reshape(nb * 4, 128)[:, :blocks]
    bp_out[...] = jnp.sum(jnp.where(pick[...] > 0.5, back, 0.0), axis=0, keepdims=True)


def finish(pop_in, seg_in, bp_in, pop_out, seg_out, bp_out, sems):
    copies = [pltpu.make_async_copy(pop_in.at[i], pop_out.at[i], sems.at[i]) for i in range(pop_in.shape[0])]
    copies.append(pltpu.make_async_copy(seg_in, seg_out, sems.at[len(copies)]))
    copies.append(pltpu.make_async_copy(bp_in, bp_out, sems.at[len(copies)]))
    for c in copies:
        c.start()
    for c in copies:
        c.wait()


def local(
    populations,
    solid,
    boundary_pressure,
    block_col,
    block_dest,
    block_seg,
    seg_pressure,
    seg_rate,
    seg_leak,
    profile_weights,
    junc_members,
    junc_arity,
    junc_res,
    junc_cross,
):
    nb, ns = lax.axis_size("brick"), lax.axis_size("sub")
    ny = ns // 2
    _, cx, cy, cz = populations.shape
    segs, blocks, junctions = seg_pressure.shape[0], block_col.shape[0], junc_arity.shape[0]
    rows, links = segs // 128, 4 * junctions
    vmem, dma = pltpu.VMEM, pltpu.SemaphoreType.DMA
    scratch = [
        vmem((19, cx, cy, cz), F32),
        vmem((cx, cy, cz), jnp.int32),
        vmem((1, blocks), F32),
        vmem((1, blocks), jnp.int32),
        vmem((1, blocks), jnp.int32),
        vmem((1, blocks), jnp.int32),
        vmem((rows, 128), F32),
        vmem((segs, cz), F32),
        vmem((4, junctions), jnp.int32),
        vmem((1, junctions), jnp.int32),
        vmem((4, junctions), F32),
        vmem((4, 4, junctions), F32),
        dma((14,)),
        vmem((19, cx, cy, cz), F32),
        vmem((cx, cy, cz), F32),
        vmem((cx, cy, cz), F32),
        vmem((5, cy, cz), F32),
        vmem((5, cy, cz), F32),
        vmem((5, cx, cz), F32),
        vmem((5, cx, cz), F32),
        vmem((4, 8, cz), F32),
        vmem((2, 5, cy, cz), F32),
        vmem((2, 5, cy, cz), F32),
        vmem((2, 5, cx, cz), F32),
        vmem((2, 5, cx, cz), F32),
        vmem((2, 4, 8, cz), F32),
        vmem((ns, rows, 128), F32),
        vmem((2, rows, 128), F32),
        vmem((ns, 2, rows, 128), F32),
        vmem((ns, rows, 128), F32),
        vmem((rows, 128), F32),
        vmem((4, junctions), jnp.int32),
        vmem((2, 8, junctions), F32),
        vmem((2, 1, links), jnp.int32),
        vmem((2, 128, links), BF16),
        vmem((2, ns * rows, links), BF16),
        vmem((2, ny, ns * rows, 128), F32),
        vmem((nb, 4, cz), F32),
        vmem((nb, 4, cz), F32),
        vmem((nb * 4, blocks), F32),
        vmem((2, nb, 1, 128), F32),
        vmem((2, nb * 4, 128), jnp.int32),
        vmem((rows, 128), F32),
        vmem((segs, 3 * cz), BF16),
        vmem((2, nb, 4, 128), F32),
        vmem((nb, 4, 128), F32),
        dma((8,)),
        dma((2, 8)),
        dma((ny,)),
        dma((ns,)),
        dma((ny,)),
        dma((ns,)),
        dma((ny,)),
        dma((ns,)),
        dma((4,)),
        dma((4,)),
        dma((ny - 1,)),
        dma((2, ny - 1)),
        dma((ny - 1, 2)),
        dma((ny - 1, 2)),
        dma,
        dma,
        dma((2,)),
        dma,
    ]
    spec = pl.BlockSpec(memory_space=vmem)
    lattice, pressure, back = pl.pallas_call(
        functools.partial(kernel, nb, ns),
        out_shape=(
            pltpu.VMEM(populations.shape, F32),
            pltpu.VMEM((rows, 128), F32),
            pltpu.VMEM((1, blocks), F32),
        ),
        in_specs=[pl.BlockSpec(memory_space=pltpu.HBM)] * 14,
        out_specs=(spec, spec, spec),
        scratch_shapes=scratch,
        compiler_params=pltpu.CompilerParams(
            collective_id=0, has_side_effects=True, vmem_limit_bytes=56 * 2**20
        ),
        name="coupled",
    )(
        populations,
        solid,
        boundary_pressure.reshape(1, blocks),
        block_col.reshape(1, blocks),
        block_dest.reshape(1, blocks),
        block_seg.reshape(1, blocks),
        seg_pressure.reshape(rows, 128),
        seg_rate.reshape(rows, 128),
        seg_leak.reshape(rows, 128),
        profile_weights,
        junc_members,
        junc_arity.reshape(1, junctions),
        junc_res,
        junc_cross,
    )
    hbm = pl.BlockSpec(memory_space=pltpu.HBM)
    lattice, pressure, back = pl.pallas_call(
        finish,
        out_shape=(
            jax.ShapeDtypeStruct(populations.shape, F32),
            jax.ShapeDtypeStruct((rows, 128), F32),
            jax.ShapeDtypeStruct((1, blocks), F32),
        ),
        in_specs=[spec] * 3,
        out_specs=(hbm, hbm, hbm),
        scratch_shapes=[
            dma((21,)),
        ],
        compiler_params=pltpu.CompilerParams(vmem_limit_bytes=2**20),
        name="finish",
    )(lattice, pressure, back)
    return lattice, pressure.reshape(segs), back.reshape(blocks)


def solution(mesh):
    return jax.shard_map(
        local,
        mesh=mesh,
        in_specs=(
            P(None, "brick", "sub", None),
            P("brick", "sub", None),
            P(("brick", "sub")),
            P(("brick", "sub")),
            P(("brick", "sub"), None),
            P(("brick", "sub")),
            P(("brick", "sub")),
            P(("brick", "sub")),
            P(("brick", "sub")),
            P(("brick", "sub"), None),
            P(None, ("brick", "sub")),
            P(("brick", "sub")),
            P(None, ("brick", "sub")),
            P(None, None, ("brick", "sub")),
        ),
        out_specs=(P(None, "brick", "sub", None), P(("brick", "sub")), P(("brick", "sub"))),
        check_vma=False,
    )
```
